32 devices in a mesh: dp: 32 (over z, y, x, core).
Axes of the slice: x: 2, y: 2, z: 4, core: 2. Of those that a mesh axis runs over, the one named last changes fastest.
Arguments:
- node_feats: bfloat16 [20480, 256], P('dp'), may hold values from -6 to 6
- edge_feats: bfloat16 [20480, 256], P('dp'), may hold values from -6 to 6
- segment_ids: int32 [20480], P('dp'), may hold values from 0 to 4, as said below
- neighbours: int32 [20480, 16], P('dp'), may hold values from 0 to 639, as said below
- nbr_mask: int32 [20480, 16], P('dp'), may hold values from 0 to 1, as said below
- degrees: int32 [20480], P('dp'), may hold values from 1 to 63
- w_edge: bfloat16 [2, 16, 256], replicated, may hold values from -1.5 to 1.5
- w_pre: bfloat16 [2, 768, 256], replicated, may hold values from -0.21875 to 0.21875
- b_pre: float32 [2, 256], replicated, may hold values from -3 to 3
- w_post: bfloat16 [2, 4, 832, 64], replicated, may hold values from -0.21875 to 0.21875
- w_mix: bfloat16 [2, 256, 256], replicated, may hold values from -0.375 to 0.375
- bn_gain: float32 [2, 256], replicated, may hold values from 0.1 to 1.9
- bn_bias: float32 [2, 256], replicated, may hold values from -3 to 3
- readout_grad: float32 [128, 256], P('dp'), may hold values from -6 to 6
Outputs:
- readout: float32 [128, 256], P('dp')
- node_grad: float32 [20480, 256], P('dp')
- edge_grad: float32 [20480, 256], P('dp')
- g_w_edge: float32 [2, 16, 256], replicated
- g_w_pre: float32 [2, 768, 256], replicated
- g_b_pre: float32 [2, 256], replicated
- g_w_post: float32 [2, 4, 832, 64], replicated
- g_w_mix: float32 [2, 256, 256], replicated
- g_bn_gain: float32 [2, 256], replicated
- g_bn_bias: float32 [2, 256], replicated
The draws below stay inside these ranges and needn't reach their ends.
Inputs may be any that keep to these rules, and one draw needn't show every extreme that they name: `segment_ids`: within each device's block of 640 node slots the ids never fall; each of the 4 subgraphs holds 1 to 160 consecutive nodes and one of them exactly 160; id 4 marks the unused slots at the block's end. `neighbours`: indices count from the first node of the device's block and point into the same subgraph; an unused node slot points at itself. `nbr_mask`: slot k is used exactly when k is below the node's neighbour count: 15 for the first node of a subgraph, 10 for its next 15 nodes, 1 to 4 for the others, 1 for unused node slots.
All inputs are finite; a program needn't handle non-finite values.
Results may differ from the reference program's by a relative error of at most 0.039.
Values sent between devices are 32-bit elements; how exact they have to be, the bound alone decides.
No kernel may reach another device: no remote copies, remote signals or barrier semaphores. Data moves between devices by JAX's collectives and lax.ppermute only.
A program may use at most 128 MiB of HBM per device.

```python
import jax
import jax.numpy as jnp
from jax import lax

H = 256
EDGE = 16
TOWERS = 4
TW = 64
NBR = 16
LAYERS = 2
SUB_MAX = 160
SUB_DEV = 4
NODES_DEV = 640
NODES = 20480
SEEDS = 128


def sample_graph_ordering(key):
    device_count = NODES // NODES_DEV
    key_sizes, key_largest, key_links, key_leaves = jax.random.split(key, 4)
    position = jnp.arange(device_count)
    low_bound = max(SUB_MAX // 10, 1)
    ceiling = SUB_MAX // 5 + (SUB_MAX - SUB_MAX // 5) * position // max(device_count - 1, 1)
    ceiling = jnp.maximum(ceiling, low_bound)
    sizes = jax.random.randint(key_sizes, (device_count, SUB_DEV), low_bound, ceiling[:, None] + 1)
    largest = jax.random.randint(key_largest, (device_count,), 0, SUB_DEV)
    sizes = jnp.where(jnp.arange(SUB_DEV)[None, :] == largest[:, None], SUB_MAX, sizes).astype(jnp.int32)
    ends = jnp.cumsum(sizes, axis=1)
    starts = ends - sizes
    slot_index = jnp.arange(NODES_DEV, dtype=jnp.int32)
    member = jnp.sum((slot_index[None, :, None] >= ends[:, None, :]).astype(jnp.int32), axis=2)
    bounded = jnp.minimum(member, SUB_DEV - 1)
    first_node = jnp.take_along_axis(starts, bounded, axis=1)
    node_total = jnp.take_along_axis(sizes, bounded, axis=1)
    padding = member == SUB_DEV
    first_node = jnp.where(padding, slot_index[None, :], first_node)
    node_total = jnp.where(padding, 1, node_total)
    rank = slot_index[None, :] - first_node
    links = first_node[:, :, None] + jax.random.randint(key_links, (device_count, NODES_DEV, NBR), 0, node_total[:, :, None])
    leaves = jax.random.randint(key_leaves, (device_count, NODES_DEV), 1, 5)
    live_count = jnp.where(rank == 0, 15, jnp.where(rank <= 15, 10, leaves))
    live_count = jnp.where(padding, 1, live_count)
    used = (jnp.arange(NBR)[None, None, :] < live_count[:, :, None]).astype(jnp.int32)
    return (member.reshape(NODES).astype(jnp.int32), links.reshape(NODES, NBR).astype(jnp.int32), used.reshape(NODES, NBR))


def draw_segment_ids(key, part):
    return sample_graph_ordering(key)[0]


def draw_neighbours(key, part):
    return sample_graph_ordering(key)[1]


def draw_nbr_mask(key, part):
    return sample_graph_ordering(key)[2]


def place_ends(result, key, low, high):
    longest = result.shape.index(max(result.shape))
    spots = []
    for shift in (0, 1):
        where = [jax.random.randint(jax.random.fold_in(key, axis), (), 0, length) for axis, length in enumerate(result.shape)]
        where[longest] = (where[longest] + shift) % result.shape[longest]
        spots.append(tuple(where))
    return result.at[spots[0]].set(low).at[spots[1]].set(high)


def levels(stream_key, dims, shards, low, high):
    def one(dim, shards_of):
        draws = jax.random.uniform(jax.random.fold_in(jax.random.fold_in(stream_key, 6), dim), (shards_of,), jnp.float32, low / len(shards), high / len(shards))
        return jnp.repeat(jnp.exp(draws), dims[dim] // shards_of).reshape((-1,) + (1,) * (len(dims) - dim - 1))

    factor_of = one(*shards[0])
    for cut in shards[1:]:
        factor_of = factor_of * one(*cut)
    return factor_of


def gaussian(own_key, extent, width, most, cuts=(), kind=jnp.bfloat16):
    level = levels(own_key, extent, cuts, -0.22, 0.18) if cuts else 1.0
    entries = jax.random.normal(own_key, extent, jnp.float32) * width * level
    return jnp.minimum(jnp.maximum(entries, -most), most).astype(kind)


def setup_inputs(seed: int = 0) -> dict:
    key_list = jax.random.split(jax.random.key(seed), 15)
    return {
        "node_feats": gaussian(key_list[0], (NODES, H), 1.0, 6.0, ((0, 32),)),
        "edge_feats": gaussian(key_list[1], (NODES, NBR * EDGE), 1.0, 6.0, ((0, 32),)),
        "segment_ids": draw_segment_ids(jax.random.fold_in(key_list[14], 71), 0),
        "neighbours": draw_neighbours(jax.random.fold_in(key_list[14], 71), 0),
        "nbr_mask": draw_nbr_mask(jax.random.fold_in(key_list[14], 71), 0),
        "degrees": place_ends(jax.random.randint(key_list[5], (NODES,), 1, 64), jax.random.fold_in(key_list[5], 1), 1, 63).astype(jnp.int32),
        "w_edge": gaussian(key_list[6], (LAYERS, EDGE, H), EDGE ** -0.5, 1.5),
        "w_pre": gaussian(key_list[7], (LAYERS, 3 * H, H), (3 * H) ** -0.5, 0.21875),
        "b_pre": gaussian(key_list[8], (LAYERS, H), 0.5, 3.0, (), jnp.float32),
        "w_post": gaussian(key_list[9], (LAYERS, TOWERS, 13 * TW, TW), (13 * TW) ** -0.5, 0.21875),
        "w_mix": gaussian(key_list[10], (LAYERS, H, H), H ** -0.5, 0.375),
        "bn_gain": jnp.clip(1.0 + 0.18 * jax.random.normal(key_list[11], (LAYERS, H), jnp.float32), 0.1, 1.9),
        "bn_bias": gaussian(key_list[12], (LAYERS, H), 0.5, 3.0, (), jnp.float32),
        "readout_grad": gaussian(key_list[13], (SEEDS, H), 1.0, 6.0, ((0, 32),), jnp.float32),
    }


DEGREE_CENTER = 2.0
SPREAD_OFFSET = 0.25
STABILITY_FLOOR = 1e-05

@jax.custom_vjp
def low(v):
    return lax.optimization_barrier(v.astype(jnp.bfloat16)).astype(jnp.float32)

@jax.custom_vjp
def low_back(v):
    return v

def low_keep(v):
    return (low(v), None)

def low_pass(kept, grad):
    return (grad,)

def back_keep(v):
    return (v, None)

def back_low(kept, grad):
    return (low(grad),)
low.defvjp(low_keep, low_pass)
low_back.defvjp(back_keep, back_low)

def summarize(message, alive, filled_rows):
    weight = alive.astype(message.dtype)[:, :, None]
    live_three = alive[:, :, None]
    average = lax.optimization_barrier(jnp.sum(weight * message, axis=1)) / filled_rows[:, None]
    deviation = message - average[:, None, :]
    spread = jnp.sqrt(lax.optimization_barrier(jnp.sum(weight * deviation * deviation, axis=1)) / filled_rows[:, None] + SPREAD_OFFSET)
    highest_value = lax.optimization_barrier(jnp.max(jnp.where(live_three, message, -1e+30), axis=1))
    upper_terms = jnp.where(live_three, jnp.exp(jnp.where(live_three, message - highest_value[:, None, :], 0.0)), 0.0)
    soft_max = highest_value + jnp.log(lax.optimization_barrier(jnp.sum(upper_terms, axis=1)))
    lowest_value = lax.optimization_barrier(jnp.min(jnp.where(live_three, message, 1e+30), axis=1))
    lower_terms = jnp.where(live_three, jnp.exp(jnp.where(live_three, lowest_value[:, None, :] - message, 0.0)), 0.0)
    soft_min = lowest_value - jnp.log(lax.optimization_barrier(jnp.sum(lower_terms, axis=1)))
    return (average, soft_max, soft_min, spread)

def tower_layout(rounded, stats, amplify_rows, attenuate_rows, towers):
    row_count, feat_width = rounded.shape
    summaries = list(stats)
    grown = [member * amplify_rows[:, None] for member in summaries]
    shrunk = [member * attenuate_rows[:, None] for member in summaries]
    stacked = jnp.stack([rounded] + summaries + grown + shrunk, axis=1)
    split_up = stacked.reshape(row_count, 13, towers, feat_width // towers)
    return jnp.transpose(split_up, (0, 2, 1, 3)).reshape(row_count, towers, 13 * (feat_width // towers))

def reference(node_feats, edge_feats, segment_ids, neighbours, nbr_mask, degrees, w_edge, w_pre, b_pre, w_post, w_mix, bn_gain, bn_bias, readout_grad):
    highest = lax.Precision.HIGHEST
    total_nodes = node_feats.shape[0]
    block_count = total_nodes // NODES_DEV
    alive_nodes = (segment_ids < SUB_DEV).astype(jnp.float32)[:, None]
    alive_slots = nbr_mask > 0
    filled = lax.optimization_barrier(jnp.sum(nbr_mask.astype(jnp.float32), axis=1))
    log_degree = jnp.log(degrees.astype(jnp.float32) + 1.0)
    amplify = log_degree / DEGREE_CENTER
    attenuate = DEGREE_CENTER / log_degree

    def blocked(array):
        return array.reshape((block_count, NODES_DEV) + array.shape[1:])

    def layer_update(hidden_state, edges, weights):
        w_edge_layer, w_pre_layer, prior_offset_level, w_post_layer, w_mix_layer, gain_layer, bias_layer = weights

        def block_output(pieces):
            hidden_rows, edge_rows, neighbour_feature_rows, slot_rows, filled_rows, amplify_rows, attenuate_rows = pieces
            row_count = hidden_rows.shape[0]
            rounded = low(hidden_rows)
            own = low_back(jnp.dot(rounded, w_pre_layer[:H], precision=highest))
            near = low_back(jnp.dot(rounded, w_pre_layer[H:2 * H], precision=highest))
            edges_three = edge_rows.reshape(row_count, NBR, EDGE)
            encoded = low(low_back(jnp.einsum('nke,eh->nkh', edges_three, w_edge_layer, precision=highest)))
            edge_term = low_back(jnp.einsum('nkh,hg->nkg', encoded, w_pre_layer[2 * H:], precision=highest))
            message = own[:, None, :] + near[neighbour_feature_rows] + edge_term + prior_offset_level
            stats = summarize(message, slot_rows, filled_rows)
            tower_in = low(tower_layout(rounded, stats, amplify_rows, attenuate_rows, TOWERS))
            mixed = low(low_back(jnp.einsum('ntk,tko->nto', tower_in, w_post_layer, precision=highest))).reshape(row_count, H)
            return low_back(jnp.dot(mixed, w_mix_layer, precision=highest))
        pieces = (blocked(hidden_state), blocked(edges), blocked(neighbours), blocked(alive_slots), blocked(filled), blocked(amplify), blocked(attenuate))
        projected = lax.map(jax.checkpoint(block_output), pieces).reshape(total_nodes, H)
        tallied_entries = jnp.sum(alive_nodes)
        center = lax.optimization_barrier(jnp.sum(alive_nodes * projected, axis=0)) / tallied_entries
        sample_dispersion = lax.optimization_barrier(jnp.sum(alive_nodes * (projected - center) ** 2, axis=0)) / tallied_entries
        normed = (projected - center) * lax.rsqrt(sample_dispersion + STABILITY_FLOOR)
        gated = normed * gain_layer + bias_layer
        return hidden_state + jax.nn.silu(gated)

    def forward(start, edges, w_edge_all, w_pre_all, b_pre_all, w_post_all, w_mix_all, gain_all, bias_all):
        hidden_state = start
        for layer_index in range(LAYERS):
            weights = (w_edge_all[layer_index], w_pre_all[layer_index], b_pre_all[layer_index], w_post_all[layer_index], w_mix_all[layer_index], gain_all[layer_index], bias_all[layer_index])
            hidden_state = layer_update(hidden_state, edges, weights)
        owner = (jnp.arange(total_nodes) // NODES_DEV).astype(jnp.int32)
        anchor_vertex_position = jnp.where(segment_ids < SUB_DEV, owner * SUB_DEV + segment_ids, SEEDS).astype(jnp.int32)
        summed = jax.ops.segment_sum(hidden_state, anchor_vertex_position, num_segments=SEEDS + 1)
        return summed[:SEEDS] / SUB_MAX
    inputs = (node_feats.astype(jnp.float32), edge_feats.astype(jnp.float32), w_edge.astype(jnp.float32), w_pre.astype(jnp.float32), b_pre.astype(jnp.float32), w_post.astype(jnp.float32), w_mix.astype(jnp.float32), bn_gain.astype(jnp.float32), bn_bias.astype(jnp.float32))
    readout, pull_back = jax.vjp(forward, *inputs)
    grads = pull_back(readout_grad.astype(jnp.float32))
    return (readout, grads[0], grads[1], grads[2], grads[3], grads[4], grads[5], grads[6], grads[7], grads[8])
```

```python
import functools

import jax
import jax.numpy as jnp
from jax import lax
from jax.experimental import pallas as pl
from jax.experimental.pallas import tpu as pltpu
from jax.sharding import PartitionSpec as P

SUB_MAX = 160
DEGREE_CENTER = 2.0
SPREAD_OFFSET = 0.25
STABILITY_FLOOR = 1e-05

LEAF_SLOTS = 4
HUB_RANK = 16
F32 = jnp.float32
BF16 = jnp.bfloat16
NN = (((1,), (0,)), ((), ()))
NT = (((1,), (1,)), ((), ()))
TN = (((0,), (0,)), ((), ()))
TT = (((0,), (1,)), ((), ()))


def mm(a, b, dims=NN):
    return lax.dot_general(a, b, dims, preferred_element_type=F32)


def iota(shape, dim):
    return lax.broadcasted_iota(jnp.int32, shape, dim)


def to_col(row):
    f = row.shape[1]
    return jnp.sum(jnp.where(iota((f, f), 0) == iota((f, f), 1), row, 0.0), axis=1, keepdims=True)


def to_row(col):
    f = col.shape[0]
    return jnp.sum(jnp.where(iota((f, f), 0) == iota((f, f), 1), col, 0.0), axis=0, keepdims=True)


def fold(value, op):
    return op(value, pltpu.roll(value, 64, 1))


def split_two(value):
    high = value.astype(BF16)
    return high, (value - high.astype(F32)).astype(BF16)


def build_tables(ef_ref, seg_ref, nbr_ref, mask_ref, deg_ref, b_ref, live_ref, rows_ref, g_ref, gt_ref):
    nodes = seg_ref.shape[1]
    seg = seg_ref[...]
    lane_h = iota((1, 128), 1)
    sub_h = iota((128, 1), 0)
    node_row = jnp.zeros((1, 128), jnp.int32)
    node_col = jnp.zeros((128, 1), jnp.int32)
    lane_r, sub_r = lane_h & 15, sub_h & 15
    lane_s, sub_s = (lane_h >> 4) & 3, (sub_h >> 4) & 3
    below = [jnp.sum((seg < s).astype(jnp.int32), axis=1, keepdims=True) for s in range(5)]
    for s in range(4):
        start, size = below[s], below[s + 1] - below[s]
        node_row = jnp.where(lane_s == s, jnp.where(lane_r < size, start + lane_r, -1), node_row)
        node_col = jnp.where(sub_s == s, jnp.where(sub_r < size, start + sub_r, -1), node_col)
    node_col = jnp.where(sub_h < 64, node_col, -1)
    g = (iota((nodes, 128), 0) == node_row).astype(F32).astype(BF16)
    gt = (iota((128, nodes), 1) == node_col).astype(F32).astype(BF16)
    g_ref[...] = g
    gt_ref[...] = gt
    is_hub = jnp.sum(gt.astype(F32), axis=0, keepdims=True)

    nbr = nbr_ref[...]
    mask = (mask_ref[...] > 0).astype(F32)
    nbr_h = (
        mm((nbr >> 3).astype(F32).astype(BF16), g) * 8.0 + mm((nbr & 7).astype(F32).astype(BF16), g)
    ).astype(jnp.int32)
    mask_h = mm(mask.astype(BF16), g)
    valid = (node_row >= 0).astype(F32)
    first = (lane_h < 64).astype(F32)

    def degree_rows(deg):
        log_degree = jnp.log(deg + 1.0)
        return log_degree / DEGREE_CENTER, DEGREE_CENTER / log_degree

    deg = deg_ref[...].astype(F32)
    deg_h = mm(jnp.broadcast_to(deg, (8, nodes)).astype(BF16), g)[0:1]
    deg_h = jnp.where(valid > 0, deg_h, 1.0)
    amp, att = degree_rows(deg)
    amp_h, att_h = degree_rows(deg_h)
    filled = jnp.sum(mask, axis=0, keepdims=True)
    filled_h = jnp.maximum(jnp.sum(mask_h, axis=0, keepdims=True), 1.0)
    rows_ref[...] = jnp.zeros_like(rows_ref)
    for i, (leaf, hub) in enumerate(
        (
            (amp, amp_h),
            (att, att_h),
            (1.0 / filled, 1.0 / filled_h),
            ((seg < 4).astype(F32), None),
            (1.0 - is_hub, valid * first),
            (is_hub, valid),
        )
    ):
        rows_ref[i : i + 1, 0:nodes] = leaf
        if hub is not None:
            rows_ref[i : i + 1, nodes : nodes + 128] = hub

    ef_t = ef_ref[...].T
    ef_h = mm(ef_t, g).astype(BF16)
    node_iota = iota((nodes, nodes), 0)
    hub_iota = iota((nodes, 128), 0)
    zero16 = jnp.zeros((16, nodes), BF16)
    for k in range(LEAF_SLOTS):
        lo = k * nodes
        b_ref[0:nodes, lo : lo + nodes] = (node_iota == nbr[k : k + 1]).astype(F32).astype(BF16)
        piece = ef_t[16 * k : 16 * k + 16]
        for r, part in enumerate((piece, zero16, piece, zero16)):
            b_ref[nodes + 16 * r : nodes + 16 * r + 16, lo : lo + nodes] = part
        live_ref[0:1, lo : lo + nodes] = mask[k : k + 1]
    own_half = (iota((32, 128), 0) < 16) == (iota((32, 128), 1) < 64)
    for j in range(8):
        lo = LEAF_SLOTS * nodes + 128 * j
        index = jnp.where(lane_h < 64, nbr_h[2 * j : 2 * j + 1], nbr_h[2 * j + 1 : 2 * j + 2])
        b_ref[0:nodes, lo : lo + 128] = (hub_iota == index).astype(F32).astype(BF16)
        piece = jnp.where(own_half, ef_h[32 * j : 32 * j + 32].astype(F32), 0.0).astype(BF16)
        b_ref[nodes : nodes + 32, lo : lo + 128] = piece
        b_ref[nodes + 32 : nodes + 64, lo : lo + 128] = piece
        live_ref[0:1, lo : lo + 128] = jnp.where(
            lane_h < 64, mask_h[2 * j : 2 * j + 1], mask_h[2 * j + 1 : 2 * j + 2]
        )


def tower_weights(wpost_ref, layer, t):
    w = wpost_ref[layer, t]
    inner = iota((64, 320), 1) >= 64
    zero = jnp.zeros((64, 320), BF16)
    return jnp.concatenate(
        [w[:, 0:320], jnp.where(inner, w[:, 256:576], zero), jnp.where(inner, w[:, 512:832], zero)], axis=0
    )


def forward_layer(
    layer, x_ref, wedge_ref, wpre_ref, bias, wpost_ref, wmix_ref, b_ref, live_ref, rows_ref, g_ref, gt_ref,
    m_ref, s_ref, z_ref, y_ref, u_ref, part_ref, a_ref, ya_ref,
):
    width, nodes = x_ref.shape
    leaf_cols = LEAF_SLOTS * nodes
    x = x_ref[...]
    g = g_ref[...]
    own = mm(wpre_ref[layer, 0:width], x, TN) + bias
    a_ref[:, 0:nodes] = mm(wpre_ref[layer, width : 2 * width], x, TN).astype(BF16)
    wedge = wedge_ref[layer]
    both = mm(wpre_ref[layer, 2 * width :], jnp.concatenate([wedge] * 4, axis=0), TT)
    high, rest = split_two(both)
    a_ref[:, nodes : nodes + 64] = jnp.where(iota((width, 64), 1) < 32, high, rest)
    own_high, own_rest = split_two(own)
    own_h = mm(own_high, g) + mm(own_rest, g)
    a = a_ref[...]
    for k in range(LEAF_SLOTS):
        lo = k * nodes
        m_ref[:, lo : lo + nodes] = mm(a, b_ref[:, lo : lo + nodes]) + own
    for j in range(8):
        lo = leaf_cols + 128 * j
        m_ref[:, lo : lo + 128] = mm(a, b_ref[:, lo : lo + 128]) + own_h
    x_h = mm(x, g).astype(BF16)
    for t in range(4):
        z_ref[320 * t : 320 * t + 64, 0:nodes] = x[64 * t : 64 * t + 64]
        z_ref[320 * t : 320 * t + 64, nodes:] = x_h[64 * t : 64 * t + 64]

    def summarize(msgs, lives, inv, folded):
        def total(parts, op):
            acc = parts[0]
            for p in parts[1:]:
                acc = op(acc, p)
            return fold(acc, op) if folded else acc

        mean = total([jnp.where(l, m, 0.0) for m, l in zip(msgs, lives)], jnp.add) * inv
        square = total([jnp.where(l, (m - mean) * (m - mean), 0.0) for m, l in zip(msgs, lives)], jnp.add)
        std = jnp.sqrt(square * inv + SPREAD_OFFSET)
        ups = [jnp.where(l, m, -1e30) for m, l in zip(msgs, lives)]
        top = total(ups, jnp.maximum)
        smax = top + jnp.log(total([jnp.exp(m - top) for m in ups], jnp.add))
        downs = [jnp.where(l, m, 1e30) for m, l in zip(msgs, lives)]
        low = total(downs, jnp.minimum)
        smin = low - jnp.log(total([jnp.exp(low - m) for m in downs], jnp.add))
        return mean, smax, smin, std

    def row_step(i, _):
        r = pl.multiple_of(i * 16, 16)
        zr = pl.multiple_of((i // 4) * 320 + 64 + (i % 4) * 16, 16)
        for c in range(nodes // 128 + 1):
            lanes = slice(128 * c, 128 * c + 128)
            if c < nodes // 128:
                cols = [k * nodes + 128 * c for k in range(LEAF_SLOTS)]
            else:
                cols = [leaf_cols + 128 * j for j in range(8)]
            msgs = [m_ref[pl.ds(r, 16), lo : lo + 128] for lo in cols]
            lives = [live_ref[0:1, lo : lo + 128] > 0 for lo in cols]
            stats = summarize(msgs, lives, rows_ref[2:3, lanes], c == nodes // 128)
            if c == nodes // 128:
                stats = [jnp.where(rows_ref[5:6, lanes] > 0, s, 0.0) for s in stats]
            for n, s in enumerate(stats):
                s_ref[n, pl.ds(r, 16), lanes] = s
                z_ref[pl.ds(zr + 64 * n, 16), lanes] = s.astype(BF16)
        return 0

    lax.fori_loop(0, width // 16, row_step, 0)

    amp, att = rows_ref[0:1], rows_ref[1:2]
    for t in range(4):
        r = mm(tower_weights(wpost_ref, layer, t), z_ref[320 * t : 320 * t + 320])
        ya_ref[64 * t : 64 * t + 64] = (r[0:64] + amp * r[64:128] + att * r[128:192]).astype(BF16)
    spread_out = mm(ya_ref[:, nodes:], gt_ref[...])
    y = jnp.where(rows_ref[5:6, 0:nodes] > 0, spread_out, ya_ref[:, 0:nodes].astype(F32)).astype(BF16)
    y_ref[...] = y
    u = mm(wmix_ref[layer], y, TN)
    u_ref[...] = u
    alive = rows_ref[3:4, 0:nodes]
    count = jnp.sum(alive, axis=1, keepdims=True)
    mean = jnp.sum(alive * u, axis=1, keepdims=True) / count
    off = u - mean
    square = jnp.sum(alive * off * off, axis=1, keepdims=True)
    row = jnp.concatenate([to_row(mean), to_row(square), jnp.broadcast_to(count, (1, 128))], axis=1)
    part_ref[...] = jnp.broadcast_to(row[None], part_ref.shape)


def forward_first_kernel(
    layer, nf_ref, ef_ref, seg_ref, nbr_ref, mask_ref, deg_ref, wedge_ref, wpre_ref, bpre_ref, wpost_ref, wmix_ref,
    x_ref, b_ref, live_ref, rows_ref, g_ref, gt_ref, m_ref, s_ref, z_ref, y_ref, u_ref, part_ref,
    a_ref, ya_ref,
):
    build_tables(ef_ref, seg_ref, nbr_ref, mask_ref, deg_ref, b_ref, live_ref, rows_ref, g_ref, gt_ref)
    x_ref[...] = nf_ref[...].T
    forward_layer(
        layer, x_ref, wedge_ref, wpre_ref, to_col(bpre_ref[layer : layer + 1]), wpost_ref, wmix_ref, b_ref, live_ref, rows_ref,
        g_ref, gt_ref, m_ref, s_ref, z_ref, y_ref, u_ref, part_ref, a_ref, ya_ref,
    )


def norm_rows(recv_ref):
    w = (recv_ref.shape[2] - 128) // 2
    recv = recv_ref[...]
    means, squares = recv[:, :, 0:w], recv[:, :, w : 2 * w]
    counts = jnp.concatenate([recv[:, :, 2 * w :]] * (w // 128), axis=2)
    total = jnp.sum(counts, axis=0)
    mean = jnp.sum(counts * means, axis=0) / total
    off = means - mean[None]
    var = jnp.sum(squares + counts * off * off, axis=0) / total
    return mean, lax.rsqrt(var + STABILITY_FLOOR), total


def normed(u, norm_ref, gain_ref, bias_ref, layer):
    xh = (u - to_col(norm_ref[0:1])) * to_col(norm_ref[1:2])
    v = xh * to_col(gain_ref[layer : layer + 1]) + to_col(bias_ref[layer : layer + 1])
    return xh, v


def store_norm(norm_ref, recv_ref):
    mean, scale, total = norm_rows(recv_ref)
    norm_ref[...] = jnp.zeros_like(norm_ref)
    norm_ref[0:1] = mean
    norm_ref[1:2] = scale
    norm_ref[2:3] = total


def forward_next_kernel(
    layer, recv_ref, u0_ref, x0_ref, gain_ref, bias_ref, wedge_ref, wpre_ref, bpre_ref, wpost_ref, wmix_ref,
    b_ref, live_ref, rows_ref, g_ref, gt_ref,
    norm_ref, h_ref, x_ref, m_ref, s_ref, z_ref, y_ref, u_ref, part_ref,
    a_ref, ya_ref,
):
    store_norm(norm_ref, recv_ref)
    _, v = normed(u0_ref[...], norm_ref, gain_ref, bias_ref, layer - 1)
    h = x0_ref[...].astype(F32) + v / (1.0 + jnp.exp(-v))
    h_ref[...] = h
    x_ref[...] = h.astype(BF16)
    forward_layer(
        layer, x_ref, wedge_ref, wpre_ref, to_col(bpre_ref[layer : layer + 1]), wpost_ref, wmix_ref, b_ref, live_ref,
        rows_ref, g_ref, gt_ref, m_ref, s_ref, z_ref, y_ref, u_ref, part_ref, a_ref, ya_ref,
    )


def gate_grad(dh, xh, v, dv_ref, part_ref):
    sig = 1.0 / (1.0 + jnp.exp(-v))
    dv = dh * sig * (1.0 + v * (1.0 - sig))
    dv_ref[...] = dv
    sums = [jnp.sum(p, axis=1, keepdims=True) for p in (dv, dv * xh)]
    row = jnp.concatenate([to_row(s) for s in sums], axis=1)
    part_ref[...] = jnp.broadcast_to(row[None], part_ref.shape)


def readout_kernel(
    layer, recv_ref, u_ref, h_ref, gain_ref, bias_ref, seg_ref, rg_ref,
    norm_ref, readout_ref, dh_ref, dv_ref, part_ref,
):
    store_norm(norm_ref, recv_ref)
    xh, v = normed(u_ref[...], norm_ref, gain_ref, bias_ref, layer)
    h = h_ref[...] + v / (1.0 + jnp.exp(-v))
    nodes = h.shape[1]
    seeds = rg_ref.shape[0]
    belong = (iota((8, nodes), 0) == seg_ref[...]).astype(F32)
    readout = lax.dot_general(belong, h, NT, precision=lax.Precision.HIGHEST, preferred_element_type=F32)
    readout_ref[...] = readout[0:seeds] / SUB_MAX
    dh = jnp.zeros(h.shape, F32)
    for s in range(seeds):
        dh = dh + to_col(rg_ref[s : s + 1]) * belong[s : s + 1]
    dh = dh / SUB_MAX
    dh_ref[...] = dh
    gate_grad(dh, xh, v, dv_ref, part_ref)


def backward_layer(
    layer, recv_ref, dv_ref, dh_ref, u_ref, norm_ref, gain_ref, bias_ref, wmix_ref, wpost_ref, wpre_ref,
    b_ref, live_ref, rows_ref, g_ref, gt_ref, m_ref, s_ref,
    gb_ref, du_ref, d_ref, dm_ref, dcat_ref, et_ref, ds_ref, acc_ref, bd_ref,
):
    width, nodes = dv_ref.shape
    leaf_cols = LEAF_SLOTS * nodes
    sums = jnp.sum(recv_ref[...], axis=0)
    g_bias, g_gain = sums[:, 0:width], sums[:, width:]
    gb_ref[...] = sums
    count = norm_ref[2:3, 0:1]
    xh, _ = normed(u_ref[...], norm_ref, gain_ref, bias_ref, layer)
    alive = rows_ref[3:4, 0:nodes]
    scale = to_col(norm_ref[1:2] * gain_ref[layer : layer + 1])
    du = scale * (dv_ref[...] - alive * (to_col(g_bias) + xh * to_col(g_gain)) / count)
    du = du.astype(BF16)
    du_ref[...] = du
    dy = mm(wmix_ref[layer], du)
    dy_low = dy.astype(BF16)
    dcat_ref[2 * width :] = dy_low
    dy_h = mm(dy_low, g_ref[...])
    keep = rows_ref[4:5]
    amp, att = rows_ref[0:1], rows_ref[1:2]
    dy_all = jnp.concatenate([dy_low.astype(F32), dy_h], axis=1) * keep
    bd_ref[...] = jnp.zeros_like(bd_ref)
    for t in range(4):
        part = dy_all[64 * t : 64 * t + 64]
        d_ref[192 * t : 192 * t + 64] = part.astype(BF16)
        d_ref[192 * t + 64 : 192 * t + 128] = (part * amp).astype(BF16)
        d_ref[192 * t + 128 : 192 * t + 192] = (part * att).astype(BF16)
        w = tower_weights(wpost_ref, layer, t)
        dz = mm(w, d_ref[192 * t : 192 * t + 192], TN)
        for n in range(4):
            rows = slice(64 * t, 64 * t + 64)
            block = dz[64 * (n + 1) : 64 * (n + 2)]
            ds_ref[n, rows, 0:nodes] = block[:, 0:nodes]
            ds_ref[n, rows, nodes:] = fold(block[:, nodes:], jnp.add)
        bd_ref[64 * t : 64 * t + 64, 64 * t : 64 * t + 64] = wpost_ref[layer, t][:, 0:64]

    def row_step(i, _):
        r = pl.multiple_of(i * 16, 16)
        for c in range(nodes // 128 + 1):
            lanes = slice(128 * c, 128 * c + 128)
            if c < nodes // 128:
                cols = [k * nodes + 128 * c for k in range(LEAF_SLOTS)]
            else:
                cols = [leaf_cols + 128 * j for j in range(8)]
            mean, smax, smin, std = (s_ref[n, pl.ds(r, 16), lanes] for n in range(4))
            dmean, dsmax, dsmin, dstd = (ds_ref[n, pl.ds(r, 16), lanes] for n in range(4))
            inv = rows_ref[2:3, lanes]
            c0 = dmean * inv
            c1 = dstd * inv / std
            acc = None
            for lo in cols:
                m = m_ref[pl.ds(r, 16), lo : lo + 128]
                d = c0 + (m - mean) * c1 + dsmax * jnp.exp(m - smax) + dsmin * jnp.exp(smin - m)
                d = jnp.where(live_ref[0:1, lo : lo + 128] > 0, d, 0.0)
                acc = d if acc is None else acc + d
                dm_ref[pl.ds(r, 16), lo : lo + 128] = d.astype(BF16)
            if c == nodes // 128:
                acc = fold(acc, jnp.add)
            acc_ref[pl.ds(r, 16), lanes] = acc
        return 0

    lax.fori_loop(0, width // 16, row_step, 0)

    down = acc_ref[:, 0:nodes] + mm(acc_ref[:, nodes:].astype(BF16), gt_ref[...])
    dcat_ref[0:width] = down.astype(BF16)
    landed = mm(dm_ref[...], b_ref[0 : nodes + 32], NT)
    dcat_ref[width : 2 * width] = landed[:, 0:nodes].astype(BF16)
    et_ref[...] = landed[:, nodes : nodes + 16] + landed[:, nodes + 16 : nodes + 32]
    weights = jnp.concatenate([wpre_ref[layer, 0:width], wpre_ref[layer, width : 2 * width]], axis=1)
    dh = mm(weights, dcat_ref[0 : 2 * width])
    dh = dh + mm(bd_ref[...], dcat_ref[2 * width :], TN)
    return dh_ref[...] + dh


def backward_first_kernel(
    layer, recv_ref, dv_ref, dh_ref, u_ref, norm_ref, gain_ref, bias_ref, wmix_ref, wpost_ref, wpre_ref,
    b_ref, live_ref, rows_ref, g_ref, gt_ref, m_ref, s_ref, u_low_ref, norm_low_ref,
    gb_ref, du_ref, d_ref, dm_ref, dcat_ref, et_ref, acc_ref, dh_out_ref, dv_out_ref, part_ref,
    ds_ref, bd_ref,
):
    dh = backward_layer(
        layer, recv_ref, dv_ref, dh_ref, u_ref, norm_ref, gain_ref, bias_ref, wmix_ref, wpost_ref, wpre_ref,
        b_ref, live_ref, rows_ref, g_ref, gt_ref, m_ref, s_ref,
        gb_ref, du_ref, d_ref, dm_ref, dcat_ref, et_ref, ds_ref, acc_ref, bd_ref,
    )
    dh_out_ref[...] = dh
    xh, v = normed(u_low_ref[...], norm_low_ref, gain_ref, bias_ref, layer - 1)
    gate_grad(dh, xh, v, dv_out_ref, part_ref)


def backward_last_kernel(
    layer, recv_ref, dv_ref, dh_ref, u_ref, norm_ref, gain_ref, bias_ref, wmix_ref, wpost_ref, wpre_ref,
    b_ref, live_ref, rows_ref, g_ref, gt_ref, m_ref, s_ref,
    gb_ref, du_ref, d_ref, dm_ref, dcat_ref, et_ref, acc_ref, node_ref,
    ds_ref, bd_ref,
):
    dh = backward_layer(
        layer, recv_ref, dv_ref, dh_ref, u_ref, norm_ref, gain_ref, bias_ref, wmix_ref, wpost_ref, wpre_ref,
        b_ref, live_ref, rows_ref, g_ref, gt_ref, m_ref, s_ref,
        gb_ref, du_ref, d_ref, dm_ref, dcat_ref, et_ref, ds_ref, acc_ref, bd_ref,
    )
    node_ref[...] = dh.T


def weight_kernel(y_ref, du_ref, d_ref, z_ref, x_ref, dcat_ref, et_ref, acc_ref, grads_ref):
    width, nodes = x_ref.shape
    for t in range(4):
        r = mm(d_ref[192 * t : 192 * t + 192], z_ref[320 * t : 320 * t + 320], NT)
        rows = slice(64 * t, 64 * t + 64)
        inner = iota((64, 320), 1) >= 64
        grads_ref[rows, 0:256] = r[0:64, 0:256]
        grads_ref[rows, 256:512] = jnp.where(
            iota((64, 256), 1) < 64, jnp.concatenate([r[0:64, 256:320]] * 4, axis=1), r[64:128, 0:256]
        )
        grads_ref[rows, 512:768] = jnp.where(
            iota((64, 256), 1) < 64, jnp.concatenate([r[64:128, 256:320]] * 4, axis=1), r[128:192, 0:256]
        )
        grads_ref[rows, 768:832] = r[128:192, 256:320]
    leaf_and_hub = acc_ref[...] * jnp.where(
        iota((1, acc_ref.shape[1]), 1) < nodes + 64, 1.0, 0.0
    )
    bias = jnp.sum(leaf_and_hub, axis=1, keepdims=True)
    grads_ref[:, 832:848] = et_ref[...]
    grads_ref[:, 848:896] = jnp.broadcast_to(bias, (width, 48))
    grads_ref[:, 896:1152] = mm(y_ref[...], du_ref[...], NT)
    both = mm(x_ref[...], dcat_ref[0 : 2 * width], NT)
    grads_ref[:, 1152:1664] = both


def edge_kernel(dm0_ref, dm1_ref, wpre_ref, wedge_ref, gt_ref, out_ref, acc_ref):
    width = dm0_ref.shape[0]
    nodes = gt_ref.shape[1]
    leaf_cols = LEAF_SLOTS * nodes
    total = None
    for layer, dm_ref in ((0, dm0_ref), (1, dm1_ref)):
        w = mm(wedge_ref[layer], wpre_ref[layer, 2 * width :]).astype(BF16)
        part = mm(w, dm_ref[...])
        total = part if total is None else total + part
    hub = total[:, leaf_cols:]
    for j in range(8):
        acc_ref[32 * j : 32 * j + 16] = hub[:, 128 * j : 128 * j + 128]
        acc_ref[32 * j + 16 : 32 * j + 32] = pltpu.roll(hub[:, 128 * j : 128 * j + 128], 64, 1)
    high, rest = split_two(acc_ref[...])
    gt = gt_ref[...]
    spread_out = mm(high, gt) + mm(rest, gt)
    leaf = jnp.concatenate([total[:, k * nodes : (k + 1) * nodes] for k in range(LEAF_SLOTS)], axis=0)
    out = jnp.concatenate([spread_out[0:64] + leaf, spread_out[64:]], axis=0)
    out_ref[...] = out.T


def finish_kernel(g0_ref, g1_ref, wedge_ref, wpre_ref, gedge_ref, gpre_ref, gb_ref, gpost_ref, gmix_ref):
    width = wpre_ref.shape[2]
    for layer, g_ref in ((0, g0_ref), (1, g1_ref)):
        for t in range(4):
            gpost_ref[layer, t] = g_ref[64 * t : 64 * t + 64, 0:832]
        gmix_ref[layer] = g_ref[:, 896:1152]
        gpre_ref[layer, 0:width] = g_ref[:, 1152:1408]
        gpre_ref[layer, width : 2 * width] = g_ref[:, 1408:1664]
        gb_ref[layer : layer + 1] = to_row(g_ref[:, 848:849])
        et = g_ref[:, 832:848]
        wedge = wedge_ref[layer].astype(F32)
        hi = dict(precision=lax.Precision.HIGHEST, preferred_element_type=F32)
        gpre_ref[layer, 2 * width :] = lax.dot_general(wedge, et, TT, **hi)
        gedge_ref[layer] = lax.dot_general(et, wpre_ref[layer, 2 * width :].astype(F32), TT, **hi)


def on_device(
    devices, node_feats, edge_feats, segment_ids, neighbours, nbr_mask, degrees, w_edge, w_pre, b_pre, w_post,
    w_mix, bn_gain, bn_bias, readout_grad,
):
    nodes, width = node_feats.shape
    lanes = nodes + 128
    cols = LEAF_SLOTS * nodes + 1024
    inner = nodes + 64
    seg = segment_ids.reshape(1, nodes)
    deg = degrees.reshape(1, nodes)
    nbr_t = neighbours.T
    mask_t = nbr_mask.T
    wpost_t = jnp.swapaxes(w_post, 2, 3)

    def s(shape, dtype=F32):
        return jax.ShapeDtypeStruct(shape, dtype)

    whole = pl.BlockSpec(memory_space=pltpu.VMEM)

    def call(kernel, args, outs, scratch=(), limit=40):
        return pl.pallas_call(
            kernel,
            in_specs=[whole] * len(args),
            out_specs=[whole] * len(outs),
            out_shape=outs,
            scratch_shapes=list(scratch),
            compiler_params=pltpu.CompilerParams(vmem_limit_bytes=limit * 1024 * 1024),
        )(*args)

    def exchange(part):
        return lax.all_to_all(part, "dp", 0, 0, tiled=True)

    layer_outs = [
        s((width, cols)), s((4, width, lanes)), s((4 * 320, lanes), BF16), s((width, nodes), BF16),
        s((width, nodes)), s((devices, 1, 2 * width + 128)),
    ]
    fwd_scratch = [pltpu.VMEM((width, inner), BF16), pltpu.VMEM((width, lanes), BF16)]
    table_outs = [
        s((inner, cols), BF16), s((1, cols)), s((8, lanes)), s((nodes, 128), BF16), s((128, nodes), BF16),
    ]
    x0, b, live, rows, g, gt, m0, s0, z0, y0, u0, part = call(
        functools.partial(forward_first_kernel, 0),
        [node_feats, edge_feats, seg, nbr_t, mask_t, deg, w_edge, w_pre, b_pre, wpost_t, w_mix],
        [s((width, nodes), BF16)] + table_outs + layer_outs,
        fwd_scratch,
    )
    tables = [b, live, rows, g, gt]
    recv = exchange(part)
    norm0, h1, x1, m1, s1, z1, y1, u1, part = call(
        functools.partial(forward_next_kernel, 1),
        [recv, u0, x0, bn_gain, bn_bias, w_edge, w_pre, b_pre, wpost_t, w_mix] + tables,
        [s((8, width)), s((width, nodes)), s((width, nodes), BF16)] + layer_outs,
        fwd_scratch,
    )
    recv = exchange(part)
    sums_out = s((devices, 1, 2 * width))
    norm1, readout, dh2, dv1, part = call(
        functools.partial(readout_kernel, 1),
        [recv, u1, h1, bn_gain, bn_bias, seg, readout_grad],
        [s((8, width)), s(readout_grad.shape), s((width, nodes)), s((width, nodes)), sums_out],
    )
    back_outs = [
        s((1, 2 * width)), s((width, nodes), BF16), s((4 * 192, lanes), BF16), s((width, cols), BF16),
        s((3 * width, nodes), BF16), s((width, 16)), s((width, lanes)),
    ]
    back_scratch = [pltpu.VMEM((4, width, lanes), F32), pltpu.VMEM((width, width), BF16)]
    recv = exchange(part)
    sums1, du1, d1, dm1, dcat1, et1, acc1, dh1, dv0, part = call(
        functools.partial(backward_first_kernel, 1),
        [recv, dv1, dh2, u1, norm1, bn_gain, bn_bias, w_mix, wpost_t, w_pre] + tables + [m1, s1, u0, norm0],
        back_outs + [s((width, nodes)), s((width, nodes)), sums_out],
        back_scratch,
    )
    recv = exchange(part)
    weight_out = [s((width, 1664))]
    grads1 = call(weight_kernel, [y1, du1, d1, z1, x1, dcat1, et1, acc1], weight_out)[0]
    sums0, du0, d0, dm0, dcat0, et0, acc0, node_grad = call(
        functools.partial(backward_last_kernel, 0),
        [recv, dv0, dh1, u0, norm0, bn_gain, bn_bias, w_mix, wpost_t, w_pre] + tables + [m0, s0],
        back_outs + [s((nodes, width))],
        back_scratch,
    )
    grads0 = call(weight_kernel, [y0, du0, d0, z0, x0, dcat0, et0, acc0], weight_out)[0]
    edge_grad = call(
        edge_kernel, [dm0, dm1, w_pre, w_edge, gt], [s((nodes, width))], [pltpu.VMEM((width, 128), F32)]
    )[0]

    def reduce_all(grads):
        rows_each = width // devices if width >= devices else 1
        pieces = grads.reshape(devices, rows_each, grads.shape[1])
        mine = jnp.sum(lax.all_to_all(pieces, "dp", 0, 0, tiled=True), axis=0)
        spread_out = jnp.broadcast_to(mine[None], pieces.shape)
        return lax.all_to_all(spread_out, "dp", 0, 0, tiled=True).reshape(grads.shape)

    total1 = reduce_all(grads1)
    total0 = reduce_all(grads0)
    layers = w_pre.shape[0]
    g_edge, g_pre, g_b, g_post_t, g_mix = call(
        finish_kernel, [total0, total1, w_edge, w_pre],
        [s(w_edge.shape), s(w_pre.shape), s(b_pre.shape), s((layers, 4, 64, 832)), s(w_mix.shape)],
    )
    sums = jnp.concatenate([sums0, sums1], axis=0)
    return (
        readout, node_grad, edge_grad, g_edge, g_pre, g_b, jnp.swapaxes(g_post_t, 2, 3), g_mix,
        sums[:, width:], sums[:, :width],
    )


def solution(mesh):
    split, split2, full = P("dp"), P("dp", None), P()
    in_specs = (split2, split2, split, split2, split2, split) + (full,) * 7 + (split2,)
    out_specs = (split2, split2, split2) + (full,) * 7
    return jax.shard_map(
        functools.partial(on_device, mesh.shape["dp"]),
        mesh=mesh, in_specs=in_specs, out_specs=out_specs, check_vma=False,
    )
```

```python
import functools

import jax
import jax.numpy as jnp
from jax import lax
from jax.experimental import pallas as pl
from jax.experimental.pallas import tpu as pltpu
from jax.sharding import PartitionSpec as P

SUB_MAX = 160
DEGREE_CENTER = 2.0
SPREAD_OFFSET = 0.25
STABILITY_FLOOR = 1e-05

LEAF_SLOTS = 4
HUB_RANK = 16
F32 = jnp.float32
BF16 = jnp.bfloat16
NN = (((1,), (0,)), ((), ()))
NT = (((1,), (1,)), ((), ()))
TN = (((0,), (0,)), ((), ()))
TT = (((0,), (1,)), ((), ()))


def mm(a, b, dims=NN):
    return lax.dot_general(a, b, dims, preferred_element_type=F32)


def iota(shape, dim):
    return lax.broadcasted_iota(jnp.int32, shape, dim)


def to_col(row):
    f = row.shape[1]
    return jnp.sum(jnp.where(iota((f, f), 0) == iota((f, f), 1), row, 0.0), axis=1, keepdims=True)


def to_row(col):
    f = col.shape[0]
    return jnp.sum(jnp.where(iota((f, f), 0) == iota((f, f), 1), col, 0.0), axis=0, keepdims=True)


def fold(value, op):
    return op(value, pltpu.roll(value, 64, 1))


def split_two(value):
    high = value.astype(BF16)
    return high, (value - high.astype(F32)).astype(BF16)


def start_copies(pairs, sems):
    copies = [pltpu.make_async_copy(src, dst, sems.at[i]) for i, (src, dst) in enumerate(pairs)]
    for copy in copies:
        copy.start()
    return copies


def wait_all(copies):
    for copy in copies:
        copy.wait()


def build_tables(ef_ref, seg_ref, nbr_ref, mask_ref, deg_ref, b_ref, live_ref, rows_ref, g_ref, gt_ref):
    nodes = seg_ref.shape[1]
    seg = seg_ref[...]
    lane_h = iota((1, 128), 1)
    sub_h = iota((128, 1), 0)
    node_row = jnp.zeros((1, 128), jnp.int32)
    node_col = jnp.zeros((128, 1), jnp.int32)
    lane_r, sub_r = lane_h & 15, sub_h & 15
    lane_s, sub_s = (lane_h >> 4) & 3, (sub_h >> 4) & 3
    below = [jnp.sum((seg < s).astype(jnp.int32), axis=1, keepdims=True) for s in range(5)]
    for s in range(4):
        start, size = below[s], below[s + 1] - below[s]
        node_row = jnp.where(lane_s == s, jnp.where(lane_r < size, start + lane_r, -1), node_row)
        node_col = jnp.where(sub_s == s, jnp.where(sub_r < size, start + sub_r, -1), node_col)
    node_col = jnp.where(sub_h < 64, node_col, -1)
    g = (iota((nodes, 128), 0) == node_row).astype(F32).astype(BF16)
    gt = (iota((128, nodes), 1) == node_col).astype(F32).astype(BF16)
    g_ref[...] = g
    gt_ref[...] = gt
    is_hub = jnp.sum(gt.astype(F32), axis=0, keepdims=True)

    nbr = nbr_ref[...]
    mask = (mask_ref[...] > 0).astype(F32)
    nbr_h = (
        mm((nbr >> 3).astype(F32).astype(BF16), g) * 8.0 + mm((nbr & 7).astype(F32).astype(BF16), g)
    ).astype(jnp.int32)
    mask_h = mm(mask.astype(BF16), g)
    valid = (node_row >= 0).astype(F32)
    first = (lane_h < 64).astype(F32)

    def degree_rows(deg):
        log_degree = jnp.log(deg + 1.0)
        return log_degree / DEGREE_CENTER, DEGREE_CENTER / log_degree

    deg = deg_ref[...].astype(F32)
    deg_h = mm(jnp.broadcast_to(deg, (8, nodes)).astype(BF16), g)[0:1]
    deg_h = jnp.where(valid > 0, deg_h, 1.0)
    amp, att = degree_rows(deg)
    amp_h, att_h = degree_rows(deg_h)
    filled = jnp.sum(mask, axis=0, keepdims=True)
    filled_h = jnp.maximum(jnp.sum(mask_h, axis=0, keepdims=True), 1.0)
    rows_ref[...] = jnp.zeros_like(rows_ref)
    for i, (leaf, hub) in enumerate(
        (
            (amp, amp_h),
            (att, att_h),
            (1.0 / filled, 1.0 / filled_h),
            ((seg < 4).astype(F32), None),
            (1.0 - is_hub, valid * first),
            (is_hub, valid),
        )
    ):
        rows_ref[i : i + 1, 0:nodes] = leaf
        if hub is not None:
            rows_ref[i : i + 1, nodes : nodes + 128] = hub

    ef_t = ef_ref[...].T
    ef_h = mm(ef_t, g).astype(BF16)
    node_iota = iota((nodes, nodes), 0)
    hub_iota = iota((nodes, 128), 0)
    zero16 = jnp.zeros((16, nodes), BF16)
    for k in range(LEAF_SLOTS):
        lo = k * nodes
        b_ref[0:nodes, lo : lo + nodes] = (node_iota == nbr[k : k + 1]).astype(F32).astype(BF16)
        piece = ef_t[16 * k : 16 * k + 16]
        for r, part in enumerate((piece, zero16, piece, zero16)):
            b_ref[nodes + 16 * r : nodes + 16 * r + 16, lo : lo + nodes] = part
        live_ref[0:1, lo : lo + nodes] = mask[k : k + 1]
    own_half = (iota((32, 128), 0) < 16) == (iota((32, 128), 1) < 64)
    for j in range(8):
        lo = LEAF_SLOTS * nodes + 128 * j
        index = jnp.where(lane_h < 64, nbr_h[2 * j : 2 * j + 1], nbr_h[2 * j + 1 : 2 * j + 2])
        b_ref[0:nodes, lo : lo + 128] = (hub_iota == index).astype(F32).astype(BF16)
        piece = jnp.where(own_half, ef_h[32 * j : 32 * j + 32].astype(F32), 0.0).astype(BF16)
        b_ref[nodes : nodes + 32, lo : lo + 128] = piece
        b_ref[nodes + 32 : nodes + 64, lo : lo + 128] = piece
        live_ref[0:1, lo : lo + 128] = jnp.where(
            lane_h < 64, mask_h[2 * j : 2 * j + 1], mask_h[2 * j + 1 : 2 * j + 2]
        )


def tower_weights(wpost_ref, layer, t):
    w = wpost_ref[layer, t]
    inner = iota((64, 320), 1) >= 64
    zero = jnp.zeros((64, 320), BF16)
    return jnp.concatenate(
        [w[:, 0:320], jnp.where(inner, w[:, 256:576], zero), jnp.where(inner, w[:, 512:832], zero)], axis=0
    )


def forward_layer(
    layer, x_ref, wedge_ref, wpre_ref, bias, wpost_ref, wmix_ref, b_ref, live_ref, rows_ref, g_ref, gt_ref,
    outs, y_ref, u_ref, part_ref, m_ref, s_ref, z_ref, a_ref, ya_ref, out_sems, ready=lambda: None,
):
    m_out, s_out, z_out = outs
    width, nodes = x_ref.shape
    leaf_cols = LEAF_SLOTS * nodes
    x = x_ref[...]
    g = g_ref[...]
    own = mm(wpre_ref[layer, 0:width], x, TN) + bias
    a_ref[:, 0:nodes] = mm(wpre_ref[layer, width : 2 * width], x, TN).astype(BF16)
    wedge = wedge_ref[layer]
    both = mm(wpre_ref[layer, 2 * width :], jnp.concatenate([wedge] * 4, axis=0), TT)
    high, rest = split_two(both)
    a_ref[:, nodes : nodes + 64] = jnp.where(iota((width, 64), 1) < 32, high, rest)
    own_high, own_rest = split_two(own)
    own_h = mm(own_high, g) + mm(own_rest, g)
    ready()
    a = a_ref[...]
    for k in range(LEAF_SLOTS):
        lo = k * nodes
        m_ref[:, lo : lo + nodes] = mm(a, b_ref[:, lo : lo + nodes]) + own
    for j in range(8):
        lo = leaf_cols + 128 * j
        m_ref[:, lo : lo + 128] = mm(a, b_ref[:, lo : lo + 128]) + own_h
    copies = start_copies([(m_ref, m_out)], out_sems)
    x_h = mm(x, g).astype(BF16)
    for t in range(4):
        z_ref[320 * t : 320 * t + 64, 0:nodes] = x[64 * t : 64 * t + 64]
        z_ref[320 * t : 320 * t + 64, nodes:] = x_h[64 * t : 64 * t + 64]

    def summarize(msgs, lives, inv, folded):
        def total(parts, op):
            acc = parts[0]
            for p in parts[1:]:
                acc = op(acc, p)
            return fold(acc, op) if folded else acc

        mean = total([jnp.where(l, m, 0.0) for m, l in zip(msgs, lives)], jnp.add) * inv
        square = total([jnp.where(l, (m - mean) * (m - mean), 0.0) for m, l in zip(msgs, lives)], jnp.add)
        std = jnp.sqrt(square * inv + SPREAD_OFFSET)
        ups = [jnp.where(l, m, -1e30) for m, l in zip(msgs, lives)]
        top = total(ups, jnp.maximum)
        smax = top + jnp.log(total([jnp.exp(m - top) for m in ups], jnp.add))
        downs = [jnp.where(l, m, 1e30) for m, l in zip(msgs, lives)]
        low = total(downs, jnp.minimum)
        smin = low - jnp.log(total([jnp.exp(low - m) for m in downs], jnp.add))
        return mean, smax, smin, std

    def row_step(i, _):
        r = pl.multiple_of(i * 16, 16)
        zr = pl.multiple_of((i // 4) * 320 + 64 + (i % 4) * 16, 16)
        for c in range(nodes // 128 + 1):
            lanes = slice(128 * c, 128 * c + 128)
            if c < nodes // 128:
                cols = [k * nodes + 128 * c for k in range(LEAF_SLOTS)]
            else:
                cols = [leaf_cols + 128 * j for j in range(8)]
            msgs = [m_ref[pl.ds(r, 16), lo : lo + 128] for lo in cols]
            lives = [live_ref[0:1, lo : lo + 128] > 0 for lo in cols]
            stats = summarize(msgs, lives, rows_ref[2:3, lanes], c == nodes // 128)
            if c == nodes // 128:
                stats = [jnp.where(rows_ref[5:6, lanes] > 0, s, 0.0) for s in stats]
            for n, s in enumerate(stats):
                s_ref[n, pl.ds(r, 16), lanes] = s
                z_ref[pl.ds(zr + 64 * n, 16), lanes] = s.astype(BF16)
        return 0

    lax.fori_loop(0, width // 16, row_step, 0)
    copies += start_copies([(s_ref, s_out), (z_ref, z_out)], out_sems.at[1:3])

    amp, att = rows_ref[0:1], rows_ref[1:2]
    for t in range(4):
        r = mm(tower_weights(wpost_ref, layer, t), z_ref[320 * t : 320 * t + 320])
        ya_ref[64 * t : 64 * t + 64] = (r[0:64] + amp * r[64:128] + att * r[128:192]).astype(BF16)
    spread_out = mm(ya_ref[:, nodes:], gt_ref[...])
    y = jnp.where(rows_ref[5:6, 0:nodes] > 0, spread_out, ya_ref[:, 0:nodes].astype(F32)).astype(BF16)
    y_ref[...] = y
    u = mm(wmix_ref[layer], y, TN)
    u_ref[...] = u
    alive = rows_ref[3:4, 0:nodes]
    count = jnp.sum(alive, axis=1, keepdims=True)
    mean = jnp.sum(alive * u, axis=1, keepdims=True) / count
    off = u - mean
    square = jnp.sum(alive * off * off, axis=1, keepdims=True)
    row = jnp.concatenate([to_row(mean), to_row(square), jnp.broadcast_to(count, (1, 128))], axis=1)
    part_ref[...] = jnp.broadcast_to(row[None], part_ref.shape)
    wait_all(copies)


def forward_first_kernel(
    layer, nf_hbm, ef_hbm, seg_ref, nbr_hbm, mask_hbm, deg_ref, wedge_hbm, wpre_hbm, bpre_hbm, wpost_hbm, wmix_hbm,
    x_ref, b_out, live_ref, rows_ref, g_ref, gt_ref, m_out, s_out, z_out, y_ref, u_ref, part_ref,
    m_ref, s_ref, z_ref, a_ref, ya_ref, out_sems, b_ref, nf_ref, ef_ref, nbr_ref, mask_ref, wedge_ref, wpre_ref,
    bpre_ref, wpost_ref, wmix_ref, in_sems, b_sem,
):
    loads = start_copies(
        [
            (nbr_hbm, nbr_ref), (mask_hbm, mask_ref), (ef_hbm, ef_ref), (nf_hbm, nf_ref), (wpre_hbm, wpre_ref),
            (wedge_hbm, wedge_ref), (bpre_hbm, bpre_ref), (wpost_hbm, wpost_ref), (wmix_hbm, wmix_ref),
        ],
        in_sems,
    )
    wait_all(loads[0:3])
    build_tables(ef_ref, seg_ref, nbr_ref, mask_ref, deg_ref, b_ref, live_ref, rows_ref, g_ref, gt_ref)
    stores = start_copies([(b_ref, b_out)], b_sem)
    wait_all(loads[3:])
    x_ref[...] = nf_ref[...].T
    forward_layer(
        layer, x_ref, wedge_ref, wpre_ref, to_col(bpre_ref[layer : layer + 1]), wpost_ref, wmix_ref, b_ref,
        live_ref, rows_ref, g_ref, gt_ref, (m_out, s_out, z_out), y_ref, u_ref, part_ref,
        m_ref, s_ref, z_ref, a_ref, ya_ref, out_sems,
    )
    wait_all(stores)


def norm_rows(recv_ref):
    w = (recv_ref.shape[2] - 128) // 2
    recv = recv_ref[...]
    means, squares = recv[:, :, 0:w], recv[:, :, w : 2 * w]
    counts = jnp.concatenate([recv[:, :, 2 * w :]] * (w // 128), axis=2)
    total = jnp.sum(counts, axis=0)
    mean = jnp.sum(counts * means, axis=0) / total
    off = means - mean[None]
    var = jnp.sum(squares + counts * off * off, axis=0) / total
    return mean, lax.rsqrt(var + STABILITY_FLOOR), total


def normed(u, norm_ref, gain_ref, bias_ref, layer):
    xh = (u - to_col(norm_ref[0:1])) * to_col(norm_ref[1:2])
    v = xh * to_col(gain_ref[layer : layer + 1]) + to_col(bias_ref[layer : layer + 1])
    return xh, v


def store_norm(norm_ref, recv_ref):
    mean, scale, total = norm_rows(recv_ref)
    norm_ref[...] = jnp.zeros_like(norm_ref)
    norm_ref[0:1] = mean
    norm_ref[1:2] = scale
    norm_ref[2:3] = total


def forward_next_kernel(
    layer, recv_ref, u0_ref, x0_ref, gain_ref, bias_ref, wedge_ref, wpre_ref, bpre_ref, wpost_ref, wmix_ref,
    b_hbm, live_ref, rows_ref, g_ref, gt_ref,
    norm_ref, h_ref, x_ref, m_out, s_out, z_out, y_ref, u_ref, part_ref,
    m_ref, s_ref, z_ref, a_ref, ya_ref, out_sems, b_ref, b_sem,
):
    loads = start_copies([(b_hbm, b_ref)], b_sem)
    store_norm(norm_ref, recv_ref)
    _, v = normed(u0_ref[...], norm_ref, gain_ref, bias_ref, layer - 1)
    h = x0_ref[...].astype(F32) + v / (1.0 + jnp.exp(-v))
    h_ref[...] = h
    x_ref[...] = h.astype(BF16)
    forward_layer(
        layer, x_ref, wedge_ref, wpre_ref, to_col(bpre_ref[layer : layer + 1]), wpost_ref, wmix_ref, b_ref,
        live_ref, rows_ref, g_ref, gt_ref, (m_out, s_out, z_out), y_ref, u_ref, part_ref,
        m_ref, s_ref, z_ref, a_ref, ya_ref, out_sems, lambda: wait_all(loads),
    )


def gate_grad(dh, xh, v, dv_ref, part_ref):
    sig = 1.0 / (1.0 + jnp.exp(-v))
    dv = dh * sig * (1.0 + v * (1.0 - sig))
    dv_ref[...] = dv
    sums = [jnp.sum(p, axis=1, keepdims=True) for p in (dv, dv * xh)]
    row = jnp.concatenate([to_row(s) for s in sums], axis=1)
    part_ref[...] = jnp.broadcast_to(row[None], part_ref.shape)


def readout_kernel(
    layer, recv_ref, u_ref, h_ref, gain_ref, bias_ref, seg_ref, rg_ref,
    norm_ref, readout_ref, dh_ref, dv_ref, part_ref,
):
    store_norm(norm_ref, recv_ref)
    xh, v = normed(u_ref[...], norm_ref, gain_ref, bias_ref, layer)
    h = h_ref[...] + v / (1.0 + jnp.exp(-v))
    nodes = h.shape[1]
    seeds = rg_ref.shape[0]
    belong = (iota((8, nodes), 0) == seg_ref[...]).astype(F32)
    readout = lax.dot_general(belong, h, NT, precision=lax.Precision.HIGHEST, preferred_element_type=F32)
    readout_ref[...] = readout[0:seeds] / SUB_MAX
    dh = jnp.zeros(h.shape, F32)
    for s in range(seeds):
        dh = dh + to_col(rg_ref[s : s + 1]) * belong[s : s + 1]
    dh = dh / SUB_MAX
    dh_ref[...] = dh
    gate_grad(dh, xh, v, dv_ref, part_ref)


def backward_layer(
    layer, recv_ref, dv_ref, dh_ref, u_ref, norm_ref, gain_ref, bias_ref, wmix_ref, wpost_ref, wpre_ref,
    b_hbm, live_ref, rows_ref, g_ref, gt_ref, m_hbm, s_hbm,
    gb_ref, du_ref, d_ref, dm_ref, dcat_ref, et_ref, ds_ref, acc_ref, bd_ref, m_ref, s_ref, b_ref, in_sems,
):
    loads = start_copies([(m_hbm, m_ref), (s_hbm, s_ref), (b_hbm, b_ref)], in_sems)
    width, nodes = dv_ref.shape
    leaf_cols = LEAF_SLOTS * nodes
    sums = jnp.sum(recv_ref[...], axis=0)
    g_bias, g_gain = sums[:, 0:width], sums[:, width:]
    gb_ref[...] = sums
    count = norm_ref[2:3, 0:1]
    xh, _ = normed(u_ref[...], norm_ref, gain_ref, bias_ref, layer)
    alive = rows_ref[3:4, 0:nodes]
    scale = to_col(norm_ref[1:2] * gain_ref[layer : layer + 1])
    du = scale * (dv_ref[...] - alive * (to_col(g_bias) + xh * to_col(g_gain)) / count)
    du = du.astype(BF16)
    du_ref[...] = du
    dy = mm(wmix_ref[layer], du)
    dy_low = dy.astype(BF16)
    dcat_ref[2 * width :] = dy_low
    dy_h = mm(dy_low, g_ref[...])
    keep = rows_ref[4:5]
    amp, att = rows_ref[0:1], rows_ref[1:2]
    dy_all = jnp.concatenate([dy_low.astype(F32), dy_h], axis=1) * keep
    bd_ref[...] = jnp.zeros_like(bd_ref)
    for t in range(4):
        part = dy_all[64 * t : 64 * t + 64]
        d_ref[192 * t : 192 * t + 64] = part.astype(BF16)
        d_ref[192 * t + 64 : 192 * t + 128] = (part * amp).astype(BF16)
        d_ref[192 * t + 128 : 192 * t + 192] = (part * att).astype(BF16)
        w = tower_weights(wpost_ref, layer, t)
        dz = mm(w, d_ref[192 * t : 192 * t + 192], TN)
        for n in range(4):
            rows = slice(64 * t, 64 * t + 64)
            block = dz[64 * (n + 1) : 64 * (n + 2)]
            ds_ref[n, rows, 0:nodes] = block[:, 0:nodes]
            ds_ref[n, rows, nodes:] = fold(block[:, nodes:], jnp.add)
        bd_ref[64 * t : 64 * t + 64, 64 * t : 64 * t + 64] = wpost_ref[layer, t][:, 0:64]

    wait_all(loads[0:2])

    def row_step(i, _):
        r = pl.multiple_of(i * 16, 16)
        for c in range(nodes // 128 + 1):
            lanes = slice(128 * c, 128 * c + 128)
            if c < nodes // 128:
                cols = [k * nodes + 128 * c for k in range(LEAF_SLOTS)]
            else:
                cols = [leaf_cols + 128 * j for j in range(8)]
            mean, smax, smin, std = (s_ref[n, pl.ds(r, 16), lanes] for n in range(4))
            dmean, dsmax, dsmin, dstd = (ds_ref[n, pl.ds(r, 16), lanes] for n in range(4))
            inv = rows_ref[2:3, lanes]
            c0 = dmean * inv
            c1 = dstd * inv / std
            acc = None
            for lo in cols:
                m = m_ref[pl.ds(r, 16), lo : lo + 128]
                d = c0 + (m - mean) * c1 + dsmax * jnp.exp(m - smax) + dsmin * jnp.exp(smin - m)
                d = jnp.where(live_ref[0:1, lo : lo + 128] > 0, d, 0.0)
                acc = d if acc is None else acc + d
                dm_ref[pl.ds(r, 16), lo : lo + 128] = d.astype(BF16)
            if c == nodes // 128:
                acc = fold(acc, jnp.add)
            acc_ref[pl.ds(r, 16), lanes] = acc
        return 0

    lax.fori_loop(0, width // 16, row_step, 0)

    down = acc_ref[:, 0:nodes] + mm(acc_ref[:, nodes:].astype(BF16), gt_ref[...])
    dcat_ref[0:width] = down.astype(BF16)
    wait_all(loads[2:])
    landed = mm(dm_ref[...], b_ref[0 : nodes + 32], NT)
    dcat_ref[width : 2 * width] = landed[:, 0:nodes].astype(BF16)
    once = jnp.where(iota((1, nodes + 128), 1) < nodes + 64, acc_ref[...], 0.0)
    bias = jnp.sum(once, axis=1, keepdims=True)
    factor = landed[:, nodes : nodes + 16] + landed[:, nodes + 16 : nodes + 32]
    et_ref[...] = jnp.concatenate([factor, jnp.broadcast_to(bias, (width, 48))], axis=1)
    weights = jnp.concatenate([wpre_ref[layer, 0:width], wpre_ref[layer, width : 2 * width]], axis=1)
    dh = mm(weights, dcat_ref[0 : 2 * width])
    dh = dh + mm(bd_ref[...], dcat_ref[2 * width :], TN)
    return dh_ref[...] + dh


def backward_first_kernel(
    layer, recv_ref, dv_ref, dh_ref, u_ref, norm_ref, gain_ref, bias_ref, wmix_ref, wpost_ref, wpre_ref,
    b_hbm, live_ref, rows_ref, g_ref, gt_ref, m_hbm, s_hbm, u_low_ref, norm_low_ref,
    gb_ref, du_out, d_out, dm_out, dcat_out, et_out, dh_out_ref, dv_out_ref, part_ref,
    du_ref, d_ref, dm_ref, dcat_ref, et_ref, ds_ref, acc_ref, bd_ref, m_ref, s_ref, b_ref, in_sems, out_sems,
):
    dh = backward_layer(
        layer, recv_ref, dv_ref, dh_ref, u_ref, norm_ref, gain_ref, bias_ref, wmix_ref, wpost_ref, wpre_ref,
        b_hbm, live_ref, rows_ref, g_ref, gt_ref, m_hbm, s_hbm,
        gb_ref, du_ref, d_ref, dm_ref, dcat_ref, et_ref, ds_ref, acc_ref, bd_ref, m_ref, s_ref, b_ref, in_sems,
    )
    stores = start_copies(
        [(dcat_ref, dcat_out), (et_ref, et_out), (du_ref, du_out), (d_ref, d_out), (dm_ref, dm_out)], out_sems
    )
    dh_out_ref[...] = dh
    xh, v = normed(u_low_ref[...], norm_low_ref, gain_ref, bias_ref, layer - 1)
    gate_grad(dh, xh, v, dv_out_ref, part_ref)
    wait_all(stores)


def piece_owner(devices, half, place):
    return half | ((place >> 2) << 1) | ((place & 3) << 3)


def put_weight_grads(y_ref, du_ref, d_ref, z_ref, x_ref, dcat_ref, et_ref, grads_ref, keep_ref, send_ref):
    width, nodes = x_ref.shape
    for t in range(4):
        r = mm(d_ref[192 * t : 192 * t + 192], z_ref[320 * t : 320 * t + 320], NT)
        rows = slice(64 * t, 64 * t + 64)
        first = iota((64, 256), 1) < 64
        grads_ref[rows, 0:256] = r[0:64, 0:256]
        grads_ref[rows, 256:512] = jnp.where(first, jnp.concatenate([r[0:64, 256:320]] * 4, axis=1), r[64:128, 0:256])
        grads_ref[rows, 512:768] = jnp.where(
            first, jnp.concatenate([r[64:128, 256:320]] * 4, axis=1), r[128:192, 0:256]
        )
        grads_ref[rows, 768:832] = r[128:192, 256:320]
    grads_ref[:, 832:896] = et_ref[...]
    grads_ref[:, 896:1152] = mm(y_ref[...], du_ref[...], NT)
    grads_ref[:, 1152:1664] = mm(x_ref[...], dcat_ref[0 : 2 * width], NT)
    me = lax.axis_index("dp") & 31
    for place in range(16):
        for half, ref in ((0, keep_ref), (1, send_ref)):
            row = pl.multiple_of((me ^ piece_owner(32, half, place)) * 8, 8)
            ref[8 * place : 8 * place + 8] = grads_ref[pl.ds(row, 8)]


def weight_kernel(
    y_hbm, du_hbm, d_hbm, z_hbm, x_hbm, dcat_hbm, et_hbm, keep_ref, send_ref,
    y_ref, du_ref, d_ref, z_ref, x_ref, dcat_ref, et_ref, grads_ref, in_sems,
):
    loads = start_copies(
        [
            (z_hbm, z_ref), (d_hbm, d_ref), (y_hbm, y_ref), (du_hbm, du_ref), (x_hbm, x_ref),
            (dcat_hbm, dcat_ref), (et_hbm, et_ref),
        ],
        in_sems,
    )
    wait_all(loads)
    put_weight_grads(y_ref, du_ref, d_ref, z_ref, x_ref, dcat_ref, et_ref, grads_ref, keep_ref, send_ref)


def backward_last_kernel(
    layer, recv_ref, dv_ref, dh_ref, u_ref, norm_ref, gain_ref, bias_ref, wmix_ref, wpost_ref, wpre_ref,
    b_hbm, live_ref, rows_ref, g_ref, gt_ref, m_hbm, s_hbm, z_hbm, y_ref, x_ref,
    gb_ref, dm_out, node_ref, keep_ref, send_ref,
    du_ref, d_ref, dm_ref, dcat_ref, et_ref, ds_ref, acc_ref, bd_ref, m_ref, s_ref, b_ref, in_sems, out_sems,
    z_ref, grads_ref, z_sem,
):
    loads = start_copies([(z_hbm, z_ref)], z_sem)
    dh = backward_layer(
        layer, recv_ref, dv_ref, dh_ref, u_ref, norm_ref, gain_ref, bias_ref, wmix_ref, wpost_ref, wpre_ref,
        b_hbm, live_ref, rows_ref, g_ref, gt_ref, m_hbm, s_hbm,
        gb_ref, du_ref, d_ref, dm_ref, dcat_ref, et_ref, ds_ref, acc_ref, bd_ref, m_ref, s_ref, b_ref, in_sems,
    )
    stores = start_copies([(dm_ref, dm_out)], out_sems)
    node_ref[...] = dh.T
    wait_all(loads)
    put_weight_grads(y_ref, du_ref, d_ref, z_ref, x_ref, dcat_ref, et_ref, grads_ref, keep_ref, send_ref)
    wait_all(stores)


def edge_kernel(dm0_ref, dm1_ref, wpre_ref, wedge_ref, gt_ref, out_ref, acc_ref):
    width = dm0_ref.shape[0]
    nodes = gt_ref.shape[1]
    leaf_cols = LEAF_SLOTS * nodes
    total = None
    for layer, dm_ref in ((0, dm0_ref), (1, dm1_ref)):
        w = mm(wedge_ref[layer], wpre_ref[layer, 2 * width :]).astype(BF16)
        part = mm(w, dm_ref[...])
        total = part if total is None else total + part
    hub = total[:, leaf_cols:]
    for j in range(8):
        acc_ref[32 * j : 32 * j + 16] = hub[:, 128 * j : 128 * j + 128]
        acc_ref[32 * j + 16 : 32 * j + 32] = pltpu.roll(hub[:, 128 * j : 128 * j + 128], 64, 1)
    high, rest = split_two(acc_ref[...])
    gt = gt_ref[...]
    spread_out = mm(high, gt) + mm(rest, gt)
    leaf = jnp.concatenate([total[:, k * nodes : (k + 1) * nodes] for k in range(LEAF_SLOTS)], axis=0)
    out = jnp.concatenate([spread_out[0:64] + leaf, spread_out[64:]], axis=0)
    out_ref[...] = out.T


def finish_kernel(
    a0_ref, b0_ref, a1_ref, b1_ref, wedge_ref, wpre_ref, gedge_ref, gpre_ref, gb_ref, gpost_ref, gmix_ref, et_ref
):
    width = wpre_ref.shape[2]
    me = lax.axis_index("dp") & 31
    for layer, halves in ((0, (a0_ref, b0_ref)), (1, (a1_ref, b1_ref))):
        for place in range(16):
            for half in range(2):
                row = pl.multiple_of((me ^ piece_owner(32, half, place)) * 8, 8)
                piece = halves[half][8 * place : 8 * place + 8]
                gpost_ref[layer, pl.ds(row, 8)] = piece[:, 0:832]
                et_ref[pl.ds(row, 8)] = piece[:, 832:896]
                gmix_ref[layer, pl.ds(row, 8)] = piece[:, 896:1152]
                gpre_ref[layer, pl.ds(row, 8)] = piece[:, 1152:1408]
                gpre_ref[layer, pl.ds(width + row, 8)] = piece[:, 1408:1664]
        gb_ref[layer : layer + 1] = to_row(et_ref[:, 16:17])
        et = et_ref[:, 0:16]
        wedge = wedge_ref[layer].astype(F32)
        hi = dict(precision=lax.Precision.HIGHEST, preferred_element_type=F32)
        gpre_ref[layer, 2 * width :] = lax.dot_general(wedge, et, TT, **hi)
        gedge_ref[layer] = lax.dot_general(et, wpre_ref[layer, 2 * width :].astype(F32), TT, **hi)


def on_device(
    devices, node_feats, edge_feats, segment_ids, neighbours, nbr_mask, degrees, w_edge, w_pre, b_pre, w_post,
    w_mix, bn_gain, bn_bias, readout_grad,
):
    nodes, width = node_feats.shape
    lanes = nodes + 128
    cols = LEAF_SLOTS * nodes + 1024
    inner = nodes + 64
    seg = segment_ids.reshape(1, nodes)
    deg = degrees.reshape(1, nodes)
    nbr_t = neighbours.T
    mask_t = nbr_mask.T
    wpost_t = jnp.swapaxes(w_post, 2, 3)

    def s(shape, dtype=F32):
        return jax.ShapeDtypeStruct(shape, dtype)

    vmem = pl.BlockSpec(memory_space=pltpu.VMEM)
    hbm = pl.BlockSpec(memory_space=pltpu.HBM)

    def call(kernel, args, outs, scratch=(), far=(), far_out=(), limit=20):
        return pl.pallas_call(
            kernel,
            in_specs=[hbm if i in far else vmem for i in range(len(args))],
            out_specs=[hbm if i in far_out else vmem for i in range(len(outs))],
            out_shape=outs,
            scratch_shapes=list(scratch),
            compiler_params=pltpu.CompilerParams(vmem_limit_bytes=limit * 1024 * 1024),
        )(*args)

    def like(shapes):
        return [pltpu.VMEM(x.shape, x.dtype) for x in shapes]

    def dma(n):
        return pltpu.SemaphoreType.DMA((n,))

    def exchange(part):
        return lax.all_to_all(part, "dp", 0, 0, tiled=True)

    m_s, s_s, z_s = s((width, cols)), s((4, width, lanes)), s((4 * 320, lanes), BF16)
    b_s = s((inner, cols), BF16)
    row_s, low_s = s((width, nodes)), s((width, nodes), BF16)
    layer_outs = [m_s, s_s, z_s, low_s, row_s, s((devices, 1, 2 * width + 128))]
    fwd_scratch = like([m_s, s_s, z_s, s((width, inner), BF16), s((width, lanes), BF16)]) + [dma(3)]
    table_outs = [b_s, s((1, cols)), s((8, lanes)), s((nodes, 128), BF16), s((128, nodes), BF16)]
    first_args = [node_feats, edge_feats, seg, nbr_t, mask_t, deg, w_edge, w_pre, b_pre, wpost_t, w_mix]
    x0, b, live, rows, g, gt, m0, s0, z0, y0, u0, part = call(
        functools.partial(forward_first_kernel, 0),
        first_args, [low_s] + table_outs + layer_outs,
        fwd_scratch + like([b_s] + [a for i, a in enumerate(first_args) if i not in (2, 5)]) + [dma(9), dma(1)],
        (0, 1, 3, 4, 6, 7, 8, 9, 10), (1, 6, 7, 8), 48,
    )
    tables = [b, live, rows, g, gt]
    recv = exchange(part)
    norm0, h1, x1, m1, s1, z1, y1, u1, part = call(
        functools.partial(forward_next_kernel, 1),
        [recv, u0, x0, bn_gain, bn_bias, w_edge, w_pre, b_pre, wpost_t, w_mix] + tables,
        [s((8, width)), row_s, low_s] + layer_outs,
        fwd_scratch + like([b_s]) + [dma(1)], (10,), (3, 4, 5), 40,
    )
    recv = exchange(part)
    sums_out = s((devices, 1, 2 * width))
    norm1, readout, dh2, dv1, part = call(
        functools.partial(readout_kernel, 1),
        [recv, u1, h1, bn_gain, bn_bias, seg, readout_grad],
        [s((8, width)), s(readout_grad.shape), row_s, row_s, sums_out],
    )
    sum_s = s((1, 2 * width))
    du_s, d_s, dm_s = low_s, s((4 * 192, lanes), BF16), s((width, cols), BF16)
    dcat_s, et_s, acc_s = s((3 * width, nodes), BF16), s((width, 64)), s((width, lanes))
    back_scratch = like([du_s, d_s, dm_s, dcat_s, et_s, s_s, acc_s, s((width, width), BF16), m_s, s_s, b_s])
    recv = exchange(part)
    sums1, du1, d1, dm1, dcat1, et1, dh1, dv0, part = call(
        functools.partial(backward_first_kernel, 1),
        [recv, dv1, dh2, u1, norm1, bn_gain, bn_bias, w_mix, wpost_t, w_pre] + tables + [m1, s1, u0, norm0],
        [sum_s, du_s, d_s, dm_s, dcat_s, et_s, row_s, row_s, sums_out],
        back_scratch + [dma(3), dma(5)], (10, 15, 16), (1, 2, 3, 4, 5), 40,
    )
    recv = exchange(part)
    grad_cols = 1664
    grad_s, half_s = s((width, grad_cols)), s((width // 2, grad_cols))
    halves1 = call(
        weight_kernel, [y1, du1, d1, z1, x1, dcat1, et1], [half_s, half_s],
        like([low_s, du_s, d_s, z_s, low_s, dcat_s, et_s, grad_s]) + [dma(7)], range(7), (), 20,
    )
    sums0, dm0, node_grad, *halves0 = call(
        functools.partial(backward_last_kernel, 0),
        [recv, dv0, dh1, u0, norm0, bn_gain, bn_bias, w_mix, wpost_t, w_pre] + tables + [m0, s0, z0, y0, x0],
        [sum_s, dm_s, s((nodes, width)), half_s, half_s],
        back_scratch + [dma(3), dma(1)] + like([z_s, grad_s]) + [dma(1)], (10, 15, 16, 17), (1,), 44,
    )
    edge_grad = call(
        edge_kernel, [dm0, dm1, w_pre, w_edge, gt], [s((nodes, width))], [pltpu.VMEM((width, 128), F32)]
    )[0]

    def swap(value, mask):
        return lax.ppermute(value, "dp", [(i, i ^ mask) for i in range(devices)])

    def reduce_all(keep, send):
        part = keep + swap(send, 1)
        for step, size in ((1, 32), (3, 8)):
            got = [swap(part[size * i : size * (i + 1)], i << step) for i in range(1, 4)]
            part = part[0:size] + got[0] + got[1] + got[2]
        mask = 32
        while mask < devices:
            part = part + swap(part, mask)
            mask *= 2
        for step in (3, 1):
            part = jnp.concatenate([part] + [swap(part, i << step) for i in range(1, 4)], axis=0)
        return part, swap(part, 1)

    total1 = reduce_all(*halves1)
    total0 = reduce_all(*halves0)
    layers = w_pre.shape[0]
    g_edge, g_pre, g_b, g_post_t, g_mix = call(
        finish_kernel, [*total0, *total1, w_edge, w_pre],
        [s(w_edge.shape), s(w_pre.shape), s(b_pre.shape), s((layers, width, 832)), s(w_mix.shape)],
        [pltpu.VMEM((width, 64), F32)],
    )
    g_post = jnp.swapaxes(g_post_t.reshape(wpost_t.shape), 2, 3)
    sums = jnp.concatenate([sums0, sums1], axis=0)
    return (
        readout, node_grad, edge_grad, g_edge, g_pre, g_b, g_post, g_mix, sums[:, width:], sums[:, :width],
    )


def solution(mesh):
    split, split2, full = P("dp"), P("dp", None), P()
    in_specs = (split2, split2, split, split2, split2, split) + (full,) * 7 + (split2,)
    out_specs = (split2, split2, split2) + (full,) * 7
    return jax.shard_map(
        functools.partial(on_device, mesh.shape["dp"]),
        mesh=mesh, in_specs=in_specs, out_specs=out_specs, check_vma=False,
    )
```

```python
import functools

import jax
import jax.numpy as jnp
from jax import lax
from jax.experimental import pallas as pl
from jax.experimental.pallas import tpu as pltpu
from jax.sharding import PartitionSpec as P

SUB_MAX = 160
DEGREE_CENTER = 2.0
SPREAD_OFFSET = 0.25
STABILITY_FLOOR = 1e-05

LEAF_SLOTS = 4
HUB_RANK = 16
LOG2E = 1.4426950408889634
LN2 = 0.6931471805599453
ROW_CHUNK = 64
F32 = jnp.float32
BF16 = jnp.bfloat16
NN = (((1,), (0,)), ((), ()))
NT = (((1,), (1,)), ((), ()))
TN = (((0,), (0,)), ((), ()))
TT = (((0,), (1,)), ((), ()))


def mm(a, b, dims=NN):
    return lax.dot_general(a, b, dims, preferred_element_type=F32)


def iota(shape, dim):
    return lax.broadcasted_iota(jnp.int32, shape, dim)


def to_cols(*rows):
    pad = [jnp.zeros((8 - len(rows), rows[0].shape[1]), F32)] if len(rows) < 8 else []
    turned = jnp.concatenate(list(rows) + pad, axis=0).T
    return [turned[:, i : i + 1] for i in range(len(rows))]


def to_rows(*cols):
    wide = jnp.concatenate([jnp.broadcast_to(c, (c.shape[0], 128 // len(cols))) for c in cols], axis=1).T
    step = 128 // len(cols)
    return [wide[i * step : i * step + 1] for i in range(len(cols))]


def fold(value, op):
    return op(value, pltpu.roll(value, 64, 1))


def split_two(value):
    high = value.astype(BF16)
    return high, (value - high.astype(F32)).astype(BF16)


def start_copies(pairs, sems):
    copies = [pltpu.make_async_copy(src, dst, sems.at[i]) for i, (src, dst) in enumerate(pairs)]
    for copy in copies:
        copy.start()
    return copies


def wait_all(copies):
    for copy in copies:
        copy.wait()


def build_tables(ef_ref, seg_ref, nbr_ref, mask_ref, deg_ref, b_ref, live_ref, rows_ref, g_ref, gt_ref):
    nodes = seg_ref.shape[0]
    seg = seg_ref[...].reshape(1, nodes)
    lane_h = iota((1, 128), 1)
    sub_h = iota((128, 1), 0)
    node_row = jnp.zeros((1, 128), jnp.int32)
    node_col = jnp.zeros((128, 1), jnp.int32)
    lane_r, sub_r = lane_h & 15, sub_h & 15
    lane_s, sub_s = (lane_h >> 4) & 3, (sub_h >> 4) & 3
    below = [jnp.sum((seg < s).astype(jnp.int32), axis=1, keepdims=True) for s in range(5)]
    for s in range(4):
        start, size = below[s], below[s + 1] - below[s]
        node_row = jnp.where(lane_s == s, jnp.where(lane_r < size, start + lane_r, -1), node_row)
        node_col = jnp.where(sub_s == s, jnp.where(sub_r < size, start + sub_r, -1), node_col)
    node_col = jnp.where(sub_h < 64, node_col, -1)
    g = (iota((nodes, 128), 0) == node_row).astype(F32).astype(BF16)
    gt = (iota((128, nodes), 1) == node_col).astype(F32).astype(BF16)
    g_ref[...] = g
    gt_ref[...] = gt
    is_hub = jnp.sum(gt.astype(F32), axis=0, keepdims=True)

    nbr = nbr_ref[...]
    mask = (mask_ref[...] > 0).astype(F32)
    nbr_h = (
        mm((nbr >> 3).astype(F32).astype(BF16), g) * 8.0 + mm((nbr & 7).astype(F32).astype(BF16), g)
    ).astype(jnp.int32)
    mask_h = mm(mask.astype(BF16), g)
    valid = (node_row >= 0).astype(F32)
    first = (lane_h < 64).astype(F32)

    def degree_rows(deg):
        log_degree = jnp.log(deg + 1.0)
        return log_degree / DEGREE_CENTER, DEGREE_CENTER / log_degree

    deg = deg_ref[...].reshape(1, nodes).astype(F32)
    deg_h = mm(jnp.broadcast_to(deg, (8, nodes)).astype(BF16), g)[0:1]
    deg_h = jnp.where(valid > 0, deg_h, 1.0)
    amp, att = degree_rows(deg)
    amp_h, att_h = degree_rows(deg_h)
    filled = jnp.sum(mask, axis=0, keepdims=True)
    filled_h = jnp.maximum(jnp.sum(mask_h, axis=0, keepdims=True), 1.0)
    rows_ref[...] = jnp.zeros_like(rows_ref)
    for i, (leaf, hub) in enumerate(
        (
            (amp, amp_h),
            (att, att_h),
            (1.0 / filled, 1.0 / filled_h),
            ((seg < 4).astype(F32), None),
            (1.0 - is_hub, valid * first),
            (is_hub, valid),
            (jnp.sum(mask[1:LEAF_SLOTS], axis=0, keepdims=True) - (LEAF_SLOTS - 2.0), filled_h - 16.0),
            (seg.astype(F32), None),
        )
    ):
        rows_ref[i : i + 1, 0:nodes] = leaf
        if hub is not None:
            rows_ref[i : i + 1, nodes : nodes + 128] = hub

    ef_t = ef_ref[...].T
    ef_h = mm(ef_t, g).astype(BF16)
    node_iota = iota((nodes, nodes), 0)
    hub_iota = iota((nodes, 128), 0)
    zero16 = jnp.zeros((16, nodes), BF16)
    for k in range(LEAF_SLOTS):
        lo = k * nodes
        b_ref[0:nodes, lo : lo + nodes] = (node_iota == nbr[k : k + 1]).astype(F32).astype(BF16)
        piece = ef_t[16 * k : 16 * k + 16]
        for r, part in enumerate((piece, zero16, piece, zero16)):
            b_ref[nodes + 16 * r : nodes + 16 * r + 16, lo : lo + nodes] = part
        live_ref[0:1, lo : lo + nodes] = mask[k : k + 1] * LOG2E
        live_ref[1:2, lo : lo + nodes] = mask[k : k + 1]
    own_half = (iota((32, 128), 0) < 16) == (iota((32, 128), 1) < 64)
    for j in range(8):
        lo = LEAF_SLOTS * nodes + 128 * j
        index = jnp.where(lane_h < 64, nbr_h[2 * j : 2 * j + 1], nbr_h[2 * j + 1 : 2 * j + 2])
        b_ref[0:nodes, lo : lo + 128] = (hub_iota == index).astype(F32).astype(BF16)
        piece = jnp.where(own_half, ef_h[32 * j : 32 * j + 32].astype(F32), 0.0).astype(BF16)
        b_ref[nodes : nodes + 32, lo : lo + 128] = piece
        b_ref[nodes + 32 : nodes + 64, lo : lo + 128] = piece
        live = jnp.where(lane_h < 64, mask_h[2 * j : 2 * j + 1], mask_h[2 * j + 1 : 2 * j + 2])
        live_ref[0:1, lo : lo + 128] = live * LOG2E
        live_ref[1:2, lo : lo + 128] = live


def tower_weights(wpost_ref, layer, t):
    w = wpost_ref[layer, t]
    inner = iota((64, 320), 1) >= 64
    zero = jnp.zeros((64, 320), BF16)
    return jnp.concatenate(
        [w[:, 0:320], jnp.where(inner, w[:, 256:576], zero), jnp.where(inner, w[:, 512:832], zero)], axis=0
    )


def forward_layer(
    layer, x_ref, wedge_ref, wpre_ref, bias, wpost_ref, wmix_ref, b_ref, live_ref, rows_ref, g_ref, gt_ref,
    m_ref, s_ref, z_ref, y_ref, u_ref, part_ref, a_ref, ya_ref, own_ref,
):
    width, nodes = x_ref.shape
    leaf_cols = LEAF_SLOTS * nodes
    x = x_ref[...]
    g = g_ref[...]
    own = mm(wpre_ref[layer, 0:width], x, TN) + bias
    own_ref[:, 0:nodes] = own
    a_ref[:, 0:nodes] = mm(wpre_ref[layer, width : 2 * width], x, TN).astype(BF16)
    wedge = wedge_ref[layer]
    both = mm(wpre_ref[layer, 2 * width :], jnp.concatenate([wedge] * 4, axis=0), TT)
    high, rest = split_two(both)
    a_ref[:, nodes : nodes + 64] = jnp.where(iota((width, 64), 1) < 32, high, rest)
    own_high, own_rest = split_two(own)
    own_ref[:, nodes:] = mm(own_high, g) + mm(own_rest, g)
    a = a_ref[...]

    def messages(lo, hi):
        m_ref[:, lo:hi] = mm(a, b_ref[:, lo:hi])

    x_h = mm(x, g).astype(BF16)
    for t in range(4):
        z_ref[320 * t : 320 * t + 64, 0:nodes] = x[64 * t : 64 * t + 64]
        z_ref[320 * t : 320 * t + 64, nodes:] = x_h[64 * t : 64 * t + 64]

    def summarize(i, tiles):
        per = 64 // ROW_CHUNK
        zr = (i // per) * 320 + 64 + (i % per) * ROW_CHUNK
        rows = pl.ds(i * ROW_CHUNK, ROW_CHUNK)
        for c in tiles:
            hub = c == nodes // 128
            lanes = slice(128 * c, 128 * c + 128)
            if hub:
                cols = [leaf_cols + 128 * j for j in range(8)]
                first = m_ref[rows, leaf_cols : leaf_cols + 128]
                first = jnp.where(iota((1, 128), 1) < 64, first, pltpu.roll(first, 64, 1))
            else:
                cols = [k * nodes + 128 * c for k in range(1, LEAF_SLOTS)]
                first = m_ref[rows, lanes]
            offs = []
            for lo in cols:
                d = (m_ref[rows, lo : lo + 128] - first) * live_ref[0:1, lo : lo + 128]
                m_ref[rows, lo : lo + 128] = d
                offs.append(d)

            def total(parts, op):
                while len(parts) > 1:
                    parts = [op(*parts[i : i + 2]) if i + 1 < len(parts) else parts[i] for i in range(0, len(parts), 2)]
                return fold(parts[0], op) if hub else parts[0]

            inv, missing = rows_ref[2:3, lanes], rows_ref[6:7, lanes]
            mean = total(offs, jnp.add) * inv
            var = total([d * d for d in offs], jnp.add) * inv - mean * mean
            spread = jnp.maximum(var * (LN2 * LN2), 0.0) + SPREAD_OFFSET
            rstd = lax.rsqrt(spread)
            top = jnp.maximum(total(offs, jnp.maximum), 0.0)
            low = jnp.minimum(total(offs, jnp.minimum), 0.0)
            ups = total([jnp.exp2(d - top) for d in offs], jnp.add) + missing * jnp.exp2(-top)
            downs = total([jnp.exp2(low - d) for d in offs], jnp.add) + missing * jnp.exp2(low)
            smax = top + jnp.log2(ups)
            smin = low - jnp.log2(downs)
            base = own_ref[rows, lanes] + first
            for n, stat in enumerate((mean, smax, smin, rstd)):
                s_ref[n, rows, lanes] = stat
                value = base + LN2 * stat if n < 3 else spread * rstd
                z_ref[pl.ds(zr + 64 * n, ROW_CHUNK), lanes] = value.astype(BF16)

    last = nodes // 128
    groups = [range(last, last + 1)] + [range(c, min(c + 2, last)) for c in range(0, last, 2)]
    waiting = None
    for tiles in groups + [None]:
        if tiles is not None:
            if tiles[0] == last:
                messages(leaf_cols, leaf_cols + 1024)
            else:
                for k in range(LEAF_SLOTS):
                    messages(k * nodes + 128 * tiles[0], k * nodes + 128 * (tiles[-1] + 1))
        if waiting is not None:
            for i in range(width // ROW_CHUNK):
                summarize(i, waiting)
        waiting = tiles

    amp, att = rows_ref[0:1], rows_ref[1:2]
    for t in range(4):
        r = mm(tower_weights(wpost_ref, layer, t), z_ref[320 * t : 320 * t + 320])
        ya_ref[64 * t : 64 * t + 64] = (r[0:64] + amp * r[64:128] + att * r[128:192]).astype(BF16)
    spread_out = mm(ya_ref[:, nodes:], gt_ref[...])
    y = jnp.where(rows_ref[5:6, 0:nodes] > 0, spread_out, ya_ref[:, 0:nodes].astype(F32)).astype(BF16)
    y_ref[...] = y
    u = mm(wmix_ref[layer], y, TN)
    u_ref[...] = u
    alive = rows_ref[3:4, 0:nodes]
    count = jnp.sum(alive, axis=1, keepdims=True)
    mean = jnp.sum(alive * u, axis=1, keepdims=True) / count
    off = u - mean
    square = jnp.sum(alive * off * off, axis=1, keepdims=True)
    row = jnp.concatenate(to_rows(mean, square) + [jnp.broadcast_to(count, (1, 128))], axis=1)
    part_ref[...] = jnp.broadcast_to(row[None], part_ref.shape)


def forward_first_kernel(
    layer, nf_hbm, ef_hbm, seg_hbm, nbr_hbm, mask_hbm, deg_hbm, wedge_hbm, wpre_hbm, bpre_hbm, wpost_hbm, wmix_hbm,
    x_ref, b_ref, live_ref, rows_ref, g_ref, gt_ref, m_ref, s_ref, z_ref, y_ref, u_ref, part_ref,
    a_ref, ya_ref, own_ref, nf_ref, ef_ref, seg_ref, nbr_ref, mask_ref, deg_ref, wedge_ref, wpre_ref, bpre_ref, wpost_ref, wmix_ref, in_sems,
):
    loads = start_copies(
        [
            (seg_hbm, seg_ref), (nbr_hbm, nbr_ref), (mask_hbm, mask_ref), (deg_hbm, deg_ref), (ef_hbm, ef_ref), (nf_hbm, nf_ref), (wpre_hbm, wpre_ref),
            (wedge_hbm, wedge_ref), (bpre_hbm, bpre_ref), (wpost_hbm, wpost_ref), (wmix_hbm, wmix_ref),
        ],
        in_sems,
    )
    wait_all(loads[0:5])
    build_tables(ef_ref, seg_ref, nbr_ref, mask_ref, deg_ref, b_ref, live_ref, rows_ref, g_ref, gt_ref)
    wait_all(loads[5:])
    x_ref[...] = nf_ref[...].T
    forward_layer(
        layer, x_ref, wedge_ref, wpre_ref, *to_cols(bpre_ref[layer : layer + 1]), wpost_ref, wmix_ref, b_ref,
        live_ref, rows_ref, g_ref, gt_ref, m_ref, s_ref, z_ref, y_ref, u_ref, part_ref, a_ref, ya_ref, own_ref,
    )


def norm_rows(recv_ref):
    w = (recv_ref.shape[2] - 128) // 2
    recv = recv_ref[...]
    means, squares = recv[:, :, 0:w], recv[:, :, w : 2 * w]
    counts = jnp.concatenate([recv[:, :, 2 * w :]] * (w // 128), axis=2)
    total = jnp.sum(counts, axis=0)
    mean = jnp.sum(counts * means, axis=0) / total
    off = means - mean[None]
    var = jnp.sum(squares + counts * off * off, axis=0) / total
    return mean, lax.rsqrt(var + STABILITY_FLOOR), total


def normed(u, norm_ref, gain_ref, bias_ref, layer):
    mean, scale, gain, bias = to_cols(
        norm_ref[0:1], norm_ref[1:2], gain_ref[layer : layer + 1], bias_ref[layer : layer + 1]
    )
    xh = (u - mean) * scale
    return xh, xh * gain + bias


def store_norm(norm_ref, recv_ref):
    mean, scale, total = norm_rows(recv_ref)
    norm_ref[...] = jnp.zeros_like(norm_ref)
    norm_ref[0:1] = mean
    norm_ref[1:2] = scale
    norm_ref[2:3] = total


def forward_next_kernel(
    layer, recv_ref, u0_ref, x0_ref, gain_ref, bias_ref, wedge_ref, wpre_ref, bpre_ref, wpost_ref, wmix_ref,
    b_ref, live_ref, rows_ref, g_ref, gt_ref,
    norm_ref, h_ref, x_ref, m_ref, s_ref, z_ref, y_ref, u_ref, part_ref, a_ref, ya_ref, own_ref,
):
    store_norm(norm_ref, recv_ref)
    _, v = normed(u0_ref[...], norm_ref, gain_ref, bias_ref, layer - 1)
    h = x0_ref[...].astype(F32) + v / (1.0 + jnp.exp(-v))
    h_ref[...] = h
    x_ref[...] = h.astype(BF16)
    forward_layer(
        layer, x_ref, wedge_ref, wpre_ref, *to_cols(bpre_ref[layer : layer + 1]), wpost_ref, wmix_ref, b_ref,
        live_ref, rows_ref, g_ref, gt_ref, m_ref, s_ref, z_ref, y_ref, u_ref, part_ref, a_ref, ya_ref, own_ref,
    )


def gate_grad(dh, xh, v, dv_ref, part_ref):
    sig = 1.0 / (1.0 + jnp.exp(-v))
    dv = dh * sig * (1.0 + v * (1.0 - sig))
    dv_ref[...] = dv
    sums = [jnp.sum(p, axis=1, keepdims=True) for p in (dv, dv * xh)]
    row = jnp.concatenate(to_rows(*sums), axis=1)
    part_ref[...] = jnp.broadcast_to(row[None], part_ref.shape)


def last_gate_kernel(
    layer, recv_ref, u_ref, h_ref, gain_ref, bias_ref, rows_ref, rg_ref, norm_ref, h_out_ref, dh_ref, dv_ref, part_ref
):
    store_norm(norm_ref, recv_ref)
    xh, v = normed(u_ref[...], norm_ref, gain_ref, bias_ref, layer)
    nodes = v.shape[1]
    seeds = rg_ref.shape[0]
    sig = 1.0 / (1.0 + jnp.exp(-v))
    h_out_ref[...] = h_ref[...] + v * sig
    dh = jnp.zeros(v.shape, F32)
    cols = to_cols(*[rg_ref[s : s + 1] / SUB_MAX for s in range(seeds)])
    for s, col in enumerate(cols):
        dh = jnp.where(rows_ref[7:8, 0:nodes] == s, col, dh)
    dh_ref[...] = dh
    gate_grad(dh, xh, v, dv_ref, part_ref)


def backward_layer(
    layer, recv_ref, dv_ref, dh_ref, u_ref, norm_ref, gain_ref, bias_ref, wmix_ref, wpost_ref, wpre_ref,
    b_ref, live_ref, rows_ref, g_ref, gt_ref, m_ref, s_ref,
    gb_ref, du_ref, d_ref, dm_ref, dcat_ref, et_ref, ds_ref, acc_ref, bd_ref, beside=(),
):
    width, nodes = dv_ref.shape
    leaf_cols = LEAF_SLOTS * nodes
    sums = jnp.sum(recv_ref[...], axis=0)
    g_bias, g_gain = sums[:, 0:width], sums[:, width:]
    gb_ref[...] = sums
    xh, _ = normed(u_ref[...], norm_ref, gain_ref, bias_ref, layer)
    alive = rows_ref[3:4, 0:nodes]
    scale, part_bias, part_gain = to_cols(
        norm_ref[1:2] * gain_ref[layer : layer + 1], g_bias / norm_ref[2:3], g_gain / norm_ref[2:3]
    )
    du = scale * (dv_ref[...] - alive * (part_bias + xh * part_gain))
    du = du.astype(BF16)
    du_ref[...] = du
    dy = mm(wmix_ref[layer], du)
    dy_low = dy.astype(BF16)
    dcat_ref[2 * width :] = dy_low
    dy_h = mm(dy_low, g_ref[...])
    keep = rows_ref[4:5]
    amp, att = rows_ref[0:1], rows_ref[1:2]
    dy_all = jnp.concatenate([dy_low.astype(F32), dy_h], axis=1) * keep
    bd_ref[...] = jnp.zeros_like(bd_ref)
    for t in range(4):
        part = dy_all[64 * t : 64 * t + 64]
        d_ref[192 * t : 192 * t + 64] = part.astype(BF16)
        d_ref[192 * t + 64 : 192 * t + 128] = (part * amp).astype(BF16)
        d_ref[192 * t + 128 : 192 * t + 192] = (part * att).astype(BF16)
        w = tower_weights(wpost_ref, layer, t)
        dz = mm(w, d_ref[192 * t : 192 * t + 192], TN)
        for n in range(4):
            rows = slice(64 * t, 64 * t + 64)
            block = dz[64 * (n + 1) : 64 * (n + 2)]
            ds_ref[n, rows, 0:nodes] = block[:, 0:nodes]
            ds_ref[n, rows, nodes:] = fold(block[:, nodes:], jnp.add)
        bd_ref[64 * t : 64 * t + 64, 64 * t : 64 * t + 64] = wpost_ref[layer, t][:, 0:64]

    def spread_back(i, tiles):
        rows = pl.ds(i * ROW_CHUNK, ROW_CHUNK)
        for c in tiles:
            hub = c == nodes // 128
            lanes = slice(128 * c, 128 * c + 128)
            mean, smax, smin, rstd = (s_ref[n, rows, lanes] for n in range(4))
            dmean, dsmax, dsmin, dstd = (ds_ref[n, rows, lanes] for n in range(4))
            inv = rows_ref[2:3, lanes]
            c1 = dstd * inv * rstd * LN2
            c0 = dmean * inv - mean * c1
            if hub:
                cols = [leaf_cols + 128 * j for j in range(8)]
                acc = None
            else:
                cols = [k * nodes + 128 * c for k in range(1, LEAF_SLOTS)]
                acc = c0 + dsmax * jnp.exp2(-smax) + dsmin * jnp.exp2(smin)
                dm_ref[rows, lanes] = acc.astype(BF16)
            for lo in cols:
                m = m_ref[rows, lo : lo + 128]
                d = c0 + m * c1 + dsmax * jnp.exp2(m - smax) + dsmin * jnp.exp2(smin - m)
                d = d * live_ref[1:2, lo : lo + 128]
                acc = d if acc is None else acc + d
                dm_ref[rows, lo : lo + 128] = d.astype(BF16)
            acc_ref[rows, lanes] = fold(acc, jnp.add) if hub else acc

    def land(lo, hi):
        return mm(dm_ref[:, lo:hi], b_ref[0 : nodes + 32, lo:hi], NT)

    last = nodes // 128
    groups = [range(last, last + 1)] + [range(c, min(c + 2, last)) for c in range(0, last, 2)]
    waiting, landed = None, None
    for step, tiles in enumerate(groups + [None]):
        if tiles is not None:
            for i in range(width // ROW_CHUNK):
                spread_back(i, tiles)
        if step < len(beside):
            beside[step]()
        if waiting is not None:
            if waiting[0] == last:
                landed = land(leaf_cols, leaf_cols + 1024)
            else:
                for k in range(LEAF_SLOTS):
                    landed = landed + land(k * nodes + 128 * waiting[0], k * nodes + 128 * (waiting[-1] + 1))
        waiting = tiles

    down = acc_ref[:, 0:nodes] + mm(acc_ref[:, nodes:].astype(BF16), gt_ref[...])
    dcat_ref[0:width] = down.astype(BF16)
    dcat_ref[width : 2 * width] = landed[:, 0:nodes].astype(BF16)
    once = jnp.where(iota((1, nodes + 128), 1) < nodes + 64, acc_ref[...], 0.0)
    bias = jnp.sum(once, axis=1, keepdims=True)
    factor = landed[:, nodes : nodes + 16] + landed[:, nodes + 16 : nodes + 32]
    et_ref[...] = jnp.concatenate([factor, jnp.broadcast_to(bias, (width, 48))], axis=1)
    weights = jnp.concatenate([wpre_ref[layer, 0:width], wpre_ref[layer, width : 2 * width]], axis=1)
    dh = mm(weights, dcat_ref[0 : 2 * width])
    dh = dh + mm(bd_ref[...], dcat_ref[2 * width :], TN)
    return dh_ref[...] + dh


def backward_first_kernel(
    layer, recv_ref, dv_ref, dh_ref, u_ref, norm_ref, gain_ref, bias_ref, wmix_ref, wpost_ref, wpre_ref,
    b_ref, live_ref, rows_ref, g_ref, gt_ref, m_ref, s_ref, u_low_ref, norm_low_ref,
    gb_ref, du_ref, d_ref, dm_ref, dcat_ref, et_ref, dh_out_ref, dv_out_ref, part_ref,
    ds_ref, acc_ref, bd_ref,
):
    dh = backward_layer(
        layer, recv_ref, dv_ref, dh_ref, u_ref, norm_ref, gain_ref, bias_ref, wmix_ref, wpost_ref, wpre_ref,
        b_ref, live_ref, rows_ref, g_ref, gt_ref, m_ref, s_ref,
        gb_ref, du_ref, d_ref, dm_ref, dcat_ref, et_ref, ds_ref, acc_ref, bd_ref,
    )
    dh_out_ref[...] = dh
    xh, v = normed(u_low_ref[...], norm_low_ref, gain_ref, bias_ref, layer - 1)
    gate_grad(dh, xh, v, dv_out_ref, part_ref)


def piece_owner(core, half, place):
    plane_first = ((place >> 2) << 1) | ((place & 3) << 3)
    line_first = ((place >> 2) << 3) | ((place & 3) << 1)
    return half + jnp.where(core == half, plane_first, line_first)


def put_tower_grad(t, d_ref, z_ref, grads_ref):
    r = mm(d_ref[192 * t : 192 * t + 192], z_ref[320 * t : 320 * t + 320], NT)
    rows = slice(64 * t, 64 * t + 64)
    first = iota((64, 256), 1) < 64
    grads_ref[rows, 0:256] = r[0:64, 0:256]
    grads_ref[rows, 256:512] = jnp.where(first, jnp.concatenate([r[0:64, 256:320]] * 4, axis=1), r[64:128, 0:256])
    grads_ref[rows, 512:768] = jnp.where(first, jnp.concatenate([r[64:128, 256:320]] * 4, axis=1), r[128:192, 0:256])
    grads_ref[rows, 768:832] = r[128:192, 256:320]


def put_mix_grad(y_ref, du_ref, grads_ref):
    grads_ref[:, 896:1152] = mm(y_ref[...], du_ref[...], NT)


def put_message_grads(x_ref, dcat_ref, et_ref, grads_ref, keep_ref, send_ref):
    width = x_ref.shape[0]
    grads_ref[:, 832:896] = et_ref[...]
    grads_ref[:, 1152:1664] = mm(x_ref[...], dcat_ref[0 : 2 * width], NT)
    me = lax.axis_index("dp") & 31
    for place in range(16):
        for half, ref in ((0, keep_ref), (1, send_ref)):
            row = pl.multiple_of((me ^ piece_owner(me & 1, half, place)) * 8, 8)
            ref[8 * place : 8 * place + 8] = grads_ref[pl.ds(row, 8)]


def weight_kernel(
    y_ref, du_ref, d_ref, z_ref, x_ref, dcat_ref, et_ref, keep_ref, send_ref, grads_ref
):
    for t in range(4):
        put_tower_grad(t, d_ref, z_ref, grads_ref)
    put_mix_grad(y_ref, du_ref, grads_ref)
    put_message_grads(x_ref, dcat_ref, et_ref, grads_ref, keep_ref, send_ref)


def backward_last_kernel(
    layer, recv_ref, dv_ref, dh_ref, u_ref, norm_ref, gain_ref, bias_ref, wmix_ref, wpost_ref, wpre_ref,
    b_ref, live_ref, rows_ref, g_ref, gt_ref, m_ref, s_ref, z_ref, y_ref, x_ref,
    gb_ref, dm_ref, node_ref, keep_ref, send_ref,
    du_ref, d_ref, dcat_ref, et_ref, ds_ref, acc_ref, bd_ref, grads_ref,
):
    beside = [functools.partial(put_tower_grad, t, d_ref, z_ref, grads_ref) for t in range(4)]
    beside[3:] = [lambda: put_tower_grad(3, d_ref, z_ref, grads_ref) or put_mix_grad(y_ref, du_ref, grads_ref)]
    dh = backward_layer(
        layer, recv_ref, dv_ref, dh_ref, u_ref, norm_ref, gain_ref, bias_ref, wmix_ref, wpost_ref, wpre_ref,
        b_ref, live_ref, rows_ref, g_ref, gt_ref, m_ref, s_ref,
        gb_ref, du_ref, d_ref, dm_ref, dcat_ref, et_ref, ds_ref, acc_ref, bd_ref, beside,
    )
    put_message_grads(x_ref, dcat_ref, et_ref, grads_ref, keep_ref, send_ref)
    node_ref[...] = dh.T


def edge_kernel(dm0_ref, dm1_ref, wpre_ref, wedge_ref, gt_ref, h_ref, rows_ref, out_ref, readout_ref, acc_ref):
    width = dm0_ref.shape[0]
    nodes = gt_ref.shape[1]
    leaf_cols = LEAF_SLOTS * nodes
    total = None
    for layer, dm_ref in ((0, dm0_ref), (1, dm1_ref)):
        w = mm(wedge_ref[layer], wpre_ref[layer, 2 * width :]).astype(BF16)
        part = mm(w, dm_ref[...])
        total = part if total is None else total + part
    hub = total[:, leaf_cols:]
    for j in range(8):
        acc_ref[32 * j : 32 * j + 16] = hub[:, 128 * j : 128 * j + 128]
        acc_ref[32 * j + 16 : 32 * j + 32] = pltpu.roll(hub[:, 128 * j : 128 * j + 128], 64, 1)
    high, rest = split_two(acc_ref[...])
    gt = gt_ref[...]
    spread_out = mm(high, gt) + mm(rest, gt)
    leaf = jnp.concatenate([total[:, k * nodes : (k + 1) * nodes] for k in range(LEAF_SLOTS)], axis=0)
    out = jnp.concatenate([spread_out[0:64] + leaf, spread_out[64:]], axis=0)
    out_ref[...] = out.T
    belong = (iota((8, nodes), 0).astype(F32) == rows_ref[7:8, 0:nodes]).astype(F32)
    total = lax.dot_general(belong, h_ref[...], NT, precision=lax.Precision.HIGHEST, preferred_element_type=F32)
    readout_ref[...] = total[0 : readout_ref.shape[0]] / SUB_MAX


def finish_half(half, half_ref, outs, bufs, sems):
    me = lax.axis_index("dp") & 31
    core = me & 1
    post, mix, pre, et = bufs
    for layer in range(post.shape[0]):
        cols = 1664 * layer
        for place in range(16):
            block = (me ^ piece_owner(core, half, place)) >> 1
            piece = half_ref[8 * place : 8 * place + 8, cols : cols + 1664]
            post[layer, block] = piece[:, 0:832]
            et[layer, block] = piece[:, 832:896]
            mix[layer, block] = piece[:, 896:1152]
            pre[layer, 0, block] = piece[:, 1152:1408]
            pre[layer, 1, block] = piece[:, 1408:1664]
    side = core ^ half
    post_out, mix_out, pre_out = outs
    pairs = [(post, post_out.at[:, :, side]), (mix, mix_out.at[:, :, side]), (pre, pre_out.at[:, 0:2, :, side])]
    return start_copies(pairs, sems)


def finish_first_kernel(half_ref, post_out, mix_out, pre_out, et, post, mix, pre, sems):
    wait_all(finish_half(0, half_ref, (post_out, mix_out, pre_out), (post, mix, pre, et), sems))


def finish_last_kernel(
    post_in, mix_in, pre_in, other_et, half_ref, wedge_ref, wpre_ref, post_out, mix_out, pre_out, gb_ref, gedge_ref,
    post, mix, pre, et, term, sems,
):
    del post_in, mix_in, pre_in
    copies = finish_half(1, half_ref, (post_out, mix_out, pre_out), (post, mix, pre, et), sems)
    width = wpre_ref.shape[2]
    core = lax.axis_index("dp") & 1
    for layer in range(2):
        mine, other = et[layer], other_et[layer]
        first, second = jnp.where(core == 0, other, mine), jnp.where(core == 0, mine, other)
        both = jnp.concatenate([first[:, None], second[:, None]], axis=1).reshape(width, 64)
        gb_ref[layer : layer + 1] = to_rows(both[:, 16:17])[0]
        factor = both[:, 0:16]
        high, rest = split_two(factor)
        last = (factor - high.astype(F32) - rest.astype(F32)).astype(BF16)
        three = jnp.concatenate([high, rest, last], axis=1)
        grad = mm(jnp.concatenate([wedge_ref[layer]] * 3, axis=0), three, TT)
        term[layer] = grad.reshape(term.shape[1:])
        parts = mm(three, wpre_ref[layer, 2 * width :], TT)
        gedge_ref[layer] = parts[0:16] + parts[16:32] + parts[32:48]
    copies += start_copies([(term, pre_out.at[:, 2])], sems.at[3:4])
    wait_all(copies)


def on_device(
    devices, node_feats, edge_feats, segment_ids, neighbours, nbr_mask, degrees, w_edge, w_pre, b_pre, w_post,
    w_mix, bn_gain, bn_bias, readout_grad,
):
    nodes, width = node_feats.shape
    lanes = nodes + 128
    cols = LEAF_SLOTS * nodes + 1024
    inner = nodes + 64
    nbr_t = neighbours.T
    mask_t = nbr_mask.T
    wpost_t = jnp.swapaxes(w_post, 2, 3)

    def s(shape, dtype=F32):
        return jax.ShapeDtypeStruct(shape, dtype)

    vmem = pl.BlockSpec(memory_space=pltpu.VMEM)
    hbm = pl.BlockSpec(memory_space=pltpu.HBM)

    def call(kernel, args, outs, scratch=(), far=(), free=(), far_out=(), alias={}, cost=0, limit=20):
        args = [pltpu.with_memory_space_constraint(a, pltpu.HBM) if i in far else a for i, a in enumerate(args)]
        return pl.pallas_call(
            kernel,
            in_specs=[hbm if i in far else vmem for i in range(len(args))],
            out_specs=[hbm if i in far_out else vmem for i in range(len(outs))],
            out_shape=[
                o if i in free else (pltpu.HBM if i in far_out else pltpu.VMEM)(o.shape, o.dtype)
                for i, o in enumerate(outs)
            ],
            scratch_shapes=list(scratch),
            input_output_aliases=alias,
            cost_estimate=pl.CostEstimate(flops=int(cost * 1e9), bytes_accessed=0, transcendentals=0) if cost else None,
            compiler_params=pltpu.CompilerParams(vmem_limit_bytes=limit * 1024 * 1024),
        )(*args)

    def like(shapes):
        return [pltpu.VMEM(x.shape, x.dtype) for x in shapes]

    def dma(n):
        return pltpu.SemaphoreType.DMA((n,))

    def exchange(part):
        return lax.all_to_all(part, "dp", 0, 0, tiled=True)

    m_s, s_s, z_s = s((width, cols)), s((4, width, lanes)), s((4 * 320, lanes), BF16)
    b_s = s((inner, cols), BF16)
    row_s, low_s = s((width, nodes)), s((width, nodes), BF16)
    layer_outs = [m_s, s_s, z_s, low_s, row_s, s((devices, 1, 2 * width + 128))]
    fwd_scratch = like([s((width, inner), BF16), s((width, lanes), BF16), s((width, lanes))])
    table_outs = [b_s, s((2, cols)), s((8, lanes)), s((nodes, 128), BF16), s((128, nodes), BF16)]
    first_args = [node_feats, edge_feats, segment_ids, nbr_t, mask_t, degrees, w_edge, w_pre, b_pre, wpost_t, w_mix]
    x0, b, live, rows, g, gt, m0, s0, z0, y0, u0, part = call(
        functools.partial(forward_first_kernel, 0),
        first_args, [low_s] + table_outs + layer_outs,
        fwd_scratch + like(first_args) + [dma(11)], range(11),
    )
    tables = [b, live, rows, g, gt]
    recv = exchange(part)
    norm0, h1, x1, m1, s1, z1, y1, u1, part = call(
        functools.partial(forward_next_kernel, 1),
        [recv, u0, x0, bn_gain, bn_bias, w_edge, w_pre, b_pre, wpost_t, w_mix] + tables,
        [s((8, width)), row_s, low_s] + layer_outs,
        fwd_scratch,
    )
    recv = exchange(part)
    sums_out = s((devices, 1, 2 * width))
    norm1, h2, dh2, dv1, part = call(
        functools.partial(last_gate_kernel, 1),
        [recv, u1, h1, bn_gain, bn_bias, rows, readout_grad],
        [s((8, width)), row_s, row_s, row_s, sums_out],
    )
    sum_s = s((1, 2 * width))
    du_s, d_s, dm_s = low_s, s((4 * 192, lanes), BF16), s((width, cols), BF16)
    dcat_s, et_s, acc_s = s((3 * width, nodes), BF16), s((width, 64)), s((width, lanes))
    back_scratch = like([s_s, acc_s, s((width, width), BF16)])
    recv = exchange(part)
    sums1, du1, d1, dm1, dcat1, et1, dh1, dv0, part = call(
        functools.partial(backward_first_kernel, 1),
        [recv, dv1, dh2, u1, norm1, bn_gain, bn_bias, w_mix, wpost_t, w_pre] + tables + [m1, s1, u0, norm0],
        [sum_s, du_s, d_s, dm_s, dcat_s, et_s, row_s, row_s, sums_out],
        back_scratch,
    )
    recv = exchange(part)
    grad_cols = 1664
    grad_s, half_s = s((width, grad_cols)), s((width // 2, grad_cols))
    sums0, dm0, node_grad, keep0, send0 = call(
        functools.partial(backward_last_kernel, 0),
        [recv, dv0, dh1, u0, norm0, bn_gain, bn_bias, w_mix, wpost_t, w_pre] + tables + [m0, s0, z0, y0, x0],
        [sum_s, dm_s, s((nodes, width)), half_s, half_s],
        like([du_s, d_s, dcat_s, et_s]) + back_scratch + like([grad_s]), free=(2,),
    )

    def swap(value, masks):
        return lax.ppermute(value, "dp", [(i, i ^ masks[i & 1]) for i in range(devices)])

    def after(value, *others):
        return lax.optimization_barrier((value, *others))[0]

    got0 = swap(send0, (1, 1))
    keep1, send1 = call(
        weight_kernel, [y1, after(du1, send0), d1, z1, x1, dcat1, et1], [half_s, half_s], like([grad_s]), cost=1.4
    )
    got1 = swap(send1, (1, 1))
    part = jnp.concatenate([keep0 + got0, keep1 + got1], axis=1)
    plane, line = (2, 4, 6), (8, 16, 24)
    stages = ((list(zip(plane, line)), 32), (list(zip(line, plane)), 8))
    edge_grad, readout = call(
        edge_kernel, [dm0, dm1, w_pre, w_edge, after(gt, part), h2, rows], [s((nodes, width)), s(readout_grad.shape)],
        [pltpu.VMEM((width, 128), F32)], free=(0, 1), cost=2,
    )
    for masks, size in stages:
        got = [swap(part[size * (i + 1) : size * (i + 2)], m) for i, m in enumerate(masks)]
        part = part[0:size] + got[0] + got[1] + got[2]
    mask = 32
    while mask < devices:
        part = part + swap(part, (mask, mask))
        mask *= 2
    for masks, _ in stages[::-1]:
        part = jnp.concatenate([part] + [swap(part, m) for m in masks], axis=0)
    other = swap(part, (1, 1))
    layers, blocks = w_pre.shape[0], width // 16
    finals = [
        s((layers, blocks, 2, 8, 832)), s((layers, blocks, 2, 8, width)), s((layers, 3, blocks, 2, 8, width)),
    ]
    bufs = [s((layers, blocks, 8, 832)), s((layers, blocks, 8, width)), s((layers, 2, blocks, 8, width))]
    ets = s((layers, blocks, 8, 64))
    *finals_in, ets_first = call(
        finish_first_kernel, [part], finals + [ets], like(bufs) + [dma(3)], far_out=(0, 1, 2), cost=2
    )
    g_post_t, g_mix, g_pre, g_b, g_edge = call(
        finish_last_kernel, [*finals_in, ets_first, other, w_edge, w_pre], finals + [s(b_pre.shape), s(w_edge.shape)],
        like(bufs + [ets, s((layers, blocks, 2, 8, width))]) + [dma(4)],
        far=(0, 1, 2), far_out=(0, 1, 2), free=(3, 4), alias={0: 0, 1: 1, 2: 2},
    )
    g_post = jnp.swapaxes(g_post_t.reshape(wpost_t.shape), 2, 3)
    g_mix, g_pre = g_mix.reshape(w_mix.shape), g_pre.reshape(w_pre.shape)
    sums = jnp.concatenate([sums0, sums1], axis=0)
    return (
        readout, node_grad, edge_grad, g_edge, g_pre, g_b, g_post, g_mix, sums[:, width:], sums[:, :width],
    )


def solution(mesh):
    split, split2, full = P("dp"), P("dp", None), P()
    in_specs = (split2, split2, split, split2, split2, split) + (full,) * 7 + (split2,)
    out_specs = (split2, split2, split2) + (full,) * 7
    return jax.shard_map(
        functools.partial(on_device, mesh.shape["dp"]),
        mesh=mesh, in_specs=in_specs, out_specs=out_specs, check_vma=False,
    )
```

```python
import functools

import jax
import jax.numpy as jnp
from jax import lax
from jax.experimental import pallas as pl
from jax.experimental.pallas import tpu as pltpu
from jax.sharding import PartitionSpec as P

SUB_MAX = 160
DEGREE_CENTER = 2.0
SPREAD_OFFSET = 0.25
STABILITY_FLOOR = 1e-05

LEAF_SLOTS = 4
HUB_RANK = 16
LOG2E = 1.4426950408889634
LN2 = 0.6931471805599453
ROW_CHUNK = 64
F32 = jnp.float32
BF16 = jnp.bfloat16
NN = (((1,), (0,)), ((), ()))
NT = (((1,), (1,)), ((), ()))
TN = (((0,), (0,)), ((), ()))
TT = (((0,), (1,)), ((), ()))


def mm(a, b, dims=NN):
    return lax.dot_general(a, b, dims, preferred_element_type=F32)


def iota(shape, dim):
    return lax.broadcasted_iota(jnp.int32, shape, dim)


def to_cols(*rows):
    pad = [jnp.zeros((8 - len(rows), rows[0].shape[1]), F32)] if len(rows) < 8 else []
    turned = jnp.concatenate(list(rows) + pad, axis=0).T
    return [turned[:, i : i + 1] for i in range(len(rows))]


def to_rows(*cols):
    wide = jnp.concatenate([jnp.broadcast_to(c, (c.shape[0], 128 // len(cols))) for c in cols], axis=1).T
    step = 128 // len(cols)
    return [wide[i * step : i * step + 1] for i in range(len(cols))]


def fold(value, op):
    return op(value, pltpu.roll(value, 64, 1))


def lane_groups(nodes):
    return [(lo, min(lo + 256, nodes)) for lo in range(0, nodes, 256)]


def leaf_col(nodes, slot, node):
    lo, hi = next(g for g in lane_groups(nodes) if g[0] <= node < g[1])
    return LEAF_SLOTS * lo + slot * (hi - lo) + node - lo


def split_two(value):
    high = value.astype(BF16)
    return high, (value - high.astype(F32)).astype(BF16)


def start_copies(pairs, sems):
    copies = [pltpu.make_async_copy(src, dst, sems.at[i]) for i, (src, dst) in enumerate(pairs)]
    for copy in copies:
        copy.start()
    return copies


def wait_all(copies):
    for copy in copies:
        copy.wait()


def build_tables(ef_ref, seg_ref, nbr_ref, mask_ref, deg_ref, b_ref, live_ref, rows_ref, g_ref, gt_ref):
    nodes = seg_ref.shape[0]
    seg = seg_ref[...].reshape(1, nodes)
    lane_h = iota((1, 128), 1)
    sub_h = iota((128, 1), 0)
    node_row = jnp.zeros((1, 128), jnp.int32)
    node_col = jnp.zeros((128, 1), jnp.int32)
    lane_r, sub_r = lane_h & 15, sub_h & 15
    lane_s, sub_s = (lane_h >> 4) & 3, (sub_h >> 4) & 3
    below = [jnp.sum((seg < s).astype(jnp.int32), axis=1, keepdims=True) for s in range(5)]
    for s in range(4):
        start, size = below[s], below[s + 1] - below[s]
        node_row = jnp.where(lane_s == s, jnp.where(lane_r < size, start + lane_r, -1), node_row)
        node_col = jnp.where(sub_s == s, jnp.where(sub_r < size, start + sub_r, -1), node_col)
    node_col = jnp.where(sub_h < 64, node_col, -1)
    g = (iota((nodes, 128), 0) == node_row).astype(F32).astype(BF16)
    gt = (iota((128, nodes), 1) == node_col).astype(F32).astype(BF16)
    g_ref[...] = g
    gt_ref[...] = gt
    is_hub = jnp.sum(gt.astype(F32), axis=0, keepdims=True)

    nbr = nbr_ref[...]
    mask = (mask_ref[...] > 0).astype(F32)
    nbr_h = (
        mm((nbr >> 3).astype(F32).astype(BF16), g) * 8.0 + mm((nbr & 7).astype(F32).astype(BF16), g)
    ).astype(jnp.int32)
    mask_h = mm(mask.astype(BF16), g)
    valid = (node_row >= 0).astype(F32)
    first = (lane_h < 64).astype(F32)

    def degree_rows(deg):
        log_degree = jnp.log(deg + 1.0)
        return log_degree / DEGREE_CENTER, DEGREE_CENTER / log_degree

    deg = deg_ref[...].reshape(1, nodes).astype(F32)
    deg_h = mm(jnp.broadcast_to(deg, (8, nodes)).astype(BF16), g)[0:1]
    deg_h = jnp.where(valid > 0, deg_h, 1.0)
    amp, att = degree_rows(deg)
    amp_h, att_h = degree_rows(deg_h)
    filled = jnp.sum(mask, axis=0, keepdims=True)
    filled_h = jnp.maximum(jnp.sum(mask_h, axis=0, keepdims=True), 1.0)
    rows_ref[...] = jnp.zeros_like(rows_ref)
    for i, (leaf, hub) in enumerate(
        (
            (amp, amp_h),
            (att, att_h),
            (1.0 / filled, 1.0 / filled_h),
            ((seg < 4).astype(F32), None),
            (1.0 - is_hub, valid * first),
            (is_hub, valid),
            (jnp.sum(mask[1:LEAF_SLOTS], axis=0, keepdims=True) - (LEAF_SLOTS - 2.0), filled_h - 16.0),
            (seg.astype(F32), None),
        )
    ):
        rows_ref[i : i + 1, 0:nodes] = leaf
        if hub is not None:
            rows_ref[i : i + 1, nodes : nodes + 128] = hub

    ef_t = ef_ref[...].T
    ef_h = mm(ef_t, g).astype(BF16)
    hub_iota = iota((nodes, 128), 0)
    for first_node, end_node in lane_groups(nodes):
        span = slice(first_node, end_node)
        size = end_node - first_node
        node_iota = iota((nodes, size), 0)
        zero16 = jnp.zeros((16, size), BF16)
        for k in range(LEAF_SLOTS):
            lo = leaf_col(nodes, k, first_node)
            cols = slice(lo, lo + size)
            b_ref[0:nodes, cols] = (node_iota == nbr[k : k + 1, span]).astype(F32).astype(BF16)
            piece = ef_t[16 * k : 16 * k + 16, span]
            for r, part in enumerate((piece, zero16, piece, zero16)):
                b_ref[nodes + 16 * r : nodes + 16 * r + 16, cols] = part
            live_ref[0:1, cols] = mask[k : k + 1, span] * LOG2E
            live_ref[1:2, cols] = mask[k : k + 1, span]
    own_half = (iota((32, 128), 0) < 16) == (iota((32, 128), 1) < 64)
    for j in range(8):
        lo = LEAF_SLOTS * nodes + 128 * j
        index = jnp.where(lane_h < 64, nbr_h[2 * j : 2 * j + 1], nbr_h[2 * j + 1 : 2 * j + 2])
        b_ref[0:nodes, lo : lo + 128] = (hub_iota == index).astype(F32).astype(BF16)
        piece = jnp.where(own_half, ef_h[32 * j : 32 * j + 32].astype(F32), 0.0).astype(BF16)
        b_ref[nodes : nodes + 32, lo : lo + 128] = piece
        b_ref[nodes + 32 : nodes + 64, lo : lo + 128] = piece
        live = jnp.where(lane_h < 64, mask_h[2 * j : 2 * j + 1], mask_h[2 * j + 1 : 2 * j + 2])
        live_ref[0:1, lo : lo + 128] = live * LOG2E
        live_ref[1:2, lo : lo + 128] = live


def tower_weights(wpost_ref, layer, t):
    w = wpost_ref[layer, t]
    inner = iota((64, 320), 1) >= 64
    zero = jnp.zeros((64, 320), BF16)
    return jnp.concatenate(
        [w[:, 0:320], jnp.where(inner, w[:, 256:576], zero), jnp.where(inner, w[:, 512:832], zero)], axis=0
    )


def forward_layer(
    layer, x_ref, wedge_ref, wpre_ref, bias, wpost_ref, wmix_ref, b_ref, live_ref, rows_ref, g_ref, gt_ref,
    m_ref, s_ref, z_ref, y_ref, u_ref, part_ref, a_ref, ya_ref, own_ref,
):
    width, nodes = x_ref.shape
    leaf_cols = LEAF_SLOTS * nodes
    x = x_ref[...]
    g = g_ref[...]
    own = mm(wpre_ref[layer, 0:width], x, TN) + bias
    own_ref[:, 0:nodes] = own
    a_ref[:, 0:nodes] = mm(wpre_ref[layer, width : 2 * width], x, TN).astype(BF16)
    wedge = wedge_ref[layer]
    both = mm(wpre_ref[layer, 2 * width :], jnp.concatenate([wedge] * 4, axis=0), TT)
    high, rest = split_two(both)
    a_ref[:, nodes : nodes + 64] = jnp.where(iota((width, 64), 1) < 32, high, rest)
    own_high, own_rest = split_two(own)
    own_ref[:, nodes:] = mm(own_high, g) + mm(own_rest, g)
    a = a_ref[...]

    def messages(lo, hi):
        m_ref[:, lo:hi] = mm(a, b_ref[:, lo:hi])

    x_h = mm(x, g).astype(BF16)
    for t in range(4):
        z_ref[320 * t : 320 * t + 64, 0:nodes] = x[64 * t : 64 * t + 64]
        z_ref[320 * t : 320 * t + 64, nodes:] = x_h[64 * t : 64 * t + 64]

    def summarize(i, tiles):
        per = 64 // ROW_CHUNK
        zr = (i // per) * 320 + 64 + (i % per) * ROW_CHUNK
        rows = pl.ds(i * ROW_CHUNK, ROW_CHUNK)
        for c in tiles:
            hub = c == nodes // 128
            lanes = slice(128 * c, 128 * c + 128)
            if hub:
                cols = [leaf_cols + 128 * j for j in range(8)]
                first = m_ref[rows, leaf_cols : leaf_cols + 128]
                first = jnp.where(iota((1, 128), 1) < 64, first, pltpu.roll(first, 64, 1))
            else:
                zero, *cols = [leaf_col(nodes, k, 128 * c) for k in range(LEAF_SLOTS)]
                first = m_ref[rows, zero : zero + 128]
            offs = []
            for lo in cols:
                d = (m_ref[rows, lo : lo + 128] - first) * live_ref[0:1, lo : lo + 128]
                m_ref[rows, lo : lo + 128] = d
                offs.append(d)

            def total(parts, op):
                while len(parts) > 1:
                    parts = [op(*parts[i : i + 2]) if i + 1 < len(parts) else parts[i] for i in range(0, len(parts), 2)]
                return fold(parts[0], op) if hub else parts[0]

            inv, missing = rows_ref[2:3, lanes], rows_ref[6:7, lanes]
            mean = total(offs, jnp.add) * inv
            var = total([d * d for d in offs], jnp.add) * inv - mean * mean
            spread = jnp.maximum(var * (LN2 * LN2), 0.0) + SPREAD_OFFSET
            rstd = lax.rsqrt(spread)
            top = jnp.maximum(total(offs, jnp.maximum), 0.0)
            low = jnp.minimum(total(offs, jnp.minimum), 0.0)
            ups = total([jnp.exp2(d - top) for d in offs], jnp.add) + missing * jnp.exp2(-top)
            downs = total([jnp.exp2(low - d) for d in offs], jnp.add) + missing * jnp.exp2(low)
            smax = top + jnp.log2(ups)
            smin = low - jnp.log2(downs)
            base = own_ref[rows, lanes] + first
            for n, stat in enumerate((mean, smax, smin, rstd)):
                s_ref[n, rows, lanes] = stat
                value = base + LN2 * stat if n < 3 else spread * rstd
                z_ref[pl.ds(zr + 64 * n, ROW_CHUNK), lanes] = value.astype(BF16)

    groups = [(leaf_cols, leaf_cols + 1024, range(nodes // 128, nodes // 128 + 1))]
    for lo, hi in lane_groups(nodes):
        groups.append((LEAF_SLOTS * lo, LEAF_SLOTS * hi, range(lo // 128, hi // 128)))
    waiting = None
    for group in groups + [None]:
        if group is not None:
            messages(*group[0:2])
        if waiting is not None:
            for i in range(width // ROW_CHUNK):
                summarize(i, waiting[2])
        waiting = group

    amp, att = rows_ref[0:1], rows_ref[1:2]
    for t in range(4):
        r = mm(tower_weights(wpost_ref, layer, t), z_ref[320 * t : 320 * t + 320])
        ya_ref[64 * t : 64 * t + 64] = (r[0:64] + amp * r[64:128] + att * r[128:192]).astype(BF16)
    spread_out = mm(ya_ref[:, nodes:], gt_ref[...])
    y = jnp.where(rows_ref[5:6, 0:nodes] > 0, spread_out, ya_ref[:, 0:nodes].astype(F32)).astype(BF16)
    y_ref[...] = y
    u = mm(wmix_ref[layer], y, TN)
    u_ref[...] = u
    alive = rows_ref[3:4, 0:nodes]
    count = jnp.sum(alive, axis=1, keepdims=True)
    mean = jnp.sum(alive * u, axis=1, keepdims=True) / count
    off = u - mean
    square = jnp.sum(alive * off * off, axis=1, keepdims=True)
    row = jnp.concatenate(to_rows(mean, square) + [jnp.broadcast_to(count, (1, 128))], axis=1)
    part_ref[...] = jnp.broadcast_to(row[None], part_ref.shape)


def forward_first_kernel(
    layer, nf_hbm, ef_hbm, seg_hbm, nbr_hbm, mask_hbm, deg_hbm, wedge_hbm, wpre_hbm, bpre_hbm, wpost_hbm, wmix_hbm,
    x_ref, b_ref, live_ref, rows_ref, g_ref, gt_ref, m_ref, s_ref, z_ref, y_ref, u_ref, part_ref,
    a_ref, ya_ref, own_ref, nf_ref, ef_ref, seg_ref, nbr_ref, mask_ref, deg_ref, wedge_ref, wpre_ref, bpre_ref, wpost_ref, wmix_ref, in_sems,
):
    loads = start_copies(
        [
            (seg_hbm, seg_ref), (nbr_hbm, nbr_ref), (mask_hbm, mask_ref), (deg_hbm, deg_ref), (ef_hbm, ef_ref), (nf_hbm, nf_ref),
            (wpre_hbm.at[0:1], wpre_ref), (wedge_hbm, wedge_ref), (bpre_hbm, bpre_ref),
            (wpost_hbm.at[0:1], wpost_ref), (wmix_hbm.at[0:1], wmix_ref),
        ],
        in_sems,
    )
    wait_all(loads)
    build_tables(ef_ref, seg_ref, nbr_ref, mask_ref, deg_ref, b_ref, live_ref, rows_ref, g_ref, gt_ref)
    x_ref[...] = nf_ref[...].T
    forward_layer(
        layer, x_ref, wedge_ref, wpre_ref, *to_cols(bpre_ref[layer : layer + 1]), wpost_ref, wmix_ref, b_ref,
        live_ref, rows_ref, g_ref, gt_ref, m_ref, s_ref, z_ref, y_ref, u_ref, part_ref, a_ref, ya_ref, own_ref,
    )


def norm_rows(recv_ref):
    w = (recv_ref.shape[2] - 128) // 2
    recv = recv_ref[...]
    means, squares = recv[:, :, 0:w], recv[:, :, w : 2 * w]
    counts = jnp.concatenate([recv[:, :, 2 * w :]] * (w // 128), axis=2)
    total = jnp.sum(counts, axis=0)
    mean = jnp.sum(counts * means, axis=0) / total
    off = means - mean[None]
    var = jnp.sum(squares + counts * off * off, axis=0) / total
    return mean, lax.rsqrt(var + STABILITY_FLOOR), total


def normed(u, norm_ref, gain_ref, bias_ref, layer):
    mean, scale, gain, bias = to_cols(
        norm_ref[0:1], norm_ref[1:2], gain_ref[layer : layer + 1], bias_ref[layer : layer + 1]
    )
    xh = (u - mean) * scale
    return xh, xh * gain + bias


def store_norm(norm_ref, recv_ref):
    mean, scale, total = norm_rows(recv_ref)
    norm_ref[...] = jnp.zeros_like(norm_ref)
    norm_ref[0:1] = mean
    norm_ref[1:2] = scale
    norm_ref[2:3] = total


def forward_next_kernel(
    layer, recv_ref, u0_ref, x0_ref, gain_ref, bias_ref, wedge_ref, wpre_ref, bpre_ref, wpost_ref, wmix_ref,
    b_ref, live_ref, rows_ref, g_ref, gt_ref,
    norm_ref, h_ref, x_ref, m_ref, s_ref, z_ref, y_ref, u_ref, part_ref, a_ref, ya_ref, own_ref,
):
    store_norm(norm_ref, recv_ref)
    _, v = normed(u0_ref[...], norm_ref, gain_ref, bias_ref, layer - 1)
    h = x0_ref[...].astype(F32) + v / (1.0 + jnp.exp(-v))
    h_ref[...] = h
    x_ref[...] = h.astype(BF16)
    forward_layer(
        layer, x_ref, wedge_ref, wpre_ref, *to_cols(bpre_ref[layer : layer + 1]), wpost_ref, wmix_ref, b_ref,
        live_ref, rows_ref, g_ref, gt_ref, m_ref, s_ref, z_ref, y_ref, u_ref, part_ref, a_ref, ya_ref, own_ref,
    )


def gate_grad(dh, xh, v, dv_ref, part_ref):
    sig = 1.0 / (1.0 + jnp.exp(-v))
    dv = dh * sig * (1.0 + v * (1.0 - sig))
    dv_ref[...] = dv
    sums = [jnp.sum(p, axis=1, keepdims=True) for p in (dv, dv * xh)]
    row = jnp.concatenate(to_rows(*sums), axis=1)
    part_ref[...] = jnp.broadcast_to(row[None], part_ref.shape)


def last_gate_kernel(
    layer, recv_ref, u_ref, h_ref, gain_ref, bias_ref, rows_ref, rg_ref, norm_ref, h_out_ref, dh_ref, dv_ref, part_ref
):
    store_norm(norm_ref, recv_ref)
    xh, v = normed(u_ref[...], norm_ref, gain_ref, bias_ref, layer)
    nodes = v.shape[1]
    seeds = rg_ref.shape[0]
    sig = 1.0 / (1.0 + jnp.exp(-v))
    h_out_ref[...] = h_ref[...] + v * sig
    dh = jnp.zeros(v.shape, F32)
    cols = to_cols(*[rg_ref[s : s + 1] / SUB_MAX for s in range(seeds)])
    for s, col in enumerate(cols):
        dh = jnp.where(rows_ref[7:8, 0:nodes] == s, col, dh)
    dh_ref[...] = dh
    gate_grad(dh, xh, v, dv_ref, part_ref)


def backward_layer(
    layer, recv_ref, dv_ref, dh_ref, u_ref, norm_ref, gain_ref, bias_ref, wmix_ref, wpost_ref, wpre_ref,
    b_ref, live_ref, rows_ref, g_ref, gt_ref, m_ref, s_ref,
    gb_ref, du_ref, d_ref, dm_ref, dcat_ref, et_ref, ds_ref, acc_ref, bd_ref, beside=(),
):
    width, nodes = dv_ref.shape
    leaf_cols = LEAF_SLOTS * nodes
    sums = jnp.sum(recv_ref[...], axis=0)
    g_bias, g_gain = sums[:, 0:width], sums[:, width:]
    gb_ref[...] = sums
    xh, _ = normed(u_ref[...], norm_ref, gain_ref, bias_ref, layer)
    alive = rows_ref[3:4, 0:nodes]
    scale, part_bias, part_gain = to_cols(
        norm_ref[1:2] * gain_ref[layer : layer + 1], g_bias / norm_ref[2:3], g_gain / norm_ref[2:3]
    )
    du = scale * (dv_ref[...] - alive * (part_bias + xh * part_gain))
    du = du.astype(BF16)
    du_ref[...] = du
    dy = mm(wmix_ref[layer], du)
    dy_low = dy.astype(BF16)
    dcat_ref[2 * width :] = dy_low
    dy_h = mm(dy_low, g_ref[...])
    keep = rows_ref[4:5]
    amp, att = rows_ref[0:1], rows_ref[1:2]
    dy_all = jnp.concatenate([dy_low.astype(F32), dy_h], axis=1) * keep
    bd_ref[...] = jnp.zeros_like(bd_ref)
    for t in range(4):
        part = dy_all[64 * t : 64 * t + 64]
        d_ref[192 * t : 192 * t + 64] = part.astype(BF16)
        d_ref[192 * t + 64 : 192 * t + 128] = (part * amp).astype(BF16)
        d_ref[192 * t + 128 : 192 * t + 192] = (part * att).astype(BF16)
        w = tower_weights(wpost_ref, layer, t)
        dz = mm(w, d_ref[192 * t : 192 * t + 192], TN)
        for n in range(4):
            rows = slice(64 * t, 64 * t + 64)
            block = dz[64 * (n + 1) : 64 * (n + 2)]
            ds_ref[n, rows, 0:nodes] = block[:, 0:nodes]
            ds_ref[n, rows, nodes:] = fold(block[:, nodes:], jnp.add)
        bd_ref[64 * t : 64 * t + 64, 64 * t : 64 * t + 64] = wpost_ref[layer, t][:, 0:64]

    def spread_back(i, tiles):
        rows = pl.ds(i * ROW_CHUNK, ROW_CHUNK)
        for c in tiles:
            hub = c == nodes // 128
            lanes = slice(128 * c, 128 * c + 128)
            mean, smax, smin, rstd = (s_ref[n, rows, lanes] for n in range(4))
            dmean, dsmax, dsmin, dstd = (ds_ref[n, rows, lanes] for n in range(4))
            inv = rows_ref[2:3, lanes]
            c1 = dstd * inv * rstd * LN2
            c0 = dmean * inv - mean * c1
            if hub:
                cols = [leaf_cols + 128 * j for j in range(8)]
                acc = None
            else:
                zero, *cols = [leaf_col(nodes, k, 128 * c) for k in range(LEAF_SLOTS)]
                acc = c0 + dsmax * jnp.exp2(-smax) + dsmin * jnp.exp2(smin)
                dm_ref[rows, zero : zero + 128] = acc.astype(BF16)
            for lo in cols:
                m = m_ref[rows, lo : lo + 128]
                d = c0 + m * c1 + dsmax * jnp.exp2(m - smax) + dsmin * jnp.exp2(smin - m)
                d = d * live_ref[1:2, lo : lo + 128]
                acc = d if acc is None else acc + d
                dm_ref[rows, lo : lo + 128] = d.astype(BF16)
            acc_ref[rows, lanes] = fold(acc, jnp.add) if hub else acc

    def land(lo, hi):
        return mm(dm_ref[:, lo:hi], b_ref[0 : nodes + 32, lo:hi], NT)

    groups = [(leaf_cols, leaf_cols + 1024, range(nodes // 128, nodes // 128 + 1))]
    for lo, hi in lane_groups(nodes):
        groups.append((LEAF_SLOTS * lo, LEAF_SLOTS * hi, range(lo // 128, hi // 128)))
    waiting, landed = None, 0.0
    for step, group in enumerate(groups + [None]):
        if group is not None:
            for i in range(width // ROW_CHUNK):
                spread_back(i, group[2])
        if step < len(beside):
            beside[step]()
        if waiting is not None:
            landed = landed + land(*waiting[0:2])
        waiting = group

    down = acc_ref[:, 0:nodes] + mm(acc_ref[:, nodes:].astype(BF16), gt_ref[...])
    dcat_ref[0:width] = down.astype(BF16)
    dcat_ref[width : 2 * width] = landed[:, 0:nodes].astype(BF16)
    once = jnp.where(iota((1, nodes + 128), 1) < nodes + 64, acc_ref[...], 0.0)
    bias = jnp.sum(once, axis=1, keepdims=True)
    factor = landed[:, nodes : nodes + 16] + landed[:, nodes + 16 : nodes + 32]
    et_ref[...] = jnp.concatenate([factor, jnp.broadcast_to(bias, (width, 48))], axis=1)
    weights = jnp.concatenate([wpre_ref[layer, 0:width], wpre_ref[layer, width : 2 * width]], axis=1)
    dh = mm(weights, dcat_ref[0 : 2 * width])
    dh = dh + mm(bd_ref[...], dcat_ref[2 * width :], TN)
    return dh_ref[...] + dh


def piece_owner(core, half, place, mixed):
    plane_first = ((place >> 2) << 1) | ((place & 3) << 3)
    line_first = ((place >> 2) << 3) | ((place & 3) << 1)
    return half + (jnp.where(core == half, plane_first, line_first) if mixed else plane_first)


def put_tower_grad(t, d_ref, z_ref, grads_ref):
    r = mm(d_ref[192 * t : 192 * t + 192], z_ref[320 * t : 320 * t + 320], NT)
    rows = slice(64 * t, 64 * t + 64)
    first = iota((64, 256), 1) < 64
    grads_ref[rows, 0:256] = r[0:64, 0:256]
    grads_ref[rows, 256:512] = jnp.where(first, jnp.concatenate([r[0:64, 256:320]] * 4, axis=1), r[64:128, 0:256])
    grads_ref[rows, 512:768] = jnp.where(first, jnp.concatenate([r[64:128, 256:320]] * 4, axis=1), r[128:192, 0:256])
    grads_ref[rows, 768:832] = r[128:192, 256:320]


def put_mix_grad(y_ref, du_ref, grads_ref):
    grads_ref[:, 896:1152] = mm(y_ref[...], du_ref[...], NT)


def put_message_grads(mixed, x_ref, dcat_ref, et_ref, grads_ref, keep_ref, send_ref):
    width = x_ref.shape[0]
    grads_ref[:, 832:896] = et_ref[...]
    grads_ref[:, 1152:1664] = mm(x_ref[...], dcat_ref[0 : 2 * width], NT)
    me = lax.axis_index("dp") & 31
    for place in range(16):
        for half, ref in ((0, keep_ref), (1, send_ref)):
            row = pl.multiple_of((me ^ piece_owner(me & 1, half, place, mixed)) * 8, 8)
            ref[8 * place : 8 * place + 8] = grads_ref[pl.ds(row, 8)]


def grad_steps(d_ref, z_ref, y_ref, du_ref, grads_ref):
    steps = [functools.partial(put_tower_grad, t, d_ref, z_ref, grads_ref) for t in range(4)]
    return steps + [functools.partial(put_mix_grad, y_ref, du_ref, grads_ref)]


def backward_first_kernel(
    layer, recv_ref, dv_ref, dh_ref, u_ref, norm_ref, gain_ref, bias_ref, wmix_ref, wpost_ref, wpre_ref,
    b_ref, live_ref, rows_ref, g_ref, gt_ref, m_ref, s_ref, z_ref, y_ref, x_ref, u_low_ref, norm_low_ref,
    gb_ref, dm_ref, dh_out_ref, dv_out_ref, part_ref, keep_ref, send_ref,
    du_ref, d_ref, dcat_ref, et_ref, ds_ref, acc_ref, bd_ref, grads_ref,
):
    dh = backward_layer(
        layer, recv_ref, dv_ref, dh_ref, u_ref, norm_ref, gain_ref, bias_ref, wmix_ref, wpost_ref, wpre_ref,
        b_ref, live_ref, rows_ref, g_ref, gt_ref, m_ref, s_ref,
        gb_ref, du_ref, d_ref, dm_ref, dcat_ref, et_ref, ds_ref, acc_ref, bd_ref,
        grad_steps(d_ref, z_ref, y_ref, du_ref, grads_ref),
    )
    put_message_grads(False, x_ref, dcat_ref, et_ref, grads_ref, keep_ref, send_ref)
    dh_out_ref[...] = dh
    xh, v = normed(u_low_ref[...], norm_low_ref, gain_ref, bias_ref, layer - 1)
    gate_grad(dh, xh, v, dv_out_ref, part_ref)


def backward_last_kernel(
    layer, recv_ref, dv_ref, dh_ref, u_ref, norm_ref, gain_ref, bias_ref, wmix_ref, wpost_ref, wpre_ref,
    b_ref, live_ref, rows_ref, g_ref, gt_ref, m_ref, s_ref, z_ref, y_ref, x_ref,
    sums1_ref, g_gain_ref, g_bias_ref, dm_ref, node_ref, keep_ref, send_ref,
    gb_ref, du_ref, d_ref, dcat_ref, et_ref, ds_ref, acc_ref, bd_ref, grads_ref,
):
    dh = backward_layer(
        layer, recv_ref, dv_ref, dh_ref, u_ref, norm_ref, gain_ref, bias_ref, wmix_ref, wpost_ref, wpre_ref,
        b_ref, live_ref, rows_ref, g_ref, gt_ref, m_ref, s_ref,
        gb_ref, du_ref, d_ref, dm_ref, dcat_ref, et_ref, ds_ref, acc_ref, bd_ref,
        grad_steps(d_ref, z_ref, y_ref, du_ref, grads_ref),
    )
    put_message_grads(True, x_ref, dcat_ref, et_ref, grads_ref, keep_ref, send_ref)
    node_ref[...] = dh.T
    width = node_ref.shape[1]
    for out_ref, cols in ((g_bias_ref, slice(0, width)), (g_gain_ref, slice(width, 2 * width))):
        out_ref[0:1] = gb_ref[:, cols]
        out_ref[1:2] = sums1_ref[:, cols]


def edge_kernel(dm0_ref, dm1_ref, wpre_ref, wedge_ref, gt_ref, h_ref, rows_ref, out_ref, readout_ref, acc_ref):
    width = dm0_ref.shape[0]
    nodes = gt_ref.shape[1]
    leaf_cols = LEAF_SLOTS * nodes
    total = None
    for layer, dm_ref in ((0, dm0_ref), (1, dm1_ref)):
        w = mm(wedge_ref[layer], wpre_ref[layer, 2 * width :]).astype(BF16)
        part = mm(w, dm_ref[...])
        total = part if total is None else total + part
    hub = total[:, leaf_cols:]
    for j in range(8):
        acc_ref[32 * j : 32 * j + 16] = hub[:, 128 * j : 128 * j + 128]
        acc_ref[32 * j + 16 : 32 * j + 32] = pltpu.roll(hub[:, 128 * j : 128 * j + 128], 64, 1)
    high, rest = split_two(acc_ref[...])
    gt = gt_ref[...]
    spread_out = mm(high, gt) + mm(rest, gt)
    leaf = []
    for k in range(LEAF_SLOTS):
        parts = []
        for lo, hi in lane_groups(nodes):
            col = leaf_col(nodes, k, lo)
            parts.append(total[:, col : col + hi - lo])
        leaf.append(jnp.concatenate(parts, axis=1))
    leaf = jnp.concatenate(leaf, axis=0)
    out = jnp.concatenate([spread_out[0:64] + leaf, spread_out[64:]], axis=0)
    out_ref[...] = out.T
    belong = (iota((8, nodes), 0).astype(F32) == rows_ref[7:8, 0:nodes]).astype(F32)
    total = lax.dot_general(belong, h_ref[...], NT, precision=lax.Precision.HIGHEST, preferred_element_type=F32)
    readout_ref[...] = total[0 : readout_ref.shape[0]] / SUB_MAX


def finish_half(half, half_refs, outs, bufs, sems):
    me = lax.axis_index("dp") & 31
    core = me & 1
    post, mix, pre, et = bufs
    for layer in range(post.shape[0]):
        for place in range(16):
            block = (me ^ piece_owner(core, half, place, layer == 0)) >> 1
            piece = half_refs[layer][8 * place : 8 * place + 8]
            post[layer, block] = piece[:, 0:832]
            et[layer, block] = piece[:, 832:896]
            mix[layer, block] = piece[:, 896:1152]
            pre[layer, 0, block] = piece[:, 1152:1408]
            pre[layer, 1, block] = piece[:, 1408:1664]
    side = core ^ half
    post_out, mix_out, pre_out = outs
    pairs = [(post, post_out.at[:, :, side]), (mix, mix_out.at[:, :, side]), (pre, pre_out.at[:, 0:2, :, side])]
    return start_copies(pairs, sems)


def finish_first_kernel(half0_ref, half1_ref, post_out, mix_out, pre_out, et, post, mix, pre, sems):
    wait_all(finish_half(0, (half0_ref, half1_ref), (post_out, mix_out, pre_out), (post, mix, pre, et), sems))


def finish_last_kernel(
    post_in, mix_in, pre_in, other_et, half0_ref, half1_ref, wedge_ref, wpre_ref, post_out, mix_out, pre_out, gb_ref, gedge_ref,
    post, mix, pre, et, term, sems,
):
    del post_in, mix_in, pre_in
    copies = finish_half(1, (half0_ref, half1_ref), (post_out, mix_out, pre_out), (post, mix, pre, et), sems)
    width = wpre_ref.shape[2]
    core = lax.axis_index("dp") & 1
    for layer in range(2):
        mine, other = et[layer], other_et[layer]
        first, second = jnp.where(core == 0, other, mine), jnp.where(core == 0, mine, other)
        both = jnp.concatenate([first[:, None], second[:, None]], axis=1).reshape(width, 64)
        gb_ref[layer : layer + 1] = to_rows(both[:, 16:17])[0]
        factor = both[:, 0:16]
        high, rest = split_two(factor)
        last = (factor - high.astype(F32) - rest.astype(F32)).astype(BF16)
        three = jnp.concatenate([high, rest, last], axis=1)
        grad = mm(jnp.concatenate([wedge_ref[layer]] * 3, axis=0), three, TT)
        term[layer] = grad.reshape(term.shape[1:])
        parts = mm(three, wpre_ref[layer, 2 * width :], TT)
        gedge_ref[layer] = parts[0:16] + parts[16:32] + parts[32:48]
    copies += start_copies([(term, pre_out.at[:, 2])], sems.at[3:4])
    wait_all(copies)


def on_device(
    devices, node_feats, edge_feats, segment_ids, neighbours, nbr_mask, degrees, w_edge, w_pre, b_pre, w_post,
    w_mix, bn_gain, bn_bias, readout_grad,
):
    nodes, width = node_feats.shape
    lanes = nodes + 128
    cols = LEAF_SLOTS * nodes + 1024
    inner = nodes + 64
    nbr_t = neighbours.T
    mask_t = nbr_mask.T
    wpost_t = jnp.swapaxes(w_post, 2, 3)

    def s(shape, dtype=F32):
        return jax.ShapeDtypeStruct(shape, dtype)

    vmem = pl.BlockSpec(memory_space=pltpu.VMEM)
    hbm = pl.BlockSpec(memory_space=pltpu.HBM)

    def call(kernel, args, outs, scratch=(), far=(), free=(), far_out=(), alias={}, cost=0, limit=20):
        args = [pltpu.with_memory_space_constraint(a, pltpu.HBM) if i in far else a for i, a in enumerate(args)]
        return pl.pallas_call(
            kernel,
            in_specs=[hbm if i in far else vmem for i in range(len(args))],
            out_specs=[hbm if i in far_out else vmem for i in range(len(outs))],
            out_shape=[
                o if i in free else (pltpu.HBM if i in far_out else pltpu.VMEM)(o.shape, o.dtype)
                for i, o in enumerate(outs)
            ],
            scratch_shapes=list(scratch),
            input_output_aliases=alias,
            cost_estimate=pl.CostEstimate(flops=int(cost * 1e9), bytes_accessed=0, transcendentals=0) if cost else None,
            compiler_params=pltpu.CompilerParams(vmem_limit_bytes=limit * 1024 * 1024),
        )(*args)

    def like(shapes):
        return [pltpu.VMEM(x.shape, x.dtype) for x in shapes]

    def dma(n):
        return pltpu.SemaphoreType.DMA((n,))

    def exchange(part):
        return lax.all_to_all(part, "dp", 0, 0, tiled=True)

    m_s, s_s, z_s = s((width, cols)), s((4, width, lanes)), s((4 * 320, lanes), BF16)
    b_s = s((inner, cols), BF16)
    row_s, low_s = s((width, nodes)), s((width, nodes), BF16)
    layer_outs = [m_s, s_s, z_s, low_s, row_s, s((devices, 1, 2 * width + 128))]
    fwd_scratch = like([s((width, inner), BF16), s((width, lanes), BF16), s((width, lanes))])
    table_outs = [b_s, s((2, cols)), s((8, lanes)), s((nodes, 128), BF16), s((128, nodes), BF16)]
    first_args = [node_feats, edge_feats, segment_ids, nbr_t, mask_t, degrees, w_edge, w_pre, b_pre, wpost_t, w_mix]
    x0, b, live, rows, g, gt, m0, s0, z0, y0, u0, part = call(
        functools.partial(forward_first_kernel, 0),
        first_args, [low_s] + table_outs + layer_outs,
        fwd_scratch + like([a[0:1] if i in (7, 9, 10) else a for i, a in enumerate(first_args)]) + [dma(11)], range(11),
    )
    tables = [b, live, rows, g, gt]
    recv = exchange(part)
    norm0, h1, x1, m1, s1, z1, y1, u1, part = call(
        functools.partial(forward_next_kernel, 1),
        [recv, u0, x0, bn_gain, bn_bias, w_edge, w_pre, b_pre, wpost_t, w_mix] + tables,
        [s((8, width)), row_s, low_s] + layer_outs,
        fwd_scratch,
    )
    recv = exchange(part)
    sums_out = s((devices, 1, 2 * width))
    norm1, h2, dh2, dv1, part = call(
        functools.partial(last_gate_kernel, 1),
        [recv, u1, h1, bn_gain, bn_bias, rows, readout_grad],
        [s((8, width)), row_s, row_s, row_s, sums_out],
    )
    sum_s = s((1, 2 * width))
    du_s, d_s, dm_s = low_s, s((4 * 192, lanes), BF16), s((width, cols), BF16)
    dcat_s, et_s, acc_s = s((3 * width, nodes), BF16), s((width, 64)), s((width, lanes))
    back_scratch = like([s_s, acc_s, s((width, width), BF16)])
    recv = exchange(part)
    grad_cols = 1664
    grad_s, half_s = s((width, grad_cols)), s((width // 2, grad_cols))
    back_scratch = like([du_s, d_s, dcat_s, et_s]) + back_scratch + like([grad_s])
    sums1, dm1, dh1, dv0, part, keep1, send1 = call(
        functools.partial(backward_first_kernel, 1),
        [recv, dv1, dh2, u1, norm1, bn_gain, bn_bias, w_mix, wpost_t, w_pre] + tables + [m1, s1, z1, y1, x1, u0, norm0],
        [sum_s, dm_s, row_s, row_s, sums_out, half_s, half_s],
        back_scratch,
    )

    def swap(value, masks):
        return lax.ppermute(value, "dp", [(i, i ^ masks[i & 1]) for i in range(devices)])

    def together(*values):
        return lax.optimization_barrier(values)

    plane, line = (2, 4, 6), (8, 16, 24)
    first, second = list(zip(plane, line)), list(zip(line, plane))
    first1, second1 = list(zip(plane, plane)), list(zip(line, line))

    def relay(value, masks):
        one, two = swap(value, masks[0]), swap(value, masks[1])
        return jnp.concatenate([value, one, two, swap(one, masks[1])], axis=0)

    def spread(value):
        mask = 32
        while mask < devices:
            value = value + swap(value, (mask, mask))
            mask *= 2
        return value

    def scatter_sum(value, masks, size):
        got = [swap(value[size * (i + 1) : size * (i + 2)], m) for i, m in enumerate(masks)]
        return value[0:size] + got[0] + got[1] + got[2]

    def gather(value, masks):
        return jnp.concatenate([value] + [swap(value, m) for m in masks], axis=0)

    got1 = swap(send1, (1, 1))
    recv, got1 = together(exchange(part), got1)
    part1 = scatter_sum(keep1 + got1, first1, 32)
    g_gain, g_bias, dm0, node_grad, keep0, send0 = call(
        functools.partial(backward_last_kernel, 0),
        [recv, dv0, dh1, u0, norm0, bn_gain, bn_bias, w_mix, wpost_t, w_pre] + tables + [m0, s0, z0, y0, x0, sums1],
        [s(bn_gain.shape), s(bn_bias.shape), dm_s, s((nodes, width)), half_s, half_s],
        like([sum_s]) + back_scratch, free=(0, 1, 3), cost=8,
    )
    edge_grad, readout = call(
        edge_kernel, [dm0, dm1, w_pre, w_edge, gt, h2, rows],
        [s((nodes, width)), s(readout_grad.shape)], [pltpu.VMEM((width, 128), F32)], free=(0, 1), cost=2,
    )
    send0, part1, edge_grad, readout = together(send0, part1, edge_grad, readout)
    got0 = swap(send0, (1, 1))
    half0 = keep0 + got0
    part0 = scatter_sum(half0, first, 32)
    part1 = gather(spread(scatter_sum(part1, second1, 8)), second1)
    part1 = relay(together(part1, part0)[0], first1)
    part0 = spread(scatter_sum(part0, second, 8))
    part0 = gather(gather(part0, second), first)
    other1 = swap(part1, (1, 1))
    other0 = swap(part0, (1, 1))
    layers, blocks = w_pre.shape[0], width // 16
    finals = [
        s((layers, blocks, 2, 8, 832)), s((layers, blocks, 2, 8, width)), s((layers, 3, blocks, 2, 8, width)),
    ]
    bufs = [s((layers, blocks, 8, 832)), s((layers, blocks, 8, width)), s((layers, 2, blocks, 8, width))]
    ets = s((layers, blocks, 8, 64))
    *finals_in, ets_first = call(
        finish_first_kernel, [part0, part1], finals + [ets], like(bufs) + [dma(3)], far_out=(0, 1, 2), cost=2
    )
    g_post_t, g_mix, g_pre, g_b, g_edge = call(
        finish_last_kernel, [*finals_in, ets_first, other0, other1, w_edge, w_pre], finals + [s(b_pre.shape), s(w_edge.shape)],
        like(bufs + [ets, s((layers, blocks, 2, 8, width))]) + [dma(4)],
        far=(0, 1, 2), far_out=(0, 1, 2), free=(3, 4), alias={0: 0, 1: 1, 2: 2},
    )
    g_post = jnp.swapaxes(g_post_t.reshape(wpost_t.shape), 2, 3)
    g_mix, g_pre = g_mix.reshape(w_mix.shape), g_pre.reshape(w_pre.shape)
    return (
        readout, node_grad, edge_grad, g_edge, g_pre, g_b, g_post, g_mix, g_gain, g_bias,
    )


def solution(mesh):
    split, split2, full = P("dp"), P("dp", None), P()
    in_specs = (split2, split2, split, split2, split2, split) + (full,) * 7 + (split2,)
    out_specs = (split2, split2, split2) + (full,) * 7
    return jax.shard_map(
        functools.partial(on_device, mesh.shape["dp"]),
        mesh=mesh, in_specs=in_specs, out_specs=out_specs, check_vma=False,
    )
```

```python
import functools

import jax
import jax.numpy as jnp
from jax import lax
from jax.experimental import pallas as pl
from jax.experimental.pallas import tpu as pltpu
from jax.sharding import PartitionSpec as P

SUB_MAX = 160
DEGREE_CENTER = 2.0
SPREAD_OFFSET = 0.25
STABILITY_FLOOR = 1e-05

LEAF_SLOTS = 4
HUB_RANK = 16
LOG2E = 1.4426950408889634
LN2 = 0.6931471805599453
ROW_CHUNK = 64
PLANE, LINE = 0, 1
MASKS = ((2, 4, 6), (8, 16, 24))
SUM_KINDS = ((PLANE, LINE), (PLANE, LINE))
GATHER_KINDS = ((PLANE, LINE), (PLANE, PLANE))
F32 = jnp.float32
BF16 = jnp.bfloat16
NN = (((1,), (0,)), ((), ()))
NT = (((1,), (1,)), ((), ()))
TN = (((0,), (0,)), ((), ()))
TT = (((0,), (1,)), ((), ()))


def mm(a, b, dims=NN):
    return lax.dot_general(a, b, dims, preferred_element_type=F32)


def iota(shape, dim):
    return lax.broadcasted_iota(jnp.int32, shape, dim)


def to_cols(*rows):
    pad = [jnp.zeros((8 - len(rows), rows[0].shape[1]), F32)] if len(rows) < 8 else []
    turned = jnp.concatenate(list(rows) + pad, axis=0).T
    return [turned[:, i : i + 1] for i in range(len(rows))]


def to_rows(*cols):
    wide = jnp.concatenate([jnp.broadcast_to(c, (c.shape[0], 128 // len(cols))) for c in cols], axis=1).T
    step = 128 // len(cols)
    return [wide[i * step : i * step + 1] for i in range(len(cols))]


def fold(value, op):
    return op(value, pltpu.roll(value, 64, 1))


def lane_groups(nodes):
    return [(lo, min(lo + 256, nodes)) for lo in range(0, nodes, 256)]


def leaf_col(nodes, slot, node):
    lo, hi = next(g for g in lane_groups(nodes) if g[0] <= node < g[1])
    return LEAF_SLOTS * lo + slot * (hi - lo) + node - lo


def split_two(value):
    high = value.astype(BF16)
    return high, (value - high.astype(F32)).astype(BF16)


def start_copies(pairs, sems):
    copies = [pltpu.make_async_copy(src, dst, sems.at[i]) for i, (src, dst) in enumerate(pairs)]
    for copy in copies:
        copy.start()
    return copies


def wait_all(copies):
    for copy in copies:
        copy.wait()


def build_tables(ef_ref, seg_ref, nbr_ref, mask_ref, deg_ref, b_ref, live_ref, rows_ref, g_ref, gt_ref):
    nodes = seg_ref.shape[0]
    seg = seg_ref[...].reshape(1, nodes)
    lane_h = iota((1, 128), 1)
    sub_h = iota((128, 1), 0)
    node_row = jnp.zeros((1, 128), jnp.int32)
    node_col = jnp.zeros((128, 1), jnp.int32)
    lane_r, sub_r = lane_h & 15, sub_h & 15
    lane_s, sub_s = (lane_h >> 4) & 3, (sub_h >> 4) & 3
    below = [jnp.sum((seg < s).astype(jnp.int32), axis=1, keepdims=True) for s in range(5)]
    for s in range(4):
        start, size = below[s], below[s + 1] - below[s]
        node_row = jnp.where(lane_s == s, jnp.where(lane_r < size, start + lane_r, -1), node_row)
        node_col = jnp.where(sub_s == s, jnp.where(sub_r < size, start + sub_r, -1), node_col)
    node_col = jnp.where(sub_h < 64, node_col, -1)
    g = (iota((nodes, 128), 0) == node_row).astype(F32).astype(BF16)
    gt = (iota((128, nodes), 1) == node_col).astype(F32).astype(BF16)
    g_ref[...] = g
    gt_ref[...] = gt
    is_hub = jnp.sum(gt.astype(F32), axis=0, keepdims=True)

    nbr = nbr_ref[...]
    mask = (mask_ref[...] > 0).astype(F32)
    nbr_h = (
        mm((nbr >> 3).astype(F32).astype(BF16), g) * 8.0 + mm((nbr & 7).astype(F32).astype(BF16), g)
    ).astype(jnp.int32)
    mask_h = mm(mask.astype(BF16), g)
    valid = (node_row >= 0).astype(F32)
    first = (lane_h < 64).astype(F32)

    def degree_rows(deg):
        log_degree = jnp.log(deg + 1.0)
        return log_degree / DEGREE_CENTER, DEGREE_CENTER / log_degree

    deg = deg_ref[...].reshape(1, nodes).astype(F32)
    deg_h = mm(jnp.broadcast_to(deg, (8, nodes)).astype(BF16), g)[0:1]
    deg_h = jnp.where(valid > 0, deg_h, 1.0)
    amp, att = degree_rows(deg)
    amp_h, att_h = degree_rows(deg_h)
    filled = jnp.sum(mask, axis=0, keepdims=True)
    filled_h = jnp.maximum(jnp.sum(mask_h, axis=0, keepdims=True), 1.0)
    rows_ref[...] = jnp.zeros_like(rows_ref)
    for i, (leaf, hub) in enumerate(
        (
            (amp, amp_h),
            (att, att_h),
            (1.0 / filled, 1.0 / filled_h),
            ((seg < 4).astype(F32), None),
            (1.0 - is_hub, valid * first),
            (is_hub, valid),
            (jnp.sum(mask[1:LEAF_SLOTS], axis=0, keepdims=True) - (LEAF_SLOTS - 2.0), filled_h - 16.0),
            (seg.astype(F32), None),
        )
    ):
        rows_ref[i : i + 1, 0:nodes] = leaf
        if hub is not None:
            rows_ref[i : i + 1, nodes : nodes + 128] = hub

    ef_t = ef_ref[...].T
    nbr16 = nbr.astype(jnp.int16)
    ef_h = mm(ef_t, g).astype(BF16)
    hub_iota = iota((nodes, 128), 0)
    for first_node, end_node in lane_groups(nodes):
        span = slice(first_node, end_node)
        size = end_node - first_node
        node_iota = iota((nodes, size), 0).astype(jnp.int16)
        one16, none16 = jnp.ones((nodes, size), BF16), jnp.zeros((nodes, size), BF16)
        zero16 = jnp.zeros((16, size), BF16)
        for k in range(LEAF_SLOTS):
            lo = leaf_col(nodes, k, first_node)
            cols = slice(lo, lo + size)
            b_ref[0:nodes, cols] = jnp.where(node_iota == nbr16[k : k + 1, span], one16, none16)
            piece = ef_t[16 * k : 16 * k + 16, span]
            for r, part in enumerate((piece, zero16, piece, zero16)):
                b_ref[nodes + 16 * r : nodes + 16 * r + 16, cols] = part
            live_ref[0:1, cols] = mask[k : k + 1, span] * LOG2E
            live_ref[1:2, cols] = mask[k : k + 1, span]
    own_half = (iota((32, 128), 0) < 16) == (iota((32, 128), 1) < 64)
    for j in range(8):
        lo = LEAF_SLOTS * nodes + 128 * j
        index = jnp.where(lane_h < 64, nbr_h[2 * j : 2 * j + 1], nbr_h[2 * j + 1 : 2 * j + 2])
        b_ref[0:nodes, lo : lo + 128] = (hub_iota == index).astype(F32).astype(BF16)
        piece = jnp.where(own_half, ef_h[32 * j : 32 * j + 32].astype(F32), 0.0).astype(BF16)
        b_ref[nodes : nodes + 32, lo : lo + 128] = piece
        b_ref[nodes + 32 : nodes + 64, lo : lo + 128] = piece
        live = jnp.where(lane_h < 64, mask_h[2 * j : 2 * j + 1], mask_h[2 * j + 1 : 2 * j + 2])
        live_ref[0:1, lo : lo + 128] = live * LOG2E
        live_ref[1:2, lo : lo + 128] = live


def tower_weights(wpost_ref, layer, t):
    w = wpost_ref[layer, t]
    inner = iota((64, 320), 1) >= 64
    zero = jnp.zeros((64, 320), BF16)
    return jnp.concatenate(
        [w[:, 0:320], jnp.where(inner, w[:, 256:576], zero), jnp.where(inner, w[:, 512:832], zero)], axis=0
    )


def forward_layer(
    layer, x_ref, wedge_ref, wpre_ref, bias, wpost_ref, wmix_ref, b_ref, live_ref, rows_ref, g_ref, gt_ref,
    m_ref, s_ref, z_ref, y_ref, u_ref, part_ref, a_ref, ya_ref, own_ref,
):
    width, nodes = x_ref.shape
    leaf_cols = LEAF_SLOTS * nodes
    x = x_ref[...]
    g = g_ref[...]
    own = mm(wpre_ref[layer, 0:width], x, TN) + bias
    own_ref[:, 0:nodes] = own
    a_ref[:, 0:nodes] = mm(wpre_ref[layer, width : 2 * width], x, TN).astype(BF16)
    wedge = wedge_ref[layer]
    both = mm(wpre_ref[layer, 2 * width :], jnp.concatenate([wedge] * 4, axis=0), TT)
    high, rest = split_two(both)
    a_ref[:, nodes : nodes + 64] = jnp.where(iota((width, 64), 1) < 32, high, rest)
    own_high, own_rest = split_two(own)
    own_ref[:, nodes:] = mm(own_high, g) + mm(own_rest, g)
    a = a_ref[...]

    def messages(lo, hi):
        m_ref[:, lo:hi] = mm(a, b_ref[:, lo:hi])

    x_h = mm(x, g).astype(BF16)
    for t in range(4):
        z_ref[320 * t : 320 * t + 64, 0:nodes] = x[64 * t : 64 * t + 64]
        z_ref[320 * t : 320 * t + 64, nodes:] = x_h[64 * t : 64 * t + 64]

    def summarize(i, tiles):
        per = 64 // ROW_CHUNK
        zr = (i // per) * 320 + 64 + (i % per) * ROW_CHUNK
        rows = pl.ds(i * ROW_CHUNK, ROW_CHUNK)
        for c in tiles:
            hub = c == nodes // 128
            lanes = slice(128 * c, 128 * c + 128)
            if hub:
                cols = [leaf_cols + 128 * j for j in range(8)]
                first = m_ref[rows, leaf_cols : leaf_cols + 128]
                first = jnp.where(iota((1, 128), 1) < 64, first, pltpu.roll(first, 64, 1))
            else:
                zero, *cols = [leaf_col(nodes, k, 128 * c) for k in range(LEAF_SLOTS)]
                first = m_ref[rows, zero : zero + 128]
            offs = []
            for lo in cols:
                d = (m_ref[rows, lo : lo + 128] - first) * live_ref[0:1, lo : lo + 128]
                m_ref[rows, lo : lo + 128] = d
                offs.append(d)

            def total(parts, op):
                while len(parts) > 1:
                    parts = [op(*parts[i : i + 2]) if i + 1 < len(parts) else parts[i] for i in range(0, len(parts), 2)]
                return fold(parts[0], op) if hub else parts[0]

            inv, missing = rows_ref[2:3, lanes], rows_ref[6:7, lanes]
            mean = total(offs, jnp.add) * inv
            var = total([d * d for d in offs], jnp.add) * inv - mean * mean
            spread = jnp.maximum(var * (LN2 * LN2), 0.0) + SPREAD_OFFSET
            rstd = lax.rsqrt(spread)
            top = jnp.maximum(total(offs, jnp.maximum), 0.0)
            low = jnp.minimum(total(offs, jnp.minimum), 0.0)
            ups = total([jnp.exp2(d - top) for d in offs], jnp.add) + missing * jnp.exp2(-top)
            downs = total([jnp.exp2(low - d) for d in offs], jnp.add) + missing * jnp.exp2(low)
            smax = top + jnp.log2(ups)
            smin = low - jnp.log2(downs)
            base = own_ref[rows, lanes] + first
            for n, stat in enumerate((mean, smax, smin, rstd)):
                s_ref[n, rows, lanes] = stat
                value = base + LN2 * stat if n < 3 else spread * rstd
                z_ref[pl.ds(zr + 64 * n, ROW_CHUNK), lanes] = value.astype(BF16)

    groups = [(leaf_cols, leaf_cols + 1024, range(nodes // 128, nodes // 128 + 1))]
    for lo, hi in lane_groups(nodes):
        groups.append((LEAF_SLOTS * lo, LEAF_SLOTS * hi, range(lo // 128, hi // 128)))
    waiting = None
    for group in groups + [None]:
        if group is not None:
            messages(*group[0:2])
        if waiting is not None:
            for i in range(width // ROW_CHUNK):
                summarize(i, waiting[2])
        waiting = group

    amp, att = rows_ref[0:1], rows_ref[1:2]
    for t in range(4):
        r = mm(tower_weights(wpost_ref, layer, t), z_ref[320 * t : 320 * t + 320])
        ya_ref[64 * t : 64 * t + 64] = (r[0:64] + amp * r[64:128] + att * r[128:192]).astype(BF16)
    spread_out = mm(ya_ref[:, nodes:], gt_ref[...])
    y = jnp.where(rows_ref[5:6, 0:nodes] > 0, spread_out, ya_ref[:, 0:nodes].astype(F32)).astype(BF16)
    y_ref[...] = y
    u = mm(wmix_ref[layer], y, TN)
    u_ref[...] = u
    alive = rows_ref[3:4, 0:nodes]
    count = jnp.sum(alive, axis=1, keepdims=True)
    mean = jnp.sum(alive * u, axis=1, keepdims=True) / count
    off = u - mean
    square = jnp.sum(alive * off * off, axis=1, keepdims=True)
    row = jnp.concatenate(to_rows(mean, square) + [jnp.broadcast_to(count, (1, 128))], axis=1)
    part_ref[...] = jnp.broadcast_to(row[None], part_ref.shape)


def forward_first_kernel(
    layer, nf_hbm, ef_hbm, seg_hbm, nbr_hbm, mask_hbm, deg_hbm, wedge_hbm, wpre_hbm, bpre_hbm, wpost_hbm, wmix_hbm,
    x_ref, b_ref, live_ref, rows_ref, g_ref, gt_ref, m_ref, s_ref, z_ref, y_ref, u_ref, part_ref,
    a_ref, ya_ref, own_ref, nf_ref, ef_ref, seg_ref, nbr_ref, mask_ref, deg_ref, wedge_ref, wpre_ref, bpre_ref, wpost_ref, wmix_ref, in_sems,
):
    loads = start_copies(
        [
            (seg_hbm, seg_ref), (nbr_hbm, nbr_ref), (mask_hbm, mask_ref), (deg_hbm, deg_ref), (ef_hbm, ef_ref), (nf_hbm, nf_ref),
            (wpre_hbm.at[0:1], wpre_ref), (wedge_hbm, wedge_ref), (bpre_hbm, bpre_ref),
            (wpost_hbm.at[0:1], wpost_ref), (wmix_hbm.at[0:1], wmix_ref),
        ],
        in_sems,
    )
    wait_all(loads)
    build_tables(ef_ref, seg_ref, nbr_ref, mask_ref, deg_ref, b_ref, live_ref, rows_ref, g_ref, gt_ref)
    x_ref[...] = nf_ref[...].T
    forward_layer(
        layer, x_ref, wedge_ref, wpre_ref, *to_cols(bpre_ref[layer : layer + 1]), wpost_ref, wmix_ref, b_ref,
        live_ref, rows_ref, g_ref, gt_ref, m_ref, s_ref, z_ref, y_ref, u_ref, part_ref, a_ref, ya_ref, own_ref,
    )


def norm_rows(recv_ref):
    w = (recv_ref.shape[2] - 128) // 2
    recv = recv_ref[...]
    means, squares = recv[:, :, 0:w], recv[:, :, w : 2 * w]
    counts = jnp.concatenate([recv[:, :, 2 * w :]] * (w // 128), axis=2)
    total = jnp.sum(counts, axis=0)
    mean = jnp.sum(counts * means, axis=0) / total
    off = means - mean[None]
    var = jnp.sum(squares + counts * off * off, axis=0) / total
    return mean, lax.rsqrt(var + STABILITY_FLOOR), total


def normed(u, norm_ref, gain_ref, bias_ref, layer):
    mean, scale, gain, bias = to_cols(
        norm_ref[0:1], norm_ref[1:2], gain_ref[layer : layer + 1], bias_ref[layer : layer + 1]
    )
    xh = (u - mean) * scale
    return xh, xh * gain + bias


def store_norm(norm_ref, recv_ref):
    mean, scale, total = norm_rows(recv_ref)
    norm_ref[...] = jnp.zeros_like(norm_ref)
    norm_ref[0:1] = mean
    norm_ref[1:2] = scale
    norm_ref[2:3] = total


def forward_next_kernel(
    layer, recv_ref, u0_ref, x0_ref, gain_ref, bias_ref, wedge_ref, wpre_ref, bpre_ref, wpost_ref, wmix_ref,
    b_ref, live_ref, rows_ref, g_ref, gt_ref,
    norm_ref, h_ref, x_ref, m_ref, s_ref, z_ref, y_ref, u_ref, part_ref, a_ref, ya_ref, own_ref,
):
    store_norm(norm_ref, recv_ref)
    _, v = normed(u0_ref[...], norm_ref, gain_ref, bias_ref, layer - 1)
    h = x0_ref[...].astype(F32) + v / (1.0 + jnp.exp(-v))
    h_ref[...] = h
    x_ref[...] = h.astype(BF16)
    forward_layer(
        layer, x_ref, wedge_ref, wpre_ref, *to_cols(bpre_ref[layer : layer + 1]), wpost_ref, wmix_ref, b_ref,
        live_ref, rows_ref, g_ref, gt_ref, m_ref, s_ref, z_ref, y_ref, u_ref, part_ref, a_ref, ya_ref, own_ref,
    )


def gate_grad(dh, xh, v, dv_ref, part_ref):
    sig = 1.0 / (1.0 + jnp.exp(-v))
    dv = dh * sig * (1.0 + v * (1.0 - sig))
    dv_ref[...] = dv
    sums = [jnp.sum(p, axis=1, keepdims=True) for p in (dv, dv * xh)]
    row = jnp.concatenate(to_rows(*sums), axis=1)
    part_ref[...] = jnp.broadcast_to(row[None], part_ref.shape)


def last_gate_kernel(
    layer, recv_ref, u_ref, h_ref, gain_ref, bias_ref, rows_ref, rg_ref, norm_ref, h_out_ref, dh_ref, dv_ref, part_ref
):
    store_norm(norm_ref, recv_ref)
    xh, v = normed(u_ref[...], norm_ref, gain_ref, bias_ref, layer)
    nodes = v.shape[1]
    seeds = rg_ref.shape[0]
    sig = 1.0 / (1.0 + jnp.exp(-v))
    h_out_ref[...] = h_ref[...] + v * sig
    dh = jnp.zeros(v.shape, F32)
    cols = to_cols(*[rg_ref[s : s + 1] / SUB_MAX for s in range(seeds)])
    for s, col in enumerate(cols):
        dh = jnp.where(rows_ref[7:8, 0:nodes] == s, col, dh)
    dh_ref[...] = dh
    gate_grad(dh, xh, v, dv_ref, part_ref)


def backward_layer(
    layer, recv_ref, dv_ref, dh_ref, u_ref, norm_ref, gain_ref, bias_ref, wmix_ref, wpost_ref, wpre_ref,
    b_ref, live_ref, rows_ref, g_ref, gt_ref, m_ref, s_ref,
    gb_ref, du_ref, d_ref, dm_ref, dcat_ref, et_ref, ds_ref, bd_ref, beside=(),
):
    width, nodes = dv_ref.shape
    leaf_cols = LEAF_SLOTS * nodes
    sums = jnp.sum(recv_ref[...], axis=0)
    g_bias, g_gain = sums[:, 0:width], sums[:, width:]
    gb_ref[...] = sums
    xh, _ = normed(u_ref[...], norm_ref, gain_ref, bias_ref, layer)
    alive = rows_ref[3:4, 0:nodes]
    scale, part_bias, part_gain = to_cols(
        norm_ref[1:2] * gain_ref[layer : layer + 1], g_bias / norm_ref[2:3], g_gain / norm_ref[2:3]
    )
    du = scale * (dv_ref[...] - alive * (part_bias + xh * part_gain))
    du = du.astype(BF16)
    du_ref[...] = du
    dy = mm(wmix_ref[layer], du)
    dy_low = dy.astype(BF16)
    dcat_ref[2 * width :] = dy_low
    dy_h = mm(dy_low, g_ref[...])
    keep = rows_ref[4:5]
    amp, att = rows_ref[0:1], rows_ref[1:2]
    dy_all = jnp.concatenate([dy_low.astype(F32), dy_h], axis=1) * keep
    bd_ref[...] = jnp.zeros_like(bd_ref)
    for t in range(4):
        part = dy_all[64 * t : 64 * t + 64]
        d_ref[192 * t : 192 * t + 64] = part.astype(BF16)
        d_ref[192 * t + 64 : 192 * t + 128] = (part * amp).astype(BF16)
        d_ref[192 * t + 128 : 192 * t + 192] = (part * att).astype(BF16)
        w = tower_weights(wpost_ref, layer, t)
        dz = mm(w, d_ref[192 * t : 192 * t + 192], TN)
        for n in range(4):
            rows = slice(64 * t, 64 * t + 64)
            block = dz[64 * (n + 1) : 64 * (n + 2)]
            ds_ref[n, rows, 0:nodes] = block[:, 0:nodes]
            ds_ref[n, rows, nodes:] = fold(block[:, nodes:], jnp.add)
        bd_ref[64 * t : 64 * t + 64, 64 * t : 64 * t + 64] = wpost_ref[layer, t][:, 0:64]

    acc = ds_ref[0] + ds_ref[1] + ds_ref[2]
    down = acc[:, 0:nodes] + mm(acc[:, nodes:].astype(BF16), gt_ref[...])
    dcat_ref[0:width] = down.astype(BF16)
    once = jnp.where(iota((1, nodes + 128), 1) < nodes + 64, acc, 0.0)
    bias = jnp.sum(once, axis=1, keepdims=True)

    def spread_back(i, tiles):
        rows = pl.ds(i * ROW_CHUNK, ROW_CHUNK)
        for c in tiles:
            hub = c == nodes // 128
            lanes = slice(128 * c, 128 * c + 128)
            mean, smax, smin, rstd = (s_ref[n, rows, lanes] for n in range(4))
            dmean, dsmax, dsmin, dstd = (ds_ref[n, rows, lanes] for n in range(4))
            inv = rows_ref[2:3, lanes]
            c1 = dstd * inv * rstd * LN2
            c0 = dmean * inv - mean * c1
            if hub:
                cols = [leaf_cols + 128 * j for j in range(8)]
            else:
                zero, *cols = [leaf_col(nodes, k, 128 * c) for k in range(LEAF_SLOTS)]
                d = c0 + dsmax * jnp.exp2(-smax) + dsmin * jnp.exp2(smin)
                dm_ref[rows, zero : zero + 128] = d.astype(BF16)
            for lo in cols:
                m = m_ref[rows, lo : lo + 128]
                d = c0 + m * c1 + dsmax * jnp.exp2(m - smax) + dsmin * jnp.exp2(smin - m)
                d = d * live_ref[1:2, lo : lo + 128]
                dm_ref[rows, lo : lo + 128] = d.astype(BF16)

    def land(lo, hi):
        return mm(dm_ref[:, lo:hi], b_ref[0 : nodes + 32, lo:hi], NT)

    groups = [(leaf_cols, leaf_cols + 1024, range(nodes // 128, nodes // 128 + 1))]
    for lo, hi in lane_groups(nodes):
        groups.append((LEAF_SLOTS * lo, LEAF_SLOTS * hi, range(lo // 128, hi // 128)))
    waiting, landed = None, 0.0
    for step, group in enumerate(groups + [None]):
        if group is not None:
            for i in range(width // ROW_CHUNK):
                spread_back(i, group[2])
        if step < len(beside):
            beside[step]()
        if waiting is not None:
            landed = landed + land(*waiting[0:2])
        waiting = group

    dcat_ref[width : 2 * width] = landed[:, 0:nodes].astype(BF16)
    factor = landed[:, nodes : nodes + 16] + landed[:, nodes + 16 : nodes + 32]
    et_ref[...] = jnp.concatenate([factor, jnp.broadcast_to(bias, (width, 48))], axis=1)
    weights = jnp.concatenate([wpre_ref[layer, 0:width], wpre_ref[layer, width : 2 * width]], axis=1)
    dh = mm(weights, dcat_ref[0 : 2 * width])
    dh = dh + mm(bd_ref[...], dcat_ref[2 * width :], TN)
    return dh_ref[...] + dh


def piece_owner(core, half, place, kind):
    plane_first = ((place >> 2) << 1) | ((place & 3) << 3)
    line_first = ((place >> 2) << 3) | ((place & 3) << 1)
    choice = [plane_first if k == PLANE else line_first for k in kind]
    return half + jnp.where(core == half, *choice)


def larger(kind):
    return list(zip(*[MASKS[k] for k in kind]))


def smaller(kind):
    return list(zip(*[MASKS[1 - k] for k in kind]))


def put_tower_grad(t, d_ref, z_ref, grads_ref):
    r = mm(d_ref[192 * t : 192 * t + 192], z_ref[320 * t : 320 * t + 320], NT)
    rows = slice(64 * t, 64 * t + 64)
    first = iota((64, 256), 1) < 64
    grads_ref[rows, 0:256] = r[0:64, 0:256]
    grads_ref[rows, 256:512] = jnp.where(first, jnp.concatenate([r[0:64, 256:320]] * 4, axis=1), r[64:128, 0:256])
    grads_ref[rows, 512:768] = jnp.where(first, jnp.concatenate([r[64:128, 256:320]] * 4, axis=1), r[128:192, 0:256])
    grads_ref[rows, 768:832] = r[128:192, 256:320]


def put_mix_grad(y_ref, du_ref, grads_ref):
    grads_ref[:, 896:1152] = mm(y_ref[...], du_ref[...], NT)


def put_message_grads(layer, x_ref, dcat_ref, et_ref, grads_ref, keep_ref, send_ref):
    width = x_ref.shape[0]
    grads_ref[:, 832:896] = et_ref[...]
    grads_ref[:, 1152:1664] = mm(x_ref[...], dcat_ref[0 : 2 * width], NT)
    me = lax.axis_index("dp") & 31
    for place in range(16):
        for half, ref in ((0, keep_ref), (1, send_ref)):
            row = pl.multiple_of((me ^ piece_owner(me & 1, half, place, SUM_KINDS[layer])) * 8, 8)
            ref[8 * place : 8 * place + 8] = grads_ref[pl.ds(row, 8)]


def grad_steps(d_ref, z_ref, y_ref, du_ref, grads_ref):
    steps = [functools.partial(put_tower_grad, t, d_ref, z_ref, grads_ref) for t in range(4)]
    return steps + [functools.partial(put_mix_grad, y_ref, du_ref, grads_ref)]


def backward_first_kernel(
    layer, recv_ref, dv_ref, dh_ref, u_ref, norm_ref, gain_ref, bias_ref, wmix_ref, wpost_ref, wpre_ref,
    b_ref, live_ref, rows_ref, g_ref, gt_ref, m_ref, s_ref, z_ref, y_ref, x_ref, u_low_ref, norm_low_ref,
    gb_ref, dm_ref, dh_out_ref, dv_out_ref, part_ref, keep_ref, send_ref,
    du_ref, d_ref, dcat_ref, et_ref, ds_ref, bd_ref, grads_ref,
):
    dh = backward_layer(
        layer, recv_ref, dv_ref, dh_ref, u_ref, norm_ref, gain_ref, bias_ref, wmix_ref, wpost_ref, wpre_ref,
        b_ref, live_ref, rows_ref, g_ref, gt_ref, m_ref, s_ref,
        gb_ref, du_ref, d_ref, dm_ref, dcat_ref, et_ref, ds_ref, bd_ref,
        grad_steps(d_ref, z_ref, y_ref, du_ref, grads_ref),
    )
    put_message_grads(layer, x_ref, dcat_ref, et_ref, grads_ref, keep_ref, send_ref)
    dh_out_ref[...] = dh
    xh, v = normed(u_low_ref[...], norm_low_ref, gain_ref, bias_ref, layer - 1)
    gate_grad(dh, xh, v, dv_out_ref, part_ref)


def backward_last_kernel(
    layer, recv_ref, dv_ref, dh_ref, u_ref, norm_ref, gain_ref, bias_ref, wmix_ref, wpost_ref, wpre_ref,
    b_ref, live_ref, rows_ref, g_ref, gt_ref, m_ref, s_ref, z_ref, y_ref, x_ref,
    gb_ref, dm_ref, dh_out_ref, keep_ref, send_ref,
    du_ref, d_ref, dcat_ref, et_ref, ds_ref, bd_ref, grads_ref,
):
    dh = backward_layer(
        layer, recv_ref, dv_ref, dh_ref, u_ref, norm_ref, gain_ref, bias_ref, wmix_ref, wpost_ref, wpre_ref,
        b_ref, live_ref, rows_ref, g_ref, gt_ref, m_ref, s_ref,
        gb_ref, du_ref, d_ref, dm_ref, dcat_ref, et_ref, ds_ref, bd_ref,
        grad_steps(d_ref, z_ref, y_ref, du_ref, grads_ref),
    )
    put_message_grads(layer, x_ref, dcat_ref, et_ref, grads_ref, keep_ref, send_ref)
    dh_out_ref[...] = dh


def edge_kernel(
    dm0_ref, dm1_ref, wpre_ref, wedge_ref, gt_ref, h_ref, rows_ref, dh_ref, sums0_ref, sums1_ref,
    out_ref, readout_ref, node_ref, g_gain_ref, g_bias_ref, acc_ref,
):
    width = dm0_ref.shape[0]
    nodes = gt_ref.shape[1]
    leaf_cols = LEAF_SLOTS * nodes
    total = None
    for layer, dm_ref in ((0, dm0_ref), (1, dm1_ref)):
        w = mm(wedge_ref[layer], wpre_ref[layer, 2 * width :]).astype(BF16)
        part = mm(w, dm_ref[...])
        total = part if total is None else total + part
    hub = total[:, leaf_cols:]
    for j in range(8):
        acc_ref[32 * j : 32 * j + 16] = hub[:, 128 * j : 128 * j + 128]
        acc_ref[32 * j + 16 : 32 * j + 32] = pltpu.roll(hub[:, 128 * j : 128 * j + 128], 64, 1)
    high, rest = split_two(acc_ref[...])
    gt = gt_ref[...]
    spread_out = mm(high, gt) + mm(rest, gt)
    leaf = []
    for k in range(LEAF_SLOTS):
        parts = []
        for lo, hi in lane_groups(nodes):
            col = leaf_col(nodes, k, lo)
            parts.append(total[:, col : col + hi - lo])
        leaf.append(jnp.concatenate(parts, axis=1))
    leaf = jnp.concatenate(leaf, axis=0)
    out = jnp.concatenate([spread_out[0:64] + leaf, spread_out[64:]], axis=0)
    out_ref[...] = out.T
    belong = (iota((8, nodes), 0).astype(F32) == rows_ref[7:8, 0:nodes]).astype(F32)
    total = lax.dot_general(belong, h_ref[...], NT, precision=lax.Precision.HIGHEST, preferred_element_type=F32)
    readout_ref[...] = total[0 : readout_ref.shape[0]] / SUB_MAX
    node_ref[...] = dh_ref[...].T
    for out_ref, cols in ((g_bias_ref, slice(0, width)), (g_gain_ref, slice(width, 2 * width))):
        out_ref[0:1] = sums0_ref[:, cols]
        out_ref[1:2] = sums1_ref[:, cols]


def finish_half(half, half_refs, outs, bufs, sems):
    me = lax.axis_index("dp") & 31
    core = me & 1
    post, mix, pre, et = bufs
    for layer in range(post.shape[0]):
        for place in range(16):
            block = (me ^ piece_owner(core, half, place, GATHER_KINDS[layer])) >> 1
            piece = half_refs[layer][8 * place : 8 * place + 8]
            post[layer, block] = piece[:, 0:832]
            et[layer, block] = piece[:, 832:896]
            mix[layer, block] = piece[:, 896:1152]
            pre[layer, 0, block] = piece[:, 1152:1408]
            pre[layer, 1, block] = piece[:, 1408:1664]
    side = core ^ half
    post_out, mix_out, pre_out = outs
    pairs = [(post, post_out.at[:, :, side]), (mix, mix_out.at[:, :, side]), (pre, pre_out.at[:, 0:2, :, side])]
    return start_copies(pairs, sems)


def finish_first_kernel(half0_ref, half1_ref, post_out, mix_out, pre_out, et, post, mix, pre, sems):
    wait_all(finish_half(0, (half0_ref, half1_ref), (post_out, mix_out, pre_out), (post, mix, pre, et), sems))


def finish_last_kernel(
    post_in, mix_in, pre_in, other_et, half0_ref, half1_ref, wedge_ref, wpre_ref, post_out, mix_out, pre_out, gb_ref, gedge_ref,
    post, mix, pre, et, term, sems,
):
    del post_in, mix_in, pre_in
    copies = finish_half(1, (half0_ref, half1_ref), (post_out, mix_out, pre_out), (post, mix, pre, et), sems)
    width = wpre_ref.shape[2]
    core = lax.axis_index("dp") & 1
    for layer in range(2):
        mine, other = et[layer], other_et[layer]
        first, second = jnp.where(core == 0, other, mine), jnp.where(core == 0, mine, other)
        both = jnp.concatenate([first[:, None], second[:, None]], axis=1).reshape(width, 64)
        turned = jnp.concatenate([both, both], axis=1).T
        gb_ref[layer : layer + 1] = turned[16:17]
        factor = turned[0:16]
        high, rest = split_two(factor)
        last = (factor - high.astype(F32) - rest.astype(F32)).astype(BF16)
        three = jnp.concatenate([high, rest, last], axis=0)
        grad = mm(jnp.concatenate([wedge_ref[layer]] * 3, axis=0), three, TN)
        term[layer] = grad.reshape(term.shape[1:])
        parts = mm(three, wpre_ref[layer, 2 * width :], NT)
        gedge_ref[layer] = parts[0:16] + parts[16:32] + parts[32:48]
    copies += start_copies([(term, pre_out.at[:, 2])], sems.at[3:4])
    wait_all(copies)


def on_device(
    devices, node_feats, edge_feats, segment_ids, neighbours, nbr_mask, degrees, w_edge, w_pre, b_pre, w_post,
    w_mix, bn_gain, bn_bias, readout_grad,
):
    nodes, width = node_feats.shape
    lanes = nodes + 128
    cols = LEAF_SLOTS * nodes + 1024
    inner = nodes + 64
    nbr_t = neighbours.T
    mask_t = nbr_mask.T
    wpost_t = jnp.swapaxes(w_post, 2, 3)

    def s(shape, dtype=F32):
        return jax.ShapeDtypeStruct(shape, dtype)

    vmem = pl.BlockSpec(memory_space=pltpu.VMEM)
    hbm = pl.BlockSpec(memory_space=pltpu.HBM)

    def call(kernel, args, outs, scratch=(), far=(), free=(), far_out=(), alias={}, cost=0, limit=20):
        args = [pltpu.with_memory_space_constraint(a, pltpu.HBM) if i in far else a for i, a in enumerate(args)]
        return pl.pallas_call(
            kernel,
            in_specs=[hbm if i in far else vmem for i in range(len(args))],
            out_specs=[hbm if i in far_out else vmem for i in range(len(outs))],
            out_shape=[
                o if i in free else (pltpu.HBM if i in far_out else pltpu.VMEM)(o.shape, o.dtype)
                for i, o in enumerate(outs)
            ],
            scratch_shapes=list(scratch),
            input_output_aliases=alias,
            cost_estimate=pl.CostEstimate(flops=int(cost * 1e9), bytes_accessed=0, transcendentals=0) if cost else None,
            compiler_params=pltpu.CompilerParams(vmem_limit_bytes=limit * 1024 * 1024),
        )(*args)

    def like(shapes):
        return [pltpu.VMEM(x.shape, x.dtype) for x in shapes]

    def dma(n):
        return pltpu.SemaphoreType.DMA((n,))

    def exchange(part):
        return lax.all_to_all(part, "dp", 0, 0, tiled=True)

    m_s, s_s, z_s = s((width, cols)), s((4, width, lanes)), s((4 * 320, lanes), BF16)
    b_s = s((inner, cols), BF16)
    row_s, low_s = s((width, nodes)), s((width, nodes), BF16)
    layer_outs = [m_s, s_s, z_s, low_s, row_s, s((devices, 1, 2 * width + 128))]
    fwd_scratch = like([s((width, inner), BF16), s((width, lanes), BF16), s((width, lanes))])
    table_outs = [b_s, s((2, cols)), s((8, lanes)), s((nodes, 128), BF16), s((128, nodes), BF16)]
    first_args = [node_feats, edge_feats, segment_ids, nbr_t, mask_t, degrees, w_edge, w_pre, b_pre, wpost_t, w_mix]
    x0, b, live, rows, g, gt, m0, s0, z0, y0, u0, part = call(
        functools.partial(forward_first_kernel, 0),
        first_args, [low_s] + table_outs + layer_outs,
        fwd_scratch + like([a[0:1] if i in (7, 9, 10) else a for i, a in enumerate(first_args)]) + [dma(11)], range(11),
    )
    tables = [b, live, rows, g, gt]
    recv = exchange(part)
    norm0, h1, x1, m1, s1, z1, y1, u1, part = call(
        functools.partial(forward_next_kernel, 1),
        [recv, u0, x0, bn_gain, bn_bias, w_edge, w_pre, b_pre, wpost_t, w_mix] + tables,
        [s((8, width)), row_s, low_s] + layer_outs,
        fwd_scratch,
    )
    recv = exchange(part)
    sums_out = s((devices, 1, 2 * width))
    norm1, h2, dh2, dv1, part = call(
        functools.partial(last_gate_kernel, 1),
        [recv, u1, h1, bn_gain, bn_bias, rows, readout_grad],
        [s((8, width)), row_s, row_s, row_s, sums_out],
    )
    sum_s = s((1, 2 * width))
    du_s, d_s, dm_s = low_s, s((4 * 192, lanes), BF16), s((width, cols), BF16)
    dcat_s, et_s = s((3 * width, nodes), BF16), s((width, 64))
    back_scratch = like([s_s, s((width, width), BF16)])
    recv = exchange(part)
    grad_cols = 1664
    grad_s, half_s = s((width, grad_cols)), s((width // 2, grad_cols))
    back_scratch = like([du_s, d_s, dcat_s, et_s]) + back_scratch + like([grad_s])
    sums1, dm1, dh1, dv0, part, keep1, send1 = call(
        functools.partial(backward_first_kernel, 1),
        [recv, dv1, dh2, u1, norm1, bn_gain, bn_bias, w_mix, wpost_t, w_pre] + tables + [m1, s1, z1, y1, x1, u0, norm0],
        [sum_s, dm_s, row_s, row_s, sums_out, half_s, half_s],
        back_scratch,
    )

    def swap(value, masks):
        return lax.ppermute(value, "dp", [(i, i ^ masks[i & 1]) for i in range(devices)])

    def together(*values):
        return lax.optimization_barrier(values)

    def relay(value, masks):
        one, two = swap(value, masks[0]), swap(value, masks[1])
        return jnp.concatenate([value, one, two, swap(one, masks[1])], axis=0)

    def spread(value):
        mask = 32
        while mask < devices:
            value = value + swap(value, (mask, mask))
            mask *= 2
        return value

    def scatter_sum(value, masks, size):
        got = [swap(value[size * (i + 1) : size * (i + 2)], m) for i, m in enumerate(masks)]
        return value[0:size] + got[0] + got[1] + got[2]

    def gather(value, masks):
        return jnp.concatenate([value] + [swap(value, m) for m in masks], axis=0)

    got1 = swap(send1, (1, 1))
    recv, got1 = together(exchange(part), got1)
    part1 = scatter_sum(keep1 + got1, larger(SUM_KINDS[1]), 32)
    sums0, dm0, dh0, keep0, send0 = call(
        functools.partial(backward_last_kernel, 0),
        [recv, dv0, dh1, u0, norm0, bn_gain, bn_bias, w_mix, wpost_t, w_pre] + tables + [m0, s0, z0, y0, x0],
        [sum_s, dm_s, row_s, half_s, half_s],
        back_scratch, cost=8,
    )
    edge_grad, readout, node_grad, g_gain, g_bias = call(
        edge_kernel, [dm0, dm1, w_pre, w_edge, gt, h2, rows, dh0, sums0, sums1],
        [s((nodes, width)), s(readout_grad.shape), s((nodes, width)), s(bn_gain.shape), s(bn_bias.shape)],
        [pltpu.VMEM((width, 128), F32)], free=range(5), cost=2,
    )
    send0, part1, edge_grad, readout = together(send0, part1, edge_grad, readout)
    got0 = swap(send0, (1, 1))
    half0 = keep0 + got0
    part0 = scatter_sum(half0, larger(SUM_KINDS[0]), 32)
    part1 = gather(spread(scatter_sum(part1, smaller(SUM_KINDS[1]), 8)), smaller(GATHER_KINDS[1]))
    part1 = relay(together(part1, part0)[0], larger(GATHER_KINDS[1]))
    part0 = spread(scatter_sum(part0, smaller(SUM_KINDS[0]), 8))
    part0 = gather(gather(part0, smaller(GATHER_KINDS[0])), larger(GATHER_KINDS[0]))
    other1 = swap(part1, (1, 1))
    other0 = swap(part0, (1, 1))
    layers, blocks = w_pre.shape[0], width // 16
    finals = [
        s((layers, blocks, 2, 8, 832)), s((layers, blocks, 2, 8, width)), s((layers, 3, blocks, 2, 8, width)),
    ]
    bufs = [s((layers, blocks, 8, 832)), s((layers, blocks, 8, width)), s((layers, 2, blocks, 8, width))]
    ets = s((layers, blocks, 8, 64))
    *finals_in, ets_first = call(
        finish_first_kernel, [part0, part1], finals + [ets], like(bufs) + [dma(3)], far_out=(0, 1, 2), cost=2
    )
    g_post_t, g_mix, g_pre, g_b, g_edge = call(
        finish_last_kernel, [*finals_in, ets_first, other0, other1, w_edge, w_pre], finals + [s(b_pre.shape), s(w_edge.shape)],
        like(bufs + [ets, s((layers, blocks, 2, 8, width))]) + [dma(4)],
        far=(0, 1, 2), far_out=(0, 1, 2), free=(3, 4), alias={0: 0, 1: 1, 2: 2},
    )
    g_post = jnp.swapaxes(g_post_t.reshape(wpost_t.shape), 2, 3)
    g_mix, g_pre = g_mix.reshape(w_mix.shape), g_pre.reshape(w_pre.shape)
    return (
        readout, node_grad, edge_grad, g_edge, g_pre, g_b, g_post, g_mix, g_gain, g_bias,
    )


def solution(mesh):
    split, split2, full = P("dp"), P("dp", None), P()
    in_specs = (split2, split2, split, split2, split2, split) + (full,) * 7 + (split2,)
    out_specs = (split2, split2, split2) + (full,) * 7
    return jax.shard_map(
        functools.partial(on_device, mesh.shape["dp"]),
        mesh=mesh, in_specs=in_specs, out_specs=out_specs, check_vma=False,
    )
```

```python
import functools

import jax
import jax.numpy as jnp
from jax import lax
from jax.experimental import pallas as pl
from jax.experimental.pallas import tpu as pltpu
from jax.sharding import PartitionSpec as P

SUB_MAX = 160
DEGREE_CENTER = 2.0
SPREAD_OFFSET = 0.25
STABILITY_FLOOR = 1e-05

LEAF_SLOTS = 4
HUB_RANK = 16
LOG2E = 1.4426950408889634
LN2 = 0.6931471805599453
ROW_CHUNK = 64
PLANE, LINE = 0, 1
MASKS = ((4, 2, 6), (16, 8, 24))
SUM_KINDS = ((PLANE, LINE), (PLANE, LINE))
GATHER_KINDS = ((PLANE, LINE), (PLANE, PLANE))
F32 = jnp.float32
BF16 = jnp.bfloat16
NN = (((1,), (0,)), ((), ()))
NT = (((1,), (1,)), ((), ()))
TN = (((0,), (0,)), ((), ()))
TT = (((0,), (1,)), ((), ()))


def mm(a, b, dims=NN):
    return lax.dot_general(a, b, dims, preferred_element_type=F32)


def iota(shape, dim):
    return lax.broadcasted_iota(jnp.int32, shape, dim)


def to_cols(*rows):
    pad = [jnp.zeros((8 - len(rows), rows[0].shape[1]), F32)] if len(rows) < 8 else []
    turned = jnp.concatenate(list(rows) + pad, axis=0).T
    return [turned[:, i : i + 1] for i in range(len(rows))]


def to_rows(*cols):
    wide = jnp.concatenate([jnp.broadcast_to(c, (c.shape[0], 128 // len(cols))) for c in cols], axis=1).T
    step = 128 // len(cols)
    return [wide[i * step : i * step + 1] for i in range(len(cols))]


def fold(value, op):
    return op(value, pltpu.roll(value, 64, 1))


def lane_groups(nodes):
    return [(lo, min(lo + 256, nodes)) for lo in range(0, nodes, 256)]


def leaf_col(nodes, slot, node):
    lo, hi = next(g for g in lane_groups(nodes) if g[0] <= node < g[1])
    return LEAF_SLOTS * lo + slot * (hi - lo) + node - lo


def column_groups(nodes):
    leaf_cols = LEAF_SLOTS * nodes
    groups = [(leaf_cols, leaf_cols + 1024, range(nodes // 128, nodes // 128 + 1))]
    for lo, hi in lane_groups(nodes):
        groups.append((LEAF_SLOTS * lo, LEAF_SLOTS * hi, range(lo // 128, hi // 128)))
    return groups


def split_two(value):
    high = value.astype(BF16)
    return high, (value - high.astype(F32)).astype(BF16)


def start_copies(pairs, sems):
    copies = [pltpu.make_async_copy(src, dst, sems.at[i]) for i, (src, dst) in enumerate(pairs)]
    for copy in copies:
        copy.start()
    return copies


def wait_all(copies):
    for copy in copies:
        copy.wait()


def build_tables(ef_ref, seg_ref, nbr_ref, mask_ref, deg_ref, b_ref, live_ref, rows_ref, g_ref, gt_ref):
    nodes = seg_ref.shape[0]
    seg = seg_ref[...].reshape(1, nodes)
    lane_h = iota((1, 128), 1)
    sub_h = iota((128, 1), 0)
    node_row = jnp.zeros((1, 128), jnp.int32)
    node_col = jnp.zeros((128, 1), jnp.int32)
    lane_r, sub_r = lane_h & 15, sub_h & 15
    lane_s, sub_s = (lane_h >> 4) & 3, (sub_h >> 4) & 3
    below = [jnp.sum((seg < s).astype(jnp.int32), axis=1, keepdims=True) for s in range(5)]
    for s in range(4):
        start, size = below[s], below[s + 1] - below[s]
        node_row = jnp.where(lane_s == s, jnp.where(lane_r < size, start + lane_r, -1), node_row)
        node_col = jnp.where(sub_s == s, jnp.where(sub_r < size, start + sub_r, -1), node_col)
    node_col = jnp.where(sub_h < 64, node_col, -1)
    g = (iota((nodes, 128), 0) == node_row).astype(F32).astype(BF16)
    gt = (iota((128, nodes), 1) == node_col).astype(F32).astype(BF16)
    g_ref[...] = g
    gt_ref[...] = gt
    is_hub = jnp.sum(gt.astype(F32), axis=0, keepdims=True)

    nbr = nbr_ref[...]
    mask = (mask_ref[...] > 0).astype(F32)
    nbr_h = (
        mm((nbr >> 3).astype(F32).astype(BF16), g) * 8.0 + mm((nbr & 7).astype(F32).astype(BF16), g)
    ).astype(jnp.int32)
    mask_h = mm(mask.astype(BF16), g)
    valid = (node_row >= 0).astype(F32)
    first = (lane_h < 64).astype(F32)

    def degree_rows(deg):
        log_degree = jnp.log(deg + 1.0)
        return log_degree / DEGREE_CENTER, DEGREE_CENTER / log_degree

    deg = deg_ref[...].reshape(1, nodes).astype(F32)
    deg_h = mm(jnp.broadcast_to(deg, (8, nodes)).astype(BF16), g)[0:1]
    deg_h = jnp.where(valid > 0, deg_h, 1.0)
    amp, att = degree_rows(deg)
    amp_h, att_h = degree_rows(deg_h)
    filled = jnp.sum(mask, axis=0, keepdims=True)
    filled_h = jnp.maximum(jnp.sum(mask_h, axis=0, keepdims=True), 1.0)
    rows_ref[...] = jnp.zeros_like(rows_ref)
    for i, (leaf, hub) in enumerate(
        (
            (amp, amp_h),
            (att, att_h),
            (1.0 / filled, 1.0 / filled_h),
            ((seg < 4).astype(F32), None),
            (1.0 - is_hub, valid * first),
            (is_hub, valid),
            (jnp.sum(mask[1:LEAF_SLOTS], axis=0, keepdims=True) - (LEAF_SLOTS - 2.0), filled_h - 16.0),
            (seg.astype(F32), None),
        )
    ):
        rows_ref[i : i + 1, 0:nodes] = leaf
        if hub is not None:
            rows_ref[i : i + 1, nodes : nodes + 128] = hub

    ef_t = ef_ref[...].T
    nbr16 = nbr.astype(jnp.int16)
    ef_h = mm(ef_t, g).astype(BF16)
    hub_iota = iota((nodes, 128), 0).astype(jnp.int16)
    one_h, none_h = jnp.ones((nodes, 128), BF16), jnp.zeros((nodes, 128), BF16)
    for first_node, end_node in lane_groups(nodes):
        span = slice(first_node, end_node)
        size = end_node - first_node
        node_iota = iota((nodes, size), 0).astype(jnp.int16)
        one16, none16 = jnp.ones((nodes, size), BF16), jnp.zeros((nodes, size), BF16)
        zero16 = jnp.zeros((16, size), BF16)
        for k in range(LEAF_SLOTS):
            lo = leaf_col(nodes, k, first_node)
            cols = slice(lo, lo + size)
            b_ref[0:nodes, cols] = jnp.where(node_iota == nbr16[k : k + 1, span], one16, none16)
            piece = ef_t[16 * k : 16 * k + 16, span]
            for r, part in enumerate((piece, zero16, piece, zero16)):
                b_ref[nodes + 16 * r : nodes + 16 * r + 16, cols] = part
            live_ref[0:1, cols] = mask[k : k + 1, span] * LOG2E
            live_ref[1:2, cols] = mask[k : k + 1, span]
    own_half = (iota((32, 128), 0) < 16) == (iota((32, 128), 1) < 64)
    for j in range(8):
        lo = LEAF_SLOTS * nodes + 128 * j
        index = jnp.where(lane_h < 64, nbr_h[2 * j : 2 * j + 1], nbr_h[2 * j + 1 : 2 * j + 2])
        b_ref[0:nodes, lo : lo + 128] = jnp.where(hub_iota == index.astype(jnp.int16), one_h, none_h)
        piece = jnp.where(own_half, ef_h[32 * j : 32 * j + 32].astype(F32), 0.0).astype(BF16)
        b_ref[nodes : nodes + 32, lo : lo + 128] = piece
        b_ref[nodes + 32 : nodes + 64, lo : lo + 128] = piece
        live = jnp.where(lane_h < 64, mask_h[2 * j : 2 * j + 1], mask_h[2 * j + 1 : 2 * j + 2])
        live_ref[0:1, lo : lo + 128] = live * LOG2E
        live_ref[1:2, lo : lo + 128] = live


def tower_weights(wpost_ref, layer, t):
    w = wpost_ref[layer, t]
    inner = iota((64, 320), 1) >= 64
    zero = jnp.zeros((64, 320), BF16)
    return jnp.concatenate(
        [w[:, 0:320], jnp.where(inner, w[:, 256:576], zero), jnp.where(inner, w[:, 512:832], zero)], axis=0
    )


def forward_layer(
    layer, x_ref, wedge_ref, wpre_ref, bias, wpost_ref, wmix_ref, b_ref, live_ref, rows_ref, g_ref, gt_ref,
    m_refs, s_ref, z_ref, y_ref, u_ref, part_ref, a_ref, ya_ref, own_ref,
):
    width, nodes = x_ref.shape
    leaf_cols = LEAF_SLOTS * nodes
    x = x_ref[...]
    g = g_ref[...]
    own = mm(wpre_ref[layer, 0:width], x, TN) + bias
    own_ref[:, 0:nodes] = own
    a_ref[:, 0:nodes] = mm(wpre_ref[layer, width : 2 * width], x, TN).astype(BF16)
    wedge = wedge_ref[layer]
    both = mm(wpre_ref[layer, 2 * width :], jnp.concatenate([wedge] * 4, axis=0), TT)
    high, rest = split_two(both)
    a_ref[:, nodes : nodes + 64] = jnp.where(iota((width, 64), 1) < 32, high, rest)
    own_high, own_rest = split_two(own)
    own_ref[:, nodes:] = mm(own_high, g) + mm(own_rest, g)
    a = a_ref[...]

    def messages(m_ref, lo, hi):
        m_ref[...] = mm(a, b_ref[:, lo:hi])

    x_h = mm(x, g).astype(BF16)
    for t in range(4):
        z_ref[320 * t : 320 * t + 64, 0:nodes] = x[64 * t : 64 * t + 64]
        z_ref[320 * t : 320 * t + 64, nodes:] = x_h[64 * t : 64 * t + 64]

    def summarize(i, tiles, m_ref, base_col):
        per = 64 // ROW_CHUNK
        zr = (i // per) * 320 + 64 + (i % per) * ROW_CHUNK
        rows = pl.ds(i * ROW_CHUNK, ROW_CHUNK)
        for c in tiles:
            hub = c == nodes // 128
            lanes = slice(128 * c, 128 * c + 128)
            if hub:
                cols = [128 * j for j in range(8)]
                first = m_ref[rows, 0:128]
                first = jnp.where(iota((1, 128), 1) < 64, first, pltpu.roll(first, 64, 1))
            else:
                zero, *cols = [leaf_col(nodes, k, 128 * c) - base_col for k in range(LEAF_SLOTS)]
                first = m_ref[rows, zero : zero + 128]
            offs = []
            for lo in cols:
                d = (m_ref[rows, lo : lo + 128] - first) * live_ref[0:1, base_col + lo : base_col + lo + 128]
                m_ref[rows, lo : lo + 128] = d
                offs.append(d)

            def total(parts, op):
                while len(parts) > 1:
                    parts = [op(*parts[i : i + 2]) if i + 1 < len(parts) else parts[i] for i in range(0, len(parts), 2)]
                return fold(parts[0], op) if hub else parts[0]

            inv, missing = rows_ref[2:3, lanes], rows_ref[6:7, lanes]
            mean = total(offs, jnp.add) * inv
            var = total([d * d for d in offs], jnp.add) * inv - mean * mean
            spread = jnp.maximum(var * (LN2 * LN2), 0.0) + SPREAD_OFFSET
            rstd = lax.rsqrt(spread)
            top = jnp.maximum(total(offs, jnp.maximum), 0.0)
            low = jnp.minimum(total(offs, jnp.minimum), 0.0)
            ups = total([jnp.exp2(d - top) for d in offs], jnp.add) + missing * jnp.exp2(-top)
            downs = total([jnp.exp2(low - d) for d in offs], jnp.add) + missing * jnp.exp2(low)
            smax = top + jnp.log2(ups)
            smin = low - jnp.log2(downs)
            base = own_ref[rows, lanes] + first
            for n, stat in enumerate((mean, smax, smin, rstd)):
                s_ref[n, rows, lanes] = stat
                value = base + LN2 * stat if n < 3 else spread * rstd
                z_ref[pl.ds(zr + 64 * n, ROW_CHUNK), lanes] = value.astype(BF16)

    groups = column_groups(nodes)
    waiting = None
    for group in [*zip(m_refs, groups), None]:
        if group is not None:
            messages(group[0], *group[1][0:2])
        if waiting is not None:
            for i in range(width // ROW_CHUNK):
                summarize(i, waiting[1][2], waiting[0], waiting[1][0])
        waiting = group

    amp, att = rows_ref[0:1], rows_ref[1:2]
    for t in range(4):
        r = mm(tower_weights(wpost_ref, layer, t), z_ref[320 * t : 320 * t + 320])
        ya_ref[64 * t : 64 * t + 64] = (r[0:64] + amp * r[64:128] + att * r[128:192]).astype(BF16)
    spread_out = mm(ya_ref[:, nodes:], gt_ref[...])
    y = jnp.where(rows_ref[5:6, 0:nodes] > 0, spread_out, ya_ref[:, 0:nodes].astype(F32)).astype(BF16)
    y_ref[...] = y
    u = mm(wmix_ref[layer], y, TN)
    u_ref[...] = u
    alive = rows_ref[3:4, 0:nodes]
    count = jnp.sum(alive, axis=1, keepdims=True)
    mean = jnp.sum(alive * u, axis=1, keepdims=True) / count
    off = u - mean
    square = jnp.sum(alive * off * off, axis=1, keepdims=True)
    row = jnp.concatenate(to_rows(mean, square) + [jnp.broadcast_to(count, (1, 128))], axis=1)
    part_ref[...] = jnp.broadcast_to(row[None], part_ref.shape)


def forward_first_kernel(
    layer, nf_hbm, ef_hbm, seg_hbm, nbr_hbm, mask_hbm, deg_hbm, wedge_hbm, wpre_hbm, bpre_hbm, wpost_hbm, wmix_hbm,
    x_ref, b_ref, live_ref, rows_ref, g_ref, gt_ref, ma_ref, mb_ref, mc_ref, md_ref,
    s_ref, z_ref, y_ref, u_ref, part_ref,
    a_ref, ya_ref, own_ref, nf_ref, ef_ref, seg_ref, nbr_ref, mask_ref, deg_ref, wedge_ref, wpre_ref, bpre_ref, wpost_ref, wmix_ref, in_sems,
):
    loads = start_copies(
        [
            (seg_hbm, seg_ref), (nbr_hbm, nbr_ref), (mask_hbm, mask_ref), (deg_hbm, deg_ref), (ef_hbm, ef_ref), (nf_hbm, nf_ref),
            (wpre_hbm.at[0:1], wpre_ref), (wedge_hbm, wedge_ref), (bpre_hbm, bpre_ref),
            (wpost_hbm.at[0:1], wpost_ref), (wmix_hbm.at[0:1], wmix_ref),
        ],
        in_sems,
    )
    wait_all(loads)
    build_tables(ef_ref, seg_ref, nbr_ref, mask_ref, deg_ref, b_ref, live_ref, rows_ref, g_ref, gt_ref)
    x_ref[...] = nf_ref[...].T
    forward_layer(
        layer, x_ref, wedge_ref, wpre_ref, *to_cols(bpre_ref[layer : layer + 1]), wpost_ref, wmix_ref, b_ref,
        live_ref, rows_ref, g_ref, gt_ref, (ma_ref, mb_ref, mc_ref, md_ref), s_ref, z_ref, y_ref, u_ref, part_ref,
        a_ref, ya_ref, own_ref,
    )


def norm_rows(recv_ref):
    w = (recv_ref.shape[2] - 128) // 2
    recv = recv_ref[...]
    means, squares = recv[:, :, 0:w], recv[:, :, w : 2 * w]
    counts = jnp.concatenate([recv[:, :, 2 * w :]] * (w // 128), axis=2)
    total = jnp.sum(counts, axis=0)
    mean = jnp.sum(counts * means, axis=0) / total
    off = means - mean[None]
    var = jnp.sum(squares + counts * off * off, axis=0) / total
    return mean, lax.rsqrt(var + STABILITY_FLOOR), total


def normed(u, norm_ref, gain_ref, bias_ref, layer):
    mean, scale, gain, bias = to_cols(
        norm_ref[0:1], norm_ref[1:2], gain_ref[layer : layer + 1], bias_ref[layer : layer + 1]
    )
    xh = (u - mean) * scale
    return xh, xh * gain + bias


def store_norm(norm_ref, recv_ref):
    mean, scale, total = norm_rows(recv_ref)
    norm_ref[...] = jnp.zeros_like(norm_ref)
    norm_ref[0:1] = mean
    norm_ref[1:2] = scale
    norm_ref[2:3] = total


def forward_next_kernel(
    layer, recv_ref, u0_ref, x0_ref, gain_ref, bias_ref, wedge_ref, wpre_ref, bpre_ref, wpost_ref, wmix_ref,
    b_ref, live_ref, rows_ref, g_ref, gt_ref,
    norm_ref, h_ref, x_ref, ma_ref, mb_ref, mc_ref, md_ref, s_ref, z_ref, y_ref, u_ref, part_ref,
    a_ref, ya_ref, own_ref,
):
    store_norm(norm_ref, recv_ref)
    _, v = normed(u0_ref[...], norm_ref, gain_ref, bias_ref, layer - 1)
    h = x0_ref[...].astype(F32) + v / (1.0 + jnp.exp(-v))
    h_ref[...] = h
    x_ref[...] = h.astype(BF16)
    forward_layer(
        layer, x_ref, wedge_ref, wpre_ref, *to_cols(bpre_ref[layer : layer + 1]), wpost_ref, wmix_ref, b_ref,
        live_ref, rows_ref, g_ref, gt_ref, (ma_ref, mb_ref, mc_ref, md_ref), s_ref, z_ref, y_ref, u_ref, part_ref,
        a_ref, ya_ref, own_ref,
    )


def gate_grad(dh, xh, v, dv_ref, part_ref):
    sig = 1.0 / (1.0 + jnp.exp(-v))
    dv = dh * sig * (1.0 + v * (1.0 - sig))
    dv_ref[...] = dv
    sums = [jnp.sum(p, axis=1, keepdims=True) for p in (dv, dv * xh)]
    row = jnp.concatenate(to_rows(*sums), axis=1)
    part_ref[...] = jnp.broadcast_to(row[None], part_ref.shape)


def last_gate_kernel(
    layer, recv_ref, u_ref, h_ref, gain_ref, bias_ref, rows_ref, rg_ref, norm_ref, h_out_ref, dh_ref, dv_ref, part_ref
):
    store_norm(norm_ref, recv_ref)
    xh, v = normed(u_ref[...], norm_ref, gain_ref, bias_ref, layer)
    nodes = v.shape[1]
    seeds = rg_ref.shape[0]
    sig = 1.0 / (1.0 + jnp.exp(-v))
    h_out_ref[...] = h_ref[...] + v * sig
    dh = jnp.zeros(v.shape, F32)
    cols = to_cols(*[rg_ref[s : s + 1] / SUB_MAX for s in range(seeds)])
    for s, col in enumerate(cols):
        dh = jnp.where(rows_ref[7:8, 0:nodes] == s, col, dh)
    dh_ref[...] = dh
    gate_grad(dh, xh, v, dv_ref, part_ref)


def backward_layer(
    layer, recv_ref, dv_ref, dh_ref, u_ref, norm_ref, gain_ref, bias_ref, wmix_ref, wpost_ref, wpre_ref,
    b_ref, live_ref, rows_ref, g_ref, gt_ref, m_refs, s_ref,
    gb_ref, du_ref, d_ref, dm_refs, dcat_ref, et_ref, ds_ref, bd_ref, beside=(),
):
    width, nodes = dv_ref.shape
    leaf_cols = LEAF_SLOTS * nodes
    sums = jnp.sum(recv_ref[...], axis=0)
    g_bias, g_gain = sums[:, 0:width], sums[:, width:]
    gb_ref[...] = sums
    xh, _ = normed(u_ref[...], norm_ref, gain_ref, bias_ref, layer)
    alive = rows_ref[3:4, 0:nodes]
    scale, part_bias, part_gain = to_cols(
        norm_ref[1:2] * gain_ref[layer : layer + 1], g_bias / norm_ref[2:3], g_gain / norm_ref[2:3]
    )
    du = scale * (dv_ref[...] - alive * (part_bias + xh * part_gain))
    du = du.astype(BF16)
    du_ref[...] = du
    dy = mm(wmix_ref[layer], du)
    dy_low = dy.astype(BF16)
    dcat_ref[2 * width :] = dy_low
    dy_h = mm(dy_low, g_ref[...])
    keep = rows_ref[4:5]
    amp, att = rows_ref[0:1], rows_ref[1:2]
    dy_all = jnp.concatenate([dy_low.astype(F32), dy_h], axis=1) * keep
    bd_ref[...] = jnp.zeros_like(bd_ref)
    for t in range(4):
        part = dy_all[64 * t : 64 * t + 64]
        d_ref[192 * t : 192 * t + 64] = part.astype(BF16)
        d_ref[192 * t + 64 : 192 * t + 128] = (part * amp).astype(BF16)
        d_ref[192 * t + 128 : 192 * t + 192] = (part * att).astype(BF16)
        w = tower_weights(wpost_ref, layer, t)
        dz = mm(w, d_ref[192 * t : 192 * t + 192], TN)
        for n in range(4):
            rows = slice(64 * t, 64 * t + 64)
            block = dz[64 * (n + 1) : 64 * (n + 2)]
            ds_ref[n, rows, 0:nodes] = block[:, 0:nodes]
            ds_ref[n, rows, nodes:] = fold(block[:, nodes:], jnp.add)
        bd_ref[64 * t : 64 * t + 64, 64 * t : 64 * t + 64] = wpost_ref[layer, t][:, 0:64]

    acc = ds_ref[0] + ds_ref[1] + ds_ref[2]
    down = acc[:, 0:nodes] + mm(acc[:, nodes:].astype(BF16), gt_ref[...])
    dcat_ref[0:width] = down.astype(BF16)
    once = jnp.where(iota((1, nodes + 128), 1) < nodes + 64, acc, 0.0)
    bias = jnp.sum(once, axis=1, keepdims=True)

    def spread_back(i, tiles, m_ref, dm_ref, base_col):
        rows = pl.ds(i * ROW_CHUNK, ROW_CHUNK)
        for c in tiles:
            hub = c == nodes // 128
            lanes = slice(128 * c, 128 * c + 128)
            mean, smax, smin, rstd = (s_ref[n, rows, lanes] for n in range(4))
            dmean, dsmax, dsmin, dstd = (ds_ref[n, rows, lanes] for n in range(4))
            inv = rows_ref[2:3, lanes]
            c1 = dstd * inv * rstd * LN2
            c0 = dmean * inv - mean * c1
            if hub:
                cols = [128 * j for j in range(8)]
            else:
                zero, *cols = [leaf_col(nodes, k, 128 * c) - base_col for k in range(LEAF_SLOTS)]
                d = c0 + dsmax * jnp.exp2(-smax) + dsmin * jnp.exp2(smin)
                dm_ref[rows, zero : zero + 128] = d.astype(BF16)
            for lo in cols:
                m = m_ref[rows, lo : lo + 128]
                d = c0 + m * c1 + dsmax * jnp.exp2(m - smax) + dsmin * jnp.exp2(smin - m)
                d = d * live_ref[1:2, base_col + lo : base_col + lo + 128]
                dm_ref[rows, lo : lo + 128] = d.astype(BF16)

    def land(dm_ref, lo, hi):
        return mm(dm_ref[...], b_ref[0 : nodes + 32, lo:hi], NT)

    groups = column_groups(nodes)
    waiting, landed = None, 0.0
    for step, group in enumerate([*zip(m_refs, dm_refs, groups), None]):
        if group is not None:
            for i in range(width // ROW_CHUNK):
                spread_back(i, group[2][2], group[0], group[1], group[2][0])
        if step < len(beside):
            beside[step]()
        if waiting is not None:
            landed = landed + land(waiting[1], *waiting[2][0:2])
        waiting = group

    dcat_ref[width : 2 * width] = landed[:, 0:nodes].astype(BF16)
    factor = landed[:, nodes : nodes + 16] + landed[:, nodes + 16 : nodes + 32]
    et_ref[...] = jnp.concatenate([factor, jnp.broadcast_to(bias, (width, 48))], axis=1)
    weights = jnp.concatenate([wpre_ref[layer, 0:width], wpre_ref[layer, width : 2 * width]], axis=1)
    dh = mm(weights, dcat_ref[0 : 2 * width])
    dh = dh + mm(bd_ref[...], dcat_ref[2 * width :], TN)
    return dh_ref[...] + dh


def piece_owner(core, half, place, kind):
    choice = [((0,) + MASKS[k])[place >> 2] | ((0,) + MASKS[1 - k])[place & 3] for k in kind]
    return half + jnp.where(core == half, *choice)


def larger(kind):
    return list(zip(*[MASKS[k] for k in kind]))


def smaller(kind):
    return list(zip(*[MASKS[1 - k] for k in kind]))


def put_tower_grad(t, d_ref, z_ref, grads_ref):
    r = mm(d_ref[192 * t : 192 * t + 192], z_ref[320 * t : 320 * t + 320], NT)
    rows = slice(64 * t, 64 * t + 64)
    first = iota((64, 256), 1) < 64
    grads_ref[rows, 0:256] = r[0:64, 0:256]
    grads_ref[rows, 256:512] = jnp.where(first, jnp.concatenate([r[0:64, 256:320]] * 4, axis=1), r[64:128, 0:256])
    grads_ref[rows, 512:768] = jnp.where(first, jnp.concatenate([r[64:128, 256:320]] * 4, axis=1), r[128:192, 0:256])
    grads_ref[rows, 768:832] = r[128:192, 256:320]


def put_mix_grad(y_ref, du_ref, grads_ref):
    grads_ref[:, 896:1152] = mm(y_ref[...], du_ref[...], NT)


def put_message_grads(layer, x_ref, dcat_ref, et_ref, grads_ref, keep_ref, send_ref):
    width = x_ref.shape[0]
    grads_ref[:, 832:896] = et_ref[...]
    grads_ref[:, 1152:1664] = mm(x_ref[...], dcat_ref[0 : 2 * width], NT)
    me = lax.axis_index("dp") & 31
    for place in range(16):
        for half, ref in ((0, keep_ref), (1, send_ref)):
            row = pl.multiple_of((me ^ piece_owner(me & 1, half, place, SUM_KINDS[layer])) * 8, 8)
            ref[8 * place : 8 * place + 8] = grads_ref[pl.ds(row, 8)]


def grad_steps(d_ref, z_ref, y_ref, du_ref, grads_ref):
    steps = [functools.partial(put_tower_grad, t, d_ref, z_ref, grads_ref) for t in range(4)]
    return steps + [functools.partial(put_mix_grad, y_ref, du_ref, grads_ref)]


def backward_first_kernel(
    layer, recv_ref, dv_ref, dh_ref, u_ref, norm_ref, gain_ref, bias_ref, wmix_ref, wpost_ref, wpre_ref,
    b_ref, live_ref, rows_ref, g_ref, gt_ref, ma_ref, mb_ref, mc_ref, md_ref, s_ref, z_ref, y_ref, x_ref, u_low_ref, norm_low_ref,
    gb_ref, dma_ref, dmb_ref, dmc_ref, dmd_ref, dh_out_ref, dv_out_ref, part_ref, keep_ref, send_ref,
    du_ref, d_ref, dcat_ref, et_ref, ds_ref, bd_ref, grads_ref,
):
    dh = backward_layer(
        layer, recv_ref, dv_ref, dh_ref, u_ref, norm_ref, gain_ref, bias_ref, wmix_ref, wpost_ref, wpre_ref,
        b_ref, live_ref, rows_ref, g_ref, gt_ref, (ma_ref, mb_ref, mc_ref, md_ref), s_ref,
        gb_ref, du_ref, d_ref, (dma_ref, dmb_ref, dmc_ref, dmd_ref), dcat_ref, et_ref, ds_ref, bd_ref,
        grad_steps(d_ref, z_ref, y_ref, du_ref, grads_ref),
    )
    put_message_grads(layer, x_ref, dcat_ref, et_ref, grads_ref, keep_ref, send_ref)
    dh_out_ref[...] = dh
    xh, v = normed(u_low_ref[...], norm_low_ref, gain_ref, bias_ref, layer - 1)
    gate_grad(dh, xh, v, dv_out_ref, part_ref)


def backward_last_kernel(
    layer, recv_ref, dv_ref, dh_ref, u_ref, norm_ref, gain_ref, bias_ref, wmix_ref, wpost_ref, wpre_ref,
    b_ref, live_ref, rows_ref, g_ref, gt_ref, ma_ref, mb_ref, mc_ref, md_ref, s_ref, z_ref, y_ref, x_ref,
    gb_ref, dma_ref, dmb_ref, dmc_ref, dmd_ref, dh_out_ref, keep_ref, send_ref,
    du_ref, d_ref, dcat_ref, et_ref, ds_ref, bd_ref, grads_ref,
):
    dh = backward_layer(
        layer, recv_ref, dv_ref, dh_ref, u_ref, norm_ref, gain_ref, bias_ref, wmix_ref, wpost_ref, wpre_ref,
        b_ref, live_ref, rows_ref, g_ref, gt_ref, (ma_ref, mb_ref, mc_ref, md_ref), s_ref,
        gb_ref, du_ref, d_ref, (dma_ref, dmb_ref, dmc_ref, dmd_ref), dcat_ref, et_ref, ds_ref, bd_ref,
        grad_steps(d_ref, z_ref, y_ref, du_ref, grads_ref),
    )
    put_message_grads(layer, x_ref, dcat_ref, et_ref, grads_ref, keep_ref, send_ref)
    dh_out_ref[...] = dh


def edge_kernel(
    a0_ref, b0_ref, c0_ref, d0_ref, a1_ref, b1_ref, c1_ref, d1_ref, wpre_ref, wedge_ref, gt_ref, h_ref, rows_ref, dh_ref, sums0_ref, sums1_ref,
    out_ref, readout_ref, node_ref, g_gain_ref, g_bias_ref, acc_ref,
):
    width = a0_ref.shape[0]
    nodes = gt_ref.shape[1]
    leaf_cols = LEAF_SLOTS * nodes
    w0, w1 = (mm(wedge_ref[layer], wpre_ref[layer, 2 * width :]).astype(BF16) for layer in range(2))
    pairs = ((a0_ref, a1_ref), (b0_ref, b1_ref), (c0_ref, c1_ref), (d0_ref, d1_ref))
    hub, *groups = [mm(w0, lower[...]) + mm(w1, upper[...]) for lower, upper in pairs]
    total = jnp.concatenate(groups, axis=1)
    for j in range(8):
        acc_ref[32 * j : 32 * j + 16] = hub[:, 128 * j : 128 * j + 128]
        acc_ref[32 * j + 16 : 32 * j + 32] = pltpu.roll(hub[:, 128 * j : 128 * j + 128], 64, 1)
    high, rest = split_two(acc_ref[...])
    gt = gt_ref[...]
    spread_out = mm(high, gt) + mm(rest, gt)
    leaf = []
    for k in range(LEAF_SLOTS):
        parts = []
        for lo, hi in lane_groups(nodes):
            col = leaf_col(nodes, k, lo)
            parts.append(total[:, col : col + hi - lo])
        leaf.append(jnp.concatenate(parts, axis=1))
    leaf = jnp.concatenate(leaf, axis=0)
    out = jnp.concatenate([spread_out[0:64] + leaf, spread_out[64:]], axis=0)
    out_ref[...] = out.T
    belong = (iota((8, nodes), 0).astype(F32) == rows_ref[7:8, 0:nodes]).astype(F32)
    total = lax.dot_general(belong, h_ref[...], NT, precision=lax.Precision.HIGHEST, preferred_element_type=F32)
    readout_ref[...] = total[0 : readout_ref.shape[0]] / SUB_MAX
    node_ref[...] = dh_ref[...].T
    for out_ref, cols in ((g_bias_ref, slice(0, width)), (g_gain_ref, slice(width, 2 * width))):
        out_ref[0:1] = sums0_ref[:, cols]
        out_ref[1:2] = sums1_ref[:, cols]


def finish_half(half, half_refs, outs, bufs, sems):
    me = lax.axis_index("dp") & 31
    core = me & 1
    post, mix, pre, et = bufs
    for layer in range(post.shape[0]):
        for place in range(16):
            block = (me ^ piece_owner(core, half, place, GATHER_KINDS[layer])) >> 1
            piece = half_refs[layer][8 * place : 8 * place + 8]
            post[layer, block] = piece[:, 0:832]
            et[layer, block] = piece[:, 832:896]
            mix[layer, block] = piece[:, 896:1152]
            pre[layer, 0, block] = piece[:, 1152:1408]
            pre[layer, 1, block] = piece[:, 1408:1664]
    side = core ^ half
    post_out, mix_out, pre_out = outs
    pairs = [(post, post_out.at[:, :, side]), (mix, mix_out.at[:, :, side]), (pre, pre_out.at[:, 0:2, :, side])]
    return start_copies(pairs, sems)


def finish_first_kernel(half0_ref, half1_ref, post_out, mix_out, pre_out, et, post, mix, pre, sems):
    wait_all(finish_half(0, (half0_ref, half1_ref), (post_out, mix_out, pre_out), (post, mix, pre, et), sems))


def finish_last_kernel(
    post_in, mix_in, pre_in, other_et, half0_ref, half1_ref, wedge_ref, wpre_ref,
    post_out, mix_out, pre_out, gb_out, gedge_out, post, mix, pre, et, term, gb_ref, gedge_ref, sems,
):
    del post_in, mix_in, pre_in
    copies = finish_half(1, (half0_ref, half1_ref), (post_out, mix_out, pre_out), (post, mix, pre, et), sems)
    width = wpre_ref.shape[2]
    core = lax.axis_index("dp") & 1
    for layer in range(2):
        mine, other = et[layer], other_et[layer]
        first, second = jnp.where(core == 0, other, mine), jnp.where(core == 0, mine, other)
        both = jnp.concatenate([first[:, None], second[:, None]], axis=1).reshape(width, 64)
        turned = jnp.concatenate([both, both], axis=1).T
        gb_ref[layer : layer + 1] = turned[16:17]
        factor = turned[0:16]
        high, rest = split_two(factor)
        last = (factor - high.astype(F32) - rest.astype(F32)).astype(BF16)
        three = jnp.concatenate([high, rest, last], axis=0)
        grad = mm(jnp.concatenate([wedge_ref[layer]] * 3, axis=0), three, TN)
        term[layer] = grad.reshape(term.shape[1:])
        parts = mm(three, wpre_ref[layer, 2 * width :], NT)
        gedge_ref[layer] = parts[0:16] + parts[16:32] + parts[32:48]
    pairs = [(term, pre_out.at[:, 2]), (gedge_ref, gedge_out), (gb_ref, gb_out)]
    copies += start_copies(pairs, sems.at[3:6])
    wait_all(copies)


def on_device(
    devices, node_feats, edge_feats, segment_ids, neighbours, nbr_mask, degrees, w_edge, w_pre, b_pre, w_post,
    w_mix, bn_gain, bn_bias, readout_grad,
):
    nodes, width = node_feats.shape
    lanes = nodes + 128
    cols = LEAF_SLOTS * nodes + 1024
    inner = nodes + 64
    nbr_t = neighbours.T
    mask_t = nbr_mask.T
    wpost_t = jnp.swapaxes(w_post, 2, 3)

    def s(shape, dtype=F32):
        return jax.ShapeDtypeStruct(shape, dtype)

    vmem = pl.BlockSpec(memory_space=pltpu.VMEM)
    hbm = pl.BlockSpec(memory_space=pltpu.HBM)

    def call(kernel, args, outs, scratch=(), far=(), free=(), far_out=(), alias={}, cost=0, limit=20):
        args = [pltpu.with_memory_space_constraint(a, pltpu.HBM) if i in far else a for i, a in enumerate(args)]
        return pl.pallas_call(
            kernel,
            in_specs=[hbm if i in far else vmem for i in range(len(args))],
            out_specs=[hbm if i in far_out else vmem for i in range(len(outs))],
            out_shape=[
                o if i in free else (pltpu.HBM if i in far_out else pltpu.VMEM)(o.shape, o.dtype)
                for i, o in enumerate(outs)
            ],
            scratch_shapes=list(scratch),
            input_output_aliases=alias,
            cost_estimate=pl.CostEstimate(flops=int(cost * 1e9), bytes_accessed=0, transcendentals=0) if cost else None,
            compiler_params=pltpu.CompilerParams(vmem_limit_bytes=limit * 1024 * 1024),
        )(*args)

    def like(shapes):
        return [pltpu.VMEM(x.shape, x.dtype) for x in shapes]

    def dma(n):
        return pltpu.SemaphoreType.DMA((n,))

    def exchange(part):
        return lax.all_to_all(part, "dp", 0, 0, tiled=True)

    spans = [hi - lo for lo, hi, _ in column_groups(nodes)]
    m_s, s_s, z_s = [s((width, n)) for n in spans], s((4, width, lanes)), s((4 * 320, lanes), BF16)
    b_s = s((inner, cols), BF16)
    row_s, low_s = s((width, nodes)), s((width, nodes), BF16)
    layer_outs = [*m_s, s_s, z_s, low_s, row_s, s((devices, 1, 2 * width + 128))]
    fwd_scratch = like([s((width, inner), BF16), s((width, lanes), BF16), s((width, lanes))])
    table_outs = [b_s, s((2, cols)), s((8, lanes)), s((nodes, 128), BF16), s((128, nodes), BF16)]
    first_args = [node_feats, edge_feats, segment_ids, nbr_t, mask_t, degrees, w_edge, w_pre, b_pre, wpost_t, w_mix]
    x0, b, live, rows, g, gt, *m0, s0, z0, y0, u0, part = call(
        functools.partial(forward_first_kernel, 0),
        first_args, [low_s] + table_outs + layer_outs,
        fwd_scratch + like([a[0:1] if i in (7, 9, 10) else a for i, a in enumerate(first_args)]) + [dma(11)], range(11),
    )
    tables = [b, live, rows, g, gt]
    recv = exchange(part)
    norm0, h1, x1, *m1, s1, z1, y1, u1, part = call(
        functools.partial(forward_next_kernel, 1),
        [recv, u0, x0, bn_gain, bn_bias, w_edge, w_pre, b_pre, wpost_t, w_mix] + tables,
        [s((8, width)), row_s, low_s] + layer_outs,
        fwd_scratch,
    )
    recv = exchange(part)
    sums_out = s((devices, 1, 2 * width))
    norm1, h2, dh2, dv1, part = call(
        functools.partial(last_gate_kernel, 1),
        [recv, u1, h1, bn_gain, bn_bias, rows, readout_grad],
        [s((8, width)), row_s, row_s, row_s, sums_out],
    )
    sum_s = s((1, 2 * width))
    du_s, d_s, dm_s = low_s, s((4 * 192, lanes), BF16), [s((width, n), BF16) for n in spans]
    dcat_s, et_s = s((3 * width, nodes), BF16), s((width, 64))
    back_scratch = like([s_s, s((width, width), BF16)])
    recv = exchange(part)
    grad_cols = 1664
    grad_s, half_s = s((width, grad_cols)), s((width // 2, grad_cols))
    back_scratch = like([du_s, d_s, dcat_s, et_s]) + back_scratch + like([grad_s])
    sums1, *dm1, dh1, dv0, part, keep1, send1 = call(
        functools.partial(backward_first_kernel, 1),
        [recv, dv1, dh2, u1, norm1, bn_gain, bn_bias, w_mix, wpost_t, w_pre] + tables + [*m1, s1, z1, y1, x1, u0, norm0],
        [sum_s, *dm_s, row_s, row_s, sums_out, half_s, half_s],
        back_scratch,
    )

    def swap(value, masks):
        return lax.ppermute(value, "dp", [(i, i ^ masks[i & 1]) for i in range(devices)])

    def together(*values):
        return lax.optimization_barrier(values)

    def relay(value, masks):
        one, two = swap(value, masks[0]), swap(value, masks[1])
        return jnp.concatenate([value, one, two, swap(one, masks[1])], axis=0)

    def spread(value):
        mask = 32
        while mask < devices:
            value = value + swap(value, (mask, mask))
            mask *= 2
        return value

    def scatter_sum(value, masks, size):
        got = [swap(value[size * (i + 1) : size * (i + 2)], m) for i, m in enumerate(masks)]
        return value[0:size] + got[0] + got[1] + got[2]

    def gather(value, masks):
        return jnp.concatenate([value] + [swap(value, m) for m in masks], axis=0)

    got1 = swap(send1, (1, 1))
    recv, got1 = together(exchange(part), got1)
    part1 = scatter_sum(keep1 + got1, larger(SUM_KINDS[1]), 32)
    sums0, *dm0, dh0, keep0, send0 = call(
        functools.partial(backward_last_kernel, 0),
        [recv, dv0, dh1, u0, norm0, bn_gain, bn_bias, w_mix, wpost_t, w_pre] + tables + [*m0, s0, z0, y0, x0],
        [sum_s, *dm_s, row_s, half_s, half_s],
        back_scratch, cost=8,
    )
    edge_grad, readout, node_grad, g_gain, g_bias = call(
        edge_kernel, [*dm0, *dm1, w_pre, w_edge, gt, h2, rows, dh0, sums0, sums1],
        [s((nodes, width)), s(readout_grad.shape), s((nodes, width)), s(bn_gain.shape), s(bn_bias.shape)],
        [pltpu.VMEM((width, 128), F32)], free=range(5), cost=2,
    )
    send0, part1, edge_grad, readout = together(send0, part1, edge_grad, readout)
    got0 = swap(send0, (1, 1))
    half0 = keep0 + got0
    outer = [swap(half0[32 * (i + 1) : 32 * (i + 2)], m) for i, m in enumerate(larger(SUM_KINDS[0]))]
    part0 = half0[0:32] + outer[0] + outer[1] + outer[2]
    part1 = spread(scatter_sum(part1, smaller(SUM_KINDS[1]), 8))
    part1 = gather(together(part1, outer[0])[0], smaller(GATHER_KINDS[1]))
    part1 = relay(together(part1, part0)[0], larger(GATHER_KINDS[1]))
    part0 = spread(scatter_sum(part0, smaller(SUM_KINDS[0]), 8))
    part0 = gather(gather(part0, smaller(GATHER_KINDS[0])), larger(GATHER_KINDS[0]))
    other1 = swap(part1, (1, 1))
    other0 = swap(part0, (1, 1))
    layers, blocks = w_pre.shape[0], width // 16
    finals = [
        s((layers, blocks, 2, 8, 832)), s((layers, blocks, 2, 8, width)), s((layers, 3, blocks, 2, 8, width)),
    ]
    bufs = [s((layers, blocks, 8, 832)), s((layers, blocks, 8, width)), s((layers, 2, blocks, 8, width))]
    ets = s((layers, blocks, 8, 64))
    *finals_in, ets_first = call(
        finish_first_kernel, [part0, part1], finals + [ets], like(bufs) + [dma(3)], far_out=(0, 1, 2), cost=2
    )
    g_post_t, g_mix, g_pre, g_b, g_edge = call(
        finish_last_kernel, [*finals_in, ets_first, other0, other1, w_edge, w_pre], finals + [s(b_pre.shape), s(w_edge.shape)],
        like(bufs + [ets, s((layers, blocks, 2, 8, width)), s(b_pre.shape), s(w_edge.shape)]) + [dma(6)],
        far=(0, 1, 2), far_out=range(5), alias={0: 0, 1: 1, 2: 2},
    )
    g_post = jnp.swapaxes(g_post_t.reshape(wpost_t.shape), 2, 3)
    g_mix, g_pre = g_mix.reshape(w_mix.shape), g_pre.reshape(w_pre.shape)
    return (
        readout, node_grad, edge_grad, g_edge, g_pre, g_b, g_post, g_mix, g_gain, g_bias,
    )


def solution(mesh):
    split, split2, full = P("dp"), P("dp", None), P()
    in_specs = (split2, split2, split, split2, split2, split) + (full,) * 7 + (split2,)
    out_specs = (split2, split2, split2) + (full,) * 7
    return jax.shard_map(
        functools.partial(on_device, mesh.shape["dp"]),
        mesh=mesh, in_specs=in_specs, out_specs=out_specs, check_vma=False,
    )
```

```python
import functools

import jax
import jax.numpy as jnp
from jax import lax
from jax.experimental import pallas as pl
from jax.experimental.pallas import tpu as pltpu
from jax.sharding import PartitionSpec as P

SUB_MAX = 160
DEGREE_CENTER = 2.0
SPREAD_OFFSET = 0.25
STABILITY_FLOOR = 1e-05

LEAF_SLOTS = 4
HUB_RANK = 16
LOG2E = 1.4426950408889634
LN2 = 0.6931471805599453
ROW_CHUNK = 64
PLANE, LINE = 0, 1
MASKS = ((4, 2, 6), (16, 8, 24))
SUM_KINDS = ((PLANE, LINE), (PLANE, LINE))
GATHER_KINDS = ((PLANE, LINE), (PLANE, PLANE))
F32 = jnp.float32
BF16 = jnp.bfloat16
NN = (((1,), (0,)), ((), ()))
NT = (((1,), (1,)), ((), ()))
TN = (((0,), (0,)), ((), ()))
TT = (((0,), (1,)), ((), ()))


def mm(a, b, dims=NN):
    return lax.dot_general(a, b, dims, preferred_element_type=F32)


def iota(shape, dim):
    return lax.broadcasted_iota(jnp.int32, shape, dim)


def to_cols(*rows):
    pad = [jnp.zeros((8 - len(rows), rows[0].shape[1]), F32)] if len(rows) < 8 else []
    turned = jnp.concatenate(list(rows) + pad, axis=0).T
    return [turned[:, i : i + 1] for i in range(len(rows))]


def to_rows(*cols):
    wide = jnp.concatenate([jnp.broadcast_to(c, (c.shape[0], 128 // len(cols))) for c in cols], axis=1).T
    step = 128 // len(cols)
    return [wide[i * step : i * step + 1] for i in range(len(cols))]


def fold(value, op):
    return op(value, pltpu.roll(value, 64, 1))


def lane_groups(nodes):
    return [(lo, min(lo + 256, nodes)) for lo in range(0, nodes, 256)]


def leaf_col(nodes, slot, node):
    lo, hi = next(g for g in lane_groups(nodes) if g[0] <= node < g[1])
    return LEAF_SLOTS * lo + slot * (hi - lo) + node - lo


def column_groups(nodes):
    leaf_cols = LEAF_SLOTS * nodes
    groups = [(leaf_cols, leaf_cols + 1024, range(nodes // 128, nodes // 128 + 1))]
    for lo, hi in lane_groups(nodes):
        groups.append((LEAF_SLOTS * lo, LEAF_SLOTS * hi, range(lo // 128, hi // 128)))
    return groups


def split_two(value):
    high = value.astype(BF16)
    return high, (value - high.astype(F32)).astype(BF16)


def start_copies(pairs, sems):
    copies = [pltpu.make_async_copy(src, dst, sems.at[i]) for i, (src, dst) in enumerate(pairs)]
    for copy in copies:
        copy.start()
    return copies


def wait_all(copies):
    for copy in copies:
        copy.wait()


def build_tables(ef_ref, seg_ref, nbr_ref, mask_ref, deg_ref, b_ref, live_ref, rows_ref, g_ref, gt_ref):
    nodes = seg_ref.shape[0]
    seg = seg_ref[...].reshape(1, nodes)
    lane_h = iota((1, 128), 1)
    sub_h = iota((128, 1), 0)
    node_row = jnp.zeros((1, 128), jnp.int32)
    node_col = jnp.zeros((128, 1), jnp.int32)
    lane_r, sub_r = lane_h & 15, sub_h & 15
    lane_s, sub_s = (lane_h >> 4) & 3, (sub_h >> 4) & 3
    below = [jnp.sum((seg < s).astype(jnp.int32), axis=1, keepdims=True) for s in range(5)]
    for s in range(4):
        start, size = below[s], below[s + 1] - below[s]
        node_row = jnp.where(lane_s == s, jnp.where(lane_r < size, start + lane_r, -1), node_row)
        node_col = jnp.where(sub_s == s, jnp.where(sub_r < size, start + sub_r, -1), node_col)
    node_col = jnp.where(sub_h < 64, node_col, -1)
    g = (iota((nodes, 128), 0) == node_row).astype(F32).astype(BF16)
    gt = (iota((128, nodes), 1) == node_col).astype(F32).astype(BF16)
    g_ref[...] = g
    gt_ref[...] = gt
    is_hub = jnp.sum(gt.astype(F32), axis=0, keepdims=True)

    nbr = nbr_ref[...]
    mask = (mask_ref[...] > 0).astype(F32)
    nbr_h = (
        mm((nbr >> 3).astype(F32).astype(BF16), g) * 8.0 + mm((nbr & 7).astype(F32).astype(BF16), g)
    ).astype(jnp.int32)
    mask_h = mm(mask.astype(BF16), g)
    valid = (node_row >= 0).astype(F32)
    first = (lane_h < 64).astype(F32)

    def degree_rows(deg):
        log_degree = jnp.log(deg + 1.0)
        return log_degree / DEGREE_CENTER, DEGREE_CENTER / log_degree

    deg = deg_ref[...].reshape(1, nodes).astype(F32)
    deg_h = mm(jnp.broadcast_to(deg, (8, nodes)).astype(BF16), g)[0:1]
    deg_h = jnp.where(valid > 0, deg_h, 1.0)
    amp, att = degree_rows(deg)
    amp_h, att_h = degree_rows(deg_h)
    filled = jnp.sum(mask, axis=0, keepdims=True)
    filled_h = jnp.maximum(jnp.sum(mask_h, axis=0, keepdims=True), 1.0)
    rows_ref[...] = jnp.zeros_like(rows_ref)
    for i, (leaf, hub) in enumerate(
        (
            (amp, amp_h),
            (att, att_h),
            (1.0 / filled, 1.0 / filled_h),
            ((seg < 4).astype(F32), None),
            (1.0 - is_hub, valid * first),
            (is_hub, valid),
            (jnp.sum(mask[1:LEAF_SLOTS], axis=0, keepdims=True) - (LEAF_SLOTS - 2.0), filled_h - 16.0),
            (seg.astype(F32), None),
        )
    ):
        rows_ref[i : i + 1, 0:nodes] = leaf
        if hub is not None:
            rows_ref[i : i + 1, nodes : nodes + 128] = hub

    ef_t = ef_ref[...].T
    nbr16 = nbr.astype(jnp.int16)
    ef_h = mm(ef_t, g).astype(BF16)
    hub_iota = iota((nodes, 128), 0).astype(jnp.int16)
    one_h, none_h = jnp.ones((nodes, 128), BF16), jnp.zeros((nodes, 128), BF16)
    for first_node, end_node in lane_groups(nodes):
        span = slice(first_node, end_node)
        size = end_node - first_node
        node_iota = iota((nodes, size), 0).astype(jnp.int16)
        one16, none16 = jnp.ones((nodes, size), BF16), jnp.zeros((nodes, size), BF16)
        zero16 = jnp.zeros((16, size), BF16)
        for k in range(LEAF_SLOTS):
            lo = leaf_col(nodes, k, first_node)
            cols = slice(lo, lo + size)
            b_ref[0:nodes, cols] = jnp.where(node_iota == nbr16[k : k + 1, span], one16, none16)
            piece = ef_t[16 * k : 16 * k + 16, span]
            for r, part in enumerate((piece, zero16, piece, zero16)):
                b_ref[nodes + 16 * r : nodes + 16 * r + 16, cols] = part
            live_ref[0:1, cols] = mask[k : k + 1, span] * LOG2E
            live_ref[1:2, cols] = mask[k : k + 1, span]
    own_half = (iota((32, 128), 0) < 16) == (iota((32, 128), 1) < 64)
    for j in range(8):
        lo = LEAF_SLOTS * nodes + 128 * j
        index = jnp.where(lane_h < 64, nbr_h[2 * j : 2 * j + 1], nbr_h[2 * j + 1 : 2 * j + 2])
        b_ref[0:nodes, lo : lo + 128] = jnp.where(hub_iota == index.astype(jnp.int16), one_h, none_h)
        piece = jnp.where(own_half, ef_h[32 * j : 32 * j + 32].astype(F32), 0.0).astype(BF16)
        b_ref[nodes : nodes + 32, lo : lo + 128] = piece
        b_ref[nodes + 32 : nodes + 64, lo : lo + 128] = piece
        live = jnp.where(lane_h < 64, mask_h[2 * j : 2 * j + 1], mask_h[2 * j + 1 : 2 * j + 2])
        live_ref[0:1, lo : lo + 128] = live * LOG2E
        live_ref[1:2, lo : lo + 128] = live


def tower_weights(wpost_ref, layer, t):
    w = wpost_ref[layer, t]
    inner = iota((64, 320), 1) >= 64
    zero = jnp.zeros((64, 320), BF16)
    return jnp.concatenate(
        [w[:, 0:320], jnp.where(inner, w[:, 256:576], zero), jnp.where(inner, w[:, 512:832], zero)], axis=0
    )


def forward_layer(
    layer, x_ref, wedge_ref, wpre_ref, bias, wpost_ref, wmix_ref, b_ref, live_ref, rows_ref, g_ref, gt_ref,
    m_refs, s_ref, z_ref, y_ref, u_ref, part_ref, a_ref, ya_ref, own_ref,
):
    width, nodes = x_ref.shape
    leaf_cols = LEAF_SLOTS * nodes
    x = x_ref[...]
    g = g_ref[...]
    own = mm(wpre_ref[layer, 0:width], x, TN) + bias
    own_ref[:, 0:nodes] = own
    a_ref[:, 0:nodes] = mm(wpre_ref[layer, width : 2 * width], x, TN).astype(BF16)
    wedge = wedge_ref[layer]
    both = mm(wpre_ref[layer, 2 * width :], jnp.concatenate([wedge] * 4, axis=0), TT)
    high, rest = split_two(both)
    a_ref[:, nodes : nodes + 64] = jnp.where(iota((width, 64), 1) < 32, high, rest)
    own_high, own_rest = split_two(own)
    own_ref[:, nodes:] = mm(own_high, g) + mm(own_rest, g)
    a = a_ref[...]

    def messages(m_ref, lo, hi):
        m_ref[...] = mm(a, b_ref[:, lo:hi])

    x_h = mm(x, g).astype(BF16)
    for t in range(4):
        z_ref[320 * t : 320 * t + 64, 0:nodes] = x[64 * t : 64 * t + 64]
        z_ref[320 * t : 320 * t + 64, nodes:] = x_h[64 * t : 64 * t + 64]

    def summarize(i, tiles, m_ref, base_col):
        per = 64 // ROW_CHUNK
        zr = (i // per) * 320 + 64 + (i % per) * ROW_CHUNK
        rows = pl.ds(i * ROW_CHUNK, ROW_CHUNK)
        for c in tiles:
            hub = c == nodes // 128
            lanes = slice(128 * c, 128 * c + 128)
            if hub:
                cols = [128 * j for j in range(8)]
                first = m_ref[rows, 0:128]
                first = jnp.where(iota((1, 128), 1) < 64, first, pltpu.roll(first, 64, 1))
            else:
                zero, *cols = [leaf_col(nodes, k, 128 * c) - base_col for k in range(LEAF_SLOTS)]
                first = m_ref[rows, zero : zero + 128]
            offs = []
            for lo in cols:
                d = (m_ref[rows, lo : lo + 128] - first) * live_ref[0:1, base_col + lo : base_col + lo + 128]
                m_ref[rows, lo : lo + 128] = d
                offs.append(d)

            def total(parts, op):
                while len(parts) > 1:
                    parts = [op(*parts[i : i + 2]) if i + 1 < len(parts) else parts[i] for i in range(0, len(parts), 2)]
                return fold(parts[0], op) if hub else parts[0]

            inv, missing = rows_ref[2:3, lanes], rows_ref[6:7, lanes]
            mean = total(offs, jnp.add) * inv
            var = total([d * d for d in offs], jnp.add) * inv - mean * mean
            spread = jnp.maximum(var * (LN2 * LN2), 0.0) + SPREAD_OFFSET
            rstd = lax.rsqrt(spread)
            top = jnp.maximum(total(offs, jnp.maximum), 0.0)
            low = jnp.minimum(total(offs, jnp.minimum), 0.0)
            ups = total([jnp.exp2(d - top) for d in offs], jnp.add) + missing * jnp.exp2(-top)
            downs = total([jnp.exp2(low - d) for d in offs], jnp.add) + missing * jnp.exp2(low)
            smax = top + jnp.log2(ups)
            smin = low - jnp.log2(downs)
            base = own_ref[rows, lanes] + first
            for n, stat in enumerate((mean, smax, smin, rstd)):
                s_ref[n, rows, lanes] = stat
                value = base + LN2 * stat if n < 3 else spread * rstd
                z_ref[pl.ds(zr + 64 * n, ROW_CHUNK), lanes] = value.astype(BF16)

    groups = column_groups(nodes)
    waiting = None
    for group in [*zip(m_refs, groups), None]:
        if group is not None:
            messages(group[0], *group[1][0:2])
        if waiting is not None:
            for i in range(width // ROW_CHUNK):
                summarize(i, waiting[1][2], waiting[0], waiting[1][0])
        waiting = group

    amp, att = rows_ref[0:1], rows_ref[1:2]
    for t in range(4):
        r = mm(tower_weights(wpost_ref, layer, t), z_ref[320 * t : 320 * t + 320])
        ya_ref[64 * t : 64 * t + 64] = (r[0:64] + amp * r[64:128] + att * r[128:192]).astype(BF16)
    spread_out = mm(ya_ref[:, nodes:], gt_ref[...])
    y = jnp.where(rows_ref[5:6, 0:nodes] > 0, spread_out, ya_ref[:, 0:nodes].astype(F32)).astype(BF16)
    y_ref[...] = y
    u = mm(wmix_ref[layer], y, TN)
    u_ref[...] = u
    alive = rows_ref[3:4, 0:nodes]
    count = jnp.sum(alive, axis=1, keepdims=True)
    mean = jnp.sum(alive * u, axis=1, keepdims=True) / count
    off = u - mean
    square = jnp.sum(alive * off * off, axis=1, keepdims=True)
    row = jnp.concatenate(to_rows(mean, square) + [jnp.broadcast_to(count, (1, 128))], axis=1)
    part_ref[...] = jnp.broadcast_to(row[None], part_ref.shape)


def forward_first_kernel(
    layer, nf_hbm, ef_hbm, seg_hbm, nbr_hbm, mask_hbm, deg_hbm, wedge_hbm, wpre_hbm, bpre_hbm, wpost_hbm, wmix_hbm,
    x_ref, b_ref, live_ref, rows_ref, g_ref, gt_ref, ma_ref, mb_ref, mc_ref, md_ref,
    s_ref, z_ref, y_ref, u_ref, part_ref,
    a_ref, ya_ref, own_ref, nf_ref, ef_ref, seg_ref, nbr_ref, mask_ref, deg_ref, wedge_ref, wpre_ref, bpre_ref, wpost_ref, wmix_ref, in_sems,
):
    loads = start_copies(
        [
            (seg_hbm, seg_ref), (nbr_hbm, nbr_ref), (mask_hbm, mask_ref), (deg_hbm, deg_ref), (ef_hbm, ef_ref), (nf_hbm, nf_ref),
            (wpre_hbm.at[0:1], wpre_ref), (wedge_hbm, wedge_ref), (bpre_hbm, bpre_ref),
            (wpost_hbm.at[0:1], wpost_ref), (wmix_hbm.at[0:1], wmix_ref),
        ],
        in_sems,
    )
    wait_all(loads)
    build_tables(ef_ref, seg_ref, nbr_ref, mask_ref, deg_ref, b_ref, live_ref, rows_ref, g_ref, gt_ref)
    x_ref[...] = nf_ref[...].T
    forward_layer(
        layer, x_ref, wedge_ref, wpre_ref, *to_cols(bpre_ref[layer : layer + 1]), wpost_ref, wmix_ref, b_ref,
        live_ref, rows_ref, g_ref, gt_ref, (ma_ref, mb_ref, mc_ref, md_ref), s_ref, z_ref, y_ref, u_ref, part_ref,
        a_ref, ya_ref, own_ref,
    )


def norm_rows(recv_ref):
    w = (recv_ref.shape[2] - 128) // 2
    recv = recv_ref[...]
    means, squares = recv[:, :, 0:w], recv[:, :, w : 2 * w]
    counts = jnp.concatenate([recv[:, :, 2 * w :]] * (w // 128), axis=2)
    total = jnp.sum(counts, axis=0)
    mean = jnp.sum(counts * means, axis=0) / total
    off = means - mean[None]
    var = jnp.sum(squares + counts * off * off, axis=0) / total
    return mean, lax.rsqrt(var + STABILITY_FLOOR), total


def normed(u, norm_ref, gain_ref, bias_ref, layer):
    mean, scale, gain, bias = to_cols(
        norm_ref[0:1], norm_ref[1:2], gain_ref[layer : layer + 1], bias_ref[layer : layer + 1]
    )
    xh = (u - mean) * scale
    return xh, xh * gain + bias


def store_norm(norm_ref, recv_ref):
    mean, scale, total = norm_rows(recv_ref)
    norm_ref[...] = jnp.zeros_like(norm_ref)
    norm_ref[0:1] = mean
    norm_ref[1:2] = scale
    norm_ref[2:3] = total


def forward_next_kernel(
    layer, recv_ref, u0_ref, x0_ref, gain_ref, bias_ref, wedge_ref, wpre_ref, bpre_ref, wpost_ref, wmix_ref,
    b_ref, live_ref, rows_ref, g_ref, gt_ref,
    norm_ref, h_ref, x_ref, ma_ref, mb_ref, mc_ref, md_ref, s_ref, z_ref, y_ref, u_ref, part_ref,
    a_ref, ya_ref, own_ref,
):
    store_norm(norm_ref, recv_ref)
    _, v = normed(u0_ref[...], norm_ref, gain_ref, bias_ref, layer - 1)
    h = x0_ref[...].astype(F32) + v / (1.0 + jnp.exp(-v))
    h_ref[...] = h
    x_ref[...] = h.astype(BF16)
    forward_layer(
        layer, x_ref, wedge_ref, wpre_ref, *to_cols(bpre_ref[layer : layer + 1]), wpost_ref, wmix_ref, b_ref,
        live_ref, rows_ref, g_ref, gt_ref, (ma_ref, mb_ref, mc_ref, md_ref), s_ref, z_ref, y_ref, u_ref, part_ref,
        a_ref, ya_ref, own_ref,
    )


def gate_grad(dh, xh, v, dv_ref, part_ref):
    sig = 1.0 / (1.0 + jnp.exp(-v))
    dv = dh * sig * (1.0 + v * (1.0 - sig))
    dv_ref[...] = dv
    sums = [jnp.sum(p, axis=1, keepdims=True) for p in (dv, dv * xh)]
    row = jnp.concatenate(to_rows(*sums), axis=1)
    part_ref[...] = jnp.broadcast_to(row[None], part_ref.shape)


def last_gate_kernel(
    layer, recv_ref, u_ref, h_ref, gain_ref, bias_ref, rows_ref, rg_ref, norm_ref, h_out_ref, dh_ref, dv_ref, part_ref
):
    store_norm(norm_ref, recv_ref)
    xh, v = normed(u_ref[...], norm_ref, gain_ref, bias_ref, layer)
    nodes = v.shape[1]
    seeds = rg_ref.shape[0]
    sig = 1.0 / (1.0 + jnp.exp(-v))
    h_out_ref[...] = h_ref[...] + v * sig
    dh = jnp.zeros(v.shape, F32)
    cols = to_cols(*[rg_ref[s : s + 1] / SUB_MAX for s in range(seeds)])
    for s, col in enumerate(cols):
        dh = jnp.where(rows_ref[7:8, 0:nodes] == s, col, dh)
    dh_ref[...] = dh
    gate_grad(dh, xh, v, dv_ref, part_ref)


def backward_layer(
    layer, recv_ref, dv_ref, dh_ref, u_ref, norm_ref, gain_ref, bias_ref, wmix_ref, wpost_ref, wpre_ref,
    b_ref, live_ref, rows_ref, g_ref, gt_ref, m_refs, s_ref,
    gb_ref, du_ref, d_ref, dm_refs, dcat_ref, et_ref, ds_ref, bd_ref, beside=(),
):
    width, nodes = dv_ref.shape
    leaf_cols = LEAF_SLOTS * nodes
    sums = jnp.sum(recv_ref[...], axis=0)
    g_bias, g_gain = sums[:, 0:width], sums[:, width:]
    gb_ref[...] = sums
    xh, _ = normed(u_ref[...], norm_ref, gain_ref, bias_ref, layer)
    alive = rows_ref[3:4, 0:nodes]
    scale, part_bias, part_gain = to_cols(
        norm_ref[1:2] * gain_ref[layer : layer + 1], g_bias / norm_ref[2:3], g_gain / norm_ref[2:3]
    )
    du = scale * (dv_ref[...] - alive * (part_bias + xh * part_gain))
    du = du.astype(BF16)
    du_ref[...] = du
    dy = mm(wmix_ref[layer], du)
    dy_low = dy.astype(BF16)
    dcat_ref[2 * width :] = dy_low
    dy_h = mm(dy_low, g_ref[...])
    keep = rows_ref[4:5]
    amp, att = rows_ref[0:1], rows_ref[1:2]
    dy_all = jnp.concatenate([dy_low.astype(F32), dy_h], axis=1) * keep
    bd_ref[...] = jnp.zeros_like(bd_ref)
    for t in range(4):
        part = dy_all[64 * t : 64 * t + 64]
        d_ref[192 * t : 192 * t + 64] = part.astype(BF16)
        d_ref[192 * t + 64 : 192 * t + 128] = (part * amp).astype(BF16)
        d_ref[192 * t + 128 : 192 * t + 192] = (part * att).astype(BF16)
        w = tower_weights(wpost_ref, layer, t)
        dz = mm(w, d_ref[192 * t : 192 * t + 192], TN)
        for n in range(4):
            rows = slice(64 * t, 64 * t + 64)
            block = dz[64 * (n + 1) : 64 * (n + 2)]
            ds_ref[n, rows, 0:nodes] = block[:, 0:nodes]
            ds_ref[n, rows, nodes:] = fold(block[:, nodes:], jnp.add)
        bd_ref[64 * t : 64 * t + 64, 64 * t : 64 * t + 64] = wpost_ref[layer, t][:, 0:64]

    acc = ds_ref[0] + ds_ref[1] + ds_ref[2]
    down = acc[:, 0:nodes] + mm(acc[:, nodes:].astype(BF16), gt_ref[...])
    dcat_ref[0:width] = down.astype(BF16)
    once = jnp.where(iota((1, nodes + 128), 1) < nodes + 64, acc, 0.0)
    bias = jnp.sum(once, axis=1, keepdims=True)

    def spread_back(i, tiles, m_ref, dm_ref, base_col):
        rows = pl.ds(i * ROW_CHUNK, ROW_CHUNK)
        for c in tiles:
            hub = c == nodes // 128
            lanes = slice(128 * c, 128 * c + 128)
            mean, smax, smin, rstd = (s_ref[n, rows, lanes] for n in range(4))
            dmean, dsmax, dsmin, dstd = (ds_ref[n, rows, lanes] for n in range(4))
            inv = rows_ref[2:3, lanes]
            c1 = dstd * inv * rstd * LN2
            c0 = dmean * inv - mean * c1
            if hub:
                cols = [128 * j for j in range(8)]
            else:
                zero, *cols = [leaf_col(nodes, k, 128 * c) - base_col for k in range(LEAF_SLOTS)]
                d = c0 + dsmax * jnp.exp2(-smax) + dsmin * jnp.exp2(smin)
                dm_ref[rows, zero : zero + 128] = d.astype(BF16)
            for lo in cols:
                m = m_ref[rows, lo : lo + 128]
                d = c0 + m * c1 + dsmax * jnp.exp2(m - smax) + dsmin * jnp.exp2(smin - m)
                d = d * live_ref[1:2, base_col + lo : base_col + lo + 128]
                dm_ref[rows, lo : lo + 128] = d.astype(BF16)

    def land(dm_ref, lo, hi):
        return mm(dm_ref[...], b_ref[0 : nodes + 32, lo:hi], NT)

    groups = column_groups(nodes)
    waiting, landed = None, 0.0
    for step, group in enumerate([*zip(m_refs, dm_refs, groups), None]):
        if group is not None:
            for i in range(width // ROW_CHUNK):
                spread_back(i, group[2][2], group[0], group[1], group[2][0])
        if step < len(beside):
            beside[step]()
        if waiting is not None:
            landed = landed + land(waiting[1], *waiting[2][0:2])
        waiting = group

    dcat_ref[width : 2 * width] = landed[:, 0:nodes].astype(BF16)
    factor = landed[:, nodes : nodes + 16] + landed[:, nodes + 16 : nodes + 32]
    et_ref[...] = jnp.concatenate([factor, jnp.broadcast_to(bias, (width, 48))], axis=1)
    weights = jnp.concatenate([wpre_ref[layer, 0:width], wpre_ref[layer, width : 2 * width]], axis=1)
    dh = mm(weights, dcat_ref[0 : 2 * width])
    dh = dh + mm(bd_ref[...], dcat_ref[2 * width :], TN)
    return dh_ref[...] + dh


def piece_owner(core, half, place, kind):
    choice = [((0,) + MASKS[k])[place >> 2] | ((0,) + MASKS[1 - k])[place & 3] for k in kind]
    return half + jnp.where(core == half, *choice)


def larger(kind):
    return list(zip(*[MASKS[k] for k in kind]))


def smaller(kind):
    return list(zip(*[MASKS[1 - k] for k in kind]))


def put_tower_grad(t, d_ref, z_ref, grads_ref):
    r = mm(d_ref[192 * t : 192 * t + 192], z_ref[320 * t : 320 * t + 320], NT)
    rows = slice(64 * t, 64 * t + 64)
    first = iota((64, 256), 1) < 64
    grads_ref[rows, 0:256] = r[0:64, 0:256]
    grads_ref[rows, 256:512] = jnp.where(first, jnp.concatenate([r[0:64, 256:320]] * 4, axis=1), r[64:128, 0:256])
    grads_ref[rows, 512:768] = jnp.where(first, jnp.concatenate([r[64:128, 256:320]] * 4, axis=1), r[128:192, 0:256])
    grads_ref[rows, 768:832] = r[128:192, 256:320]


def put_mix_grad(y_ref, du_ref, grads_ref):
    grads_ref[:, 896:1152] = mm(y_ref[...], du_ref[...], NT)


def put_message_grads(layer, x_ref, dcat_ref, et_ref, grads_ref, keep_ref, send_ref):
    width = x_ref.shape[0]
    grads_ref[:, 832:896] = et_ref[...]
    grads_ref[:, 1152:1664] = mm(x_ref[...], dcat_ref[0 : 2 * width], NT)
    me = lax.axis_index("dp") & 31
    for place in range(16):
        for half, ref in ((0, keep_ref), (1, send_ref)):
            row = pl.multiple_of((me ^ piece_owner(me & 1, half, place, SUM_KINDS[layer])) * 8, 8)
            ref[8 * place : 8 * place + 8] = grads_ref[pl.ds(row, 8)]


def grad_steps(d_ref, z_ref, y_ref, du_ref, grads_ref):
    steps = [functools.partial(put_tower_grad, t, d_ref, z_ref, grads_ref) for t in range(4)]
    return steps + [functools.partial(put_mix_grad, y_ref, du_ref, grads_ref)]


def backward_first_kernel(
    layer, recv_ref, dv_ref, dh_ref, u_ref, norm_ref, gain_ref, bias_ref, wmix_ref, wpost_ref, wpre_ref,
    b_ref, live_ref, rows_ref, g_ref, gt_ref, ma_ref, mb_ref, mc_ref, md_ref, s_ref, z_ref, y_ref, x_ref, u_low_ref, norm_low_ref,
    gb_ref, dma_ref, dmb_ref, dmc_ref, dmd_ref, dh_out_ref, dv_out_ref, part_ref, keep_ref, send_ref,
    du_ref, d_ref, dcat_ref, et_ref, ds_ref, bd_ref, grads_ref,
):
    dh = backward_layer(
        layer, recv_ref, dv_ref, dh_ref, u_ref, norm_ref, gain_ref, bias_ref, wmix_ref, wpost_ref, wpre_ref,
        b_ref, live_ref, rows_ref, g_ref, gt_ref, (ma_ref, mb_ref, mc_ref, md_ref), s_ref,
        gb_ref, du_ref, d_ref, (dma_ref, dmb_ref, dmc_ref, dmd_ref), dcat_ref, et_ref, ds_ref, bd_ref,
        grad_steps(d_ref, z_ref, y_ref, du_ref, grads_ref),
    )
    put_message_grads(layer, x_ref, dcat_ref, et_ref, grads_ref, keep_ref, send_ref)
    dh_out_ref[...] = dh
    xh, v = normed(u_low_ref[...], norm_low_ref, gain_ref, bias_ref, layer - 1)
    gate_grad(dh, xh, v, dv_out_ref, part_ref)


def backward_last_kernel(
    layer, recv_ref, dv_ref, dh_ref, u_ref, norm_ref, gain_ref, bias_ref, wmix_ref, wpost_ref, wpre_ref,
    b_ref, live_ref, rows_ref, g_ref, gt_ref, ma_ref, mb_ref, mc_ref, md_ref, s_ref, z_ref, y_ref, x_ref,
    gb_ref, dma_ref, dmb_ref, dmc_ref, dmd_ref, dh_out_ref, keep_ref, send_ref,
    du_ref, d_ref, dcat_ref, et_ref, ds_ref, bd_ref, grads_ref,
):
    dh = backward_layer(
        layer, recv_ref, dv_ref, dh_ref, u_ref, norm_ref, gain_ref, bias_ref, wmix_ref, wpost_ref, wpre_ref,
        b_ref, live_ref, rows_ref, g_ref, gt_ref, (ma_ref, mb_ref, mc_ref, md_ref), s_ref,
        gb_ref, du_ref, d_ref, (dma_ref, dmb_ref, dmc_ref, dmd_ref), dcat_ref, et_ref, ds_ref, bd_ref,
        grad_steps(d_ref, z_ref, y_ref, du_ref, grads_ref),
    )
    put_message_grads(layer, x_ref, dcat_ref, et_ref, grads_ref, keep_ref, send_ref)
    dh_out_ref[...] = dh


def edge_kernel(
    a0_ref, b0_ref, c0_ref, d0_ref, a1_ref, b1_ref, c1_ref, d1_ref, wpre_ref, wedge_ref, gt_ref, h_ref, rows_ref, dh_ref, sums0_ref, sums1_ref,
    out_ref, readout_ref, node_ref, g_gain_ref, g_bias_ref, acc_ref,
):
    width = a0_ref.shape[0]
    nodes = gt_ref.shape[1]
    leaf_cols = LEAF_SLOTS * nodes
    w0, w1 = (mm(wedge_ref[layer], wpre_ref[layer, 2 * width :]).astype(BF16) for layer in range(2))
    pairs = ((a0_ref, a1_ref), (b0_ref, b1_ref), (c0_ref, c1_ref), (d0_ref, d1_ref))
    hub, *groups = [mm(w0, lower[...]) + mm(w1, upper[...]) for lower, upper in pairs]
    total = jnp.concatenate(groups, axis=1)
    for j in range(8):
        acc_ref[32 * j : 32 * j + 16] = hub[:, 128 * j : 128 * j + 128]
        acc_ref[32 * j + 16 : 32 * j + 32] = pltpu.roll(hub[:, 128 * j : 128 * j + 128], 64, 1)
    high, rest = split_two(acc_ref[...])
    gt = gt_ref[...]
    spread_out = mm(high, gt) + mm(rest, gt)
    leaf = []
    for k in range(LEAF_SLOTS):
        parts = []
        for lo, hi in lane_groups(nodes):
            col = leaf_col(nodes, k, lo)
            parts.append(total[:, col : col + hi - lo])
        leaf.append(jnp.concatenate(parts, axis=1))
    leaf = jnp.concatenate(leaf, axis=0)
    out = jnp.concatenate([spread_out[0:64] + leaf, spread_out[64:]], axis=0)
    out_ref[...] = out.T
    belong = (iota((8, nodes), 0).astype(F32) == rows_ref[7:8, 0:nodes]).astype(F32)
    total = lax.dot_general(belong, h_ref[...], NT, precision=lax.Precision.HIGHEST, preferred_element_type=F32)
    readout_ref[...] = total[0 : readout_ref.shape[0]] / SUB_MAX
    node_ref[...] = dh_ref[...].T
    for out_ref, cols in ((g_bias_ref, slice(0, width)), (g_gain_ref, slice(width, 2 * width))):
        out_ref[0:1] = sums0_ref[:, cols]
        out_ref[1:2] = sums1_ref[:, cols]


def finish_half(half, half_refs, outs, bufs, sems):
    me = lax.axis_index("dp") & 31
    core = me & 1
    post, mix, pre, et = bufs
    for layer in range(post.shape[0]):
        for place in range(16):
            block = (me ^ piece_owner(core, half, place, GATHER_KINDS[layer])) >> 1
            piece = half_refs[layer][8 * place : 8 * place + 8]
            post[layer, block] = piece[:, 0:832]
            et[layer, block] = piece[:, 832:896]
            mix[layer, block] = piece[:, 896:1152]
            pre[layer, 0, block] = piece[:, 1152:1408]
            pre[layer, 1, block] = piece[:, 1408:1664]
    side = core ^ half
    post_out, mix_out, pre_out = outs
    pairs = [(post, post_out.at[:, :, side]), (mix, mix_out.at[:, :, side]), (pre, pre_out.at[:, 0:2, :, side])]
    return start_copies(pairs, sems)


def finish_first_kernel(half0_ref, half1_ref, post_out, mix_out, pre_out, et, post, mix, pre, sems):
    wait_all(finish_half(0, (half0_ref, half1_ref), (post_out, mix_out, pre_out), (post, mix, pre, et), sems))


def finish_last_kernel(
    post_in, mix_in, pre_in, other_et, half0_ref, half1_ref, wedge_ref, wpre_ref,
    post_out, mix_out, pre_out, gb_out, gedge_out, post, mix, pre, et, term, gb_ref, gedge_ref, sems,
):
    del post_in, mix_in, pre_in
    copies = finish_half(1, (half0_ref, half1_ref), (post_out, mix_out, pre_out), (post, mix, pre, et), sems)
    width = wpre_ref.shape[2]
    core = lax.axis_index("dp") & 1
    for layer in range(2):
        mine, other = et[layer], other_et[layer]
        first, second = jnp.where(core == 0, other, mine), jnp.where(core == 0, mine, other)
        both = jnp.concatenate([first[:, None], second[:, None]], axis=1).reshape(width, 64)
        turned = jnp.concatenate([both, both], axis=1).T
        gb_ref[layer : layer + 1] = turned[16:17]
        factor = turned[0:16]
        high, rest = split_two(factor)
        last = (factor - high.astype(F32) - rest.astype(F32)).astype(BF16)
        three = jnp.concatenate([high, rest, last], axis=0)
        grad = mm(jnp.concatenate([wedge_ref[layer]] * 3, axis=0), three, TN)
        term[layer] = grad.reshape(term.shape[1:])
        parts = mm(three, wpre_ref[layer, 2 * width :], NT)
        gedge_ref[layer] = parts[0:16] + parts[16:32] + parts[32:48]
    pairs = [(term, pre_out.at[:, 2]), (gedge_ref, gedge_out), (gb_ref, gb_out)]
    copies += start_copies(pairs, sems.at[3:6])
    wait_all(copies)


def on_device(
    devices, node_feats, edge_feats, segment_ids, neighbours, nbr_mask, degrees, w_edge, w_pre, b_pre, w_post,
    w_mix, bn_gain, bn_bias, readout_grad,
):
    nodes, width = node_feats.shape
    lanes = nodes + 128
    cols = LEAF_SLOTS * nodes + 1024
    inner = nodes + 64
    nbr_t = neighbours.T
    mask_t = nbr_mask.T
    wpost_t = jnp.swapaxes(w_post, 2, 3)

    def s(shape, dtype=F32):
        return jax.ShapeDtypeStruct(shape, dtype)

    vmem = pl.BlockSpec(memory_space=pltpu.VMEM)
    hbm = pl.BlockSpec(memory_space=pltpu.HBM)

    def call(kernel, args, outs, scratch=(), far=(), free=(), far_out=(), alias={}, cost=0, limit=20):
        args = [pltpu.with_memory_space_constraint(a, pltpu.HBM) if i in far else a for i, a in enumerate(args)]
        return pl.pallas_call(
            kernel,
            in_specs=[hbm if i in far else vmem for i in range(len(args))],
            out_specs=[hbm if i in far_out else vmem for i in range(len(outs))],
            out_shape=[
                o if i in free else (pltpu.HBM if i in far_out else pltpu.VMEM)(o.shape, o.dtype)
                for i, o in enumerate(outs)
            ],
            scratch_shapes=list(scratch),
            input_output_aliases=alias,
            cost_estimate=pl.CostEstimate(flops=int(cost * 1e9), bytes_accessed=0, transcendentals=0) if cost else None,
            compiler_params=pltpu.CompilerParams(vmem_limit_bytes=limit * 1024 * 1024),
        )(*args)

    def like(shapes):
        return [pltpu.VMEM(x.shape, x.dtype) for x in shapes]

    def dma(n):
        return pltpu.SemaphoreType.DMA((n,))

    def exchange(part):
        return lax.all_to_all(part, "dp", 0, 0, tiled=True)

    spans = [hi - lo for lo, hi, _ in column_groups(nodes)]
    m_s, s_s, z_s = [s((width, n)) for n in spans], s((4, width, lanes)), s((4 * 320, lanes), BF16)
    b_s = s((inner, cols), BF16)
    row_s, low_s = s((width, nodes)), s((width, nodes), BF16)
    layer_outs = [*m_s, s_s, z_s, low_s, row_s, s((devices, 1, 2 * width + 128))]
    fwd_scratch = like([s((width, inner), BF16), s((width, lanes), BF16), s((width, lanes))])
    table_outs = [b_s, s((2, cols)), s((8, lanes)), s((nodes, 128), BF16), s((128, nodes), BF16)]
    first_args = [node_feats, edge_feats, segment_ids, nbr_t, mask_t, degrees, w_edge, w_pre, b_pre, wpost_t, w_mix]
    x0, b, live, rows, g, gt, *m0, s0, z0, y0, u0, part = call(
        functools.partial(forward_first_kernel, 0),
        first_args, [low_s] + table_outs + layer_outs,
        fwd_scratch + like([a[0:1] if i in (7, 9, 10) else a for i, a in enumerate(first_args)]) + [dma(11)], range(11),
    )
    tables = [b, live, rows, g, gt]
    recv = exchange(part)
    norm0, h1, x1, *m1, s1, z1, y1, u1, part = call(
        functools.partial(forward_next_kernel, 1),
        [recv, u0, x0, bn_gain, bn_bias, w_edge, w_pre, b_pre, wpost_t, w_mix] + tables,
        [s((8, width)), row_s, low_s] + layer_outs,
        fwd_scratch,
    )
    recv = exchange(part)
    sums_out = s((devices, 1, 2 * width))
    norm1, h2, dh2, dv1, part = call(
        functools.partial(last_gate_kernel, 1),
        [recv, u1, h1, bn_gain, bn_bias, rows, readout_grad],
        [s((8, width)), row_s, row_s, row_s, sums_out],
    )
    sum_s = s((1, 2 * width))
    du_s, d_s, dm_s = low_s, s((4 * 192, lanes), BF16), [s((width, n), BF16) for n in spans]
    dcat_s, et_s = s((3 * width, nodes), BF16), s((width, 64))
    back_scratch = like([s_s, s((width, width), BF16)])
    recv = exchange(part)
    grad_cols = 1664
    grad_s, half_s = s((width, grad_cols)), s((width // 2, grad_cols))
    back_scratch = like([du_s, d_s, dcat_s, et_s]) + back_scratch + like([grad_s])
    sums1, *dm1, dh1, dv0, part, keep1, send1 = call(
        functools.partial(backward_first_kernel, 1),
        [recv, dv1, dh2, u1, norm1, bn_gain, bn_bias, w_mix, wpost_t, w_pre] + tables + [*m1, s1, z1, y1, x1, u0, norm0],
        [sum_s, *dm_s, row_s, row_s, sums_out, half_s, half_s],
        back_scratch,
    )

    def swap(value, masks):
        return lax.ppermute(value, "dp", [(i, i ^ masks[i & 1]) for i in range(devices)])

    def together(*values):
        return lax.optimization_barrier(values)

    def relay(value, masks):
        one, two = swap(value, masks[0]), swap(value, masks[1])
        return jnp.concatenate([value, one, two, swap(two, masks[0])], axis=0)

    def spread(value):
        mask = 32
        while mask < devices:
            value = value + swap(value, (mask, mask))
            mask *= 2
        return value

    def scatter_sum(value, masks, size):
        got = [swap(value[size * (i + 1) : size * (i + 2)], m) for i, m in enumerate(masks)]
        return value[0:size] + got[0] + got[1] + got[2]

    def gather(value, masks):
        return jnp.concatenate([value] + [swap(value, m) for m in masks], axis=0)

    got1 = swap(send1, (1, 1))
    recv, got1 = together(exchange(part), got1)
    part1 = scatter_sum(keep1 + got1, larger(SUM_KINDS[1]), 32)
    sums0, *dm0, dh0, keep0, send0 = call(
        functools.partial(backward_last_kernel, 0),
        [recv, dv0, dh1, u0, norm0, bn_gain, bn_bias, w_mix, wpost_t, w_pre] + tables + [*m0, s0, z0, y0, x0],
        [sum_s, *dm_s, row_s, half_s, half_s],
        back_scratch, cost=8,
    )
    edge_grad, readout, node_grad, g_gain, g_bias = call(
        edge_kernel, [*dm0, *dm1, w_pre, w_edge, gt, h2, rows, dh0, sums0, sums1],
        [s((nodes, width)), s(readout_grad.shape), s((nodes, width)), s(bn_gain.shape), s(bn_bias.shape)],
        [pltpu.VMEM((width, 128), F32)], free=range(5), cost=2,
    )
    send0, part1, edge_grad, readout = together(send0, part1, edge_grad, readout)
    got0 = swap(send0, (1, 1))
    half0 = keep0 + got0
    outer = [swap(half0[32 * (i + 1) : 32 * (i + 2)], m) for i, m in enumerate(larger(SUM_KINDS[0]))]
    part0 = half0[0:32] + outer[0] + outer[1] + outer[2]
    part1 = spread(scatter_sum(part1, smaller(SUM_KINDS[1]), 8))
    part1 = gather(part1, smaller(GATHER_KINDS[1]))
    part1 = relay(together(part1, part0)[0], larger(GATHER_KINDS[1]))
    part0 = spread(scatter_sum(part0, smaller(SUM_KINDS[0]), 8))
    part0 = gather(gather(part0, smaller(GATHER_KINDS[0])), larger(GATHER_KINDS[0]))
    other1 = swap(part1, (1, 1))
    other0 = swap(part0, (1, 1))
    layers, blocks = w_pre.shape[0], width // 16
    finals = [
        s((layers, blocks, 2, 8, 832)), s((layers, blocks, 2, 8, width)), s((layers, 3, blocks, 2, 8, width)),
    ]
    bufs = [s((layers, blocks, 8, 832)), s((layers, blocks, 8, width)), s((layers, 2, blocks, 8, width))]
    ets = s((layers, blocks, 8, 64))
    *finals_in, ets_first = call(
        finish_first_kernel, [part0, part1], finals + [ets], like(bufs) + [dma(3)], far_out=(0, 1, 2), cost=2
    )
    g_post_t, g_mix, g_pre, g_b, g_edge = call(
        finish_last_kernel, [*finals_in, ets_first, other0, other1, w_edge, w_pre], finals + [s(b_pre.shape), s(w_edge.shape)],
        like(bufs + [ets, s((layers, blocks, 2, 8, width)), s(b_pre.shape), s(w_edge.shape)]) + [dma(6)],
        far=(0, 1, 2), far_out=range(5), alias={0: 0, 1: 1, 2: 2},
    )
    g_post = jnp.swapaxes(g_post_t.reshape(wpost_t.shape), 2, 3)
    g_mix, g_pre = g_mix.reshape(w_mix.shape), g_pre.reshape(w_pre.shape)
    return (
        readout, node_grad, edge_grad, g_edge, g_pre, g_b, g_post, g_mix, g_gain, g_bias,
    )


def solution(mesh):
    split, split2, full = P("dp"), P("dp", None), P()
    in_specs = (split2, split2, split, split2, split2, split) + (full,) * 7 + (split2,)
    out_specs = (split2, split2, split2) + (full,) * 7
    return jax.shard_map(
        functools.partial(on_device, mesh.shape["dp"]),
        mesh=mesh, in_specs=in_specs, out_specs=out_specs, check_vma=False,
    )
```

```python
import functools

import jax
import jax.numpy as jnp
from jax import lax
from jax.experimental import pallas as pl
from jax.experimental.pallas import tpu as pltpu
from jax.sharding import PartitionSpec as P

SUB_MAX = 160
DEGREE_CENTER = 2.0
SPREAD_OFFSET = 0.25
STABILITY_FLOOR = 1e-05

LEAF_SLOTS = 4
HUB_RANK = 16
LOG2E = 1.4426950408889634
LN2 = 0.6931471805599453
ROW_CHUNK = 64
PLANE, LINE = 0, 1
MASKS = ((4, 2, 6), (16, 8, 24))
SUM_KINDS = ((PLANE, LINE), (PLANE, LINE))
GATHER_KINDS = ((PLANE, LINE), (PLANE, PLANE))
F32 = jnp.float32
BF16 = jnp.bfloat16
NN = (((1,), (0,)), ((), ()))
NT = (((1,), (1,)), ((), ()))
TN = (((0,), (0,)), ((), ()))
TT = (((0,), (1,)), ((), ()))


def mm(a, b, dims=NN):
    return lax.dot_general(a, b, dims, preferred_element_type=F32)


def iota(shape, dim):
    return lax.broadcasted_iota(jnp.int32, shape, dim)


def to_cols(*rows):
    pad = [jnp.zeros((8 - len(rows), rows[0].shape[1]), F32)] if len(rows) < 8 else []
    turned = jnp.concatenate(list(rows) + pad, axis=0).T
    return [turned[:, i : i + 1] for i in range(len(rows))]


def to_rows(*cols):
    wide = jnp.concatenate([jnp.broadcast_to(c, (c.shape[0], 128 // len(cols))) for c in cols], axis=1).T
    step = 128 // len(cols)
    return [wide[i * step : i * step + 1] for i in range(len(cols))]


def fold(value, op):
    return op(value, pltpu.roll(value, 64, 1))


def lane_groups(nodes):
    return [(lo, min(lo + 256, nodes)) for lo in range(0, nodes, 256)]


def leaf_col(nodes, slot, node):
    lo, hi = next(g for g in lane_groups(nodes) if g[0] <= node < g[1])
    return LEAF_SLOTS * lo + slot * (hi - lo) + node - lo


def column_groups(nodes):
    leaf_cols = LEAF_SLOTS * nodes
    groups = [(leaf_cols, leaf_cols + 1024, range(nodes // 128, nodes // 128 + 1))]
    for lo, hi in lane_groups(nodes):
        groups.append((LEAF_SLOTS * lo, LEAF_SLOTS * hi, range(lo // 128, hi // 128)))
    return groups


def split_two(value):
    high = value.astype(BF16)
    return high, (value - high.astype(F32)).astype(BF16)


def start_copies(pairs, sems):
    copies = [pltpu.make_async_copy(src, dst, sems.at[i]) for i, (src, dst) in enumerate(pairs)]
    for copy in copies:
        copy.start()
    return copies


def wait_all(copies):
    for copy in copies:
        copy.wait()


def build_tables(ef_ref, seg_ref, nbr_ref, mask_ref, deg_ref, b_ref, live_ref, rows_ref, g_ref, gt_ref):
    nodes = seg_ref.shape[0]
    seg = seg_ref[...].reshape(1, nodes)
    lane_h = iota((1, 128), 1)
    sub_h = iota((128, 1), 0)
    node_row = jnp.zeros((1, 128), jnp.int32)
    node_col = jnp.zeros((128, 1), jnp.int32)
    lane_r, sub_r = lane_h & 15, sub_h & 15
    lane_s, sub_s = (lane_h >> 4) & 3, (sub_h >> 4) & 3
    below = [jnp.sum((seg < s).astype(jnp.int32), axis=1, keepdims=True) for s in range(5)]
    for s in range(4):
        start, size = below[s], below[s + 1] - below[s]
        node_row = jnp.where(lane_s == s, jnp.where(lane_r < size, start + lane_r, -1), node_row)
        node_col = jnp.where(sub_s == s, jnp.where(sub_r < size, start + sub_r, -1), node_col)
    node_col = jnp.where(sub_h < 64, node_col, -1)
    g = (iota((nodes, 128), 0) == node_row).astype(F32).astype(BF16)
    gt = (iota((128, nodes), 1) == node_col).astype(F32).astype(BF16)
    g_ref[...] = g
    gt_ref[...] = gt
    is_hub = jnp.sum(gt.astype(F32), axis=0, keepdims=True)

    nbr = nbr_ref[...]
    mask = (mask_ref[...] > 0).astype(F32)
    nbr_h = (
        mm((nbr >> 3).astype(F32).astype(BF16), g) * 8.0 + mm((nbr & 7).astype(F32).astype(BF16), g)
    ).astype(jnp.int32)
    mask_h = mm(mask.astype(BF16), g)
    valid = (node_row >= 0).astype(F32)
    first = (lane_h < 64).astype(F32)

    def degree_rows(deg):
        log_degree = jnp.log(deg + 1.0)
        return log_degree / DEGREE_CENTER, DEGREE_CENTER / log_degree

    deg = deg_ref[...].reshape(1, nodes).astype(F32)
    deg_h = mm(jnp.broadcast_to(deg, (8, nodes)).astype(BF16), g)[0:1]
    deg_h = jnp.where(valid > 0, deg_h, 1.0)
    amp, att = degree_rows(deg)
    amp_h, att_h = degree_rows(deg_h)
    filled = jnp.sum(mask, axis=0, keepdims=True)
    filled_h = jnp.maximum(jnp.sum(mask_h, axis=0, keepdims=True), 1.0)
    rows_ref[...] = jnp.zeros_like(rows_ref)
    for i, (leaf, hub) in enumerate(
        (
            (amp, amp_h),
            (att, att_h),
            (1.0 / filled, 1.0 / filled_h),
            ((seg < 4).astype(F32), None),
            (1.0 - is_hub, valid * first),
            (is_hub, valid),
            (jnp.sum(mask[1:LEAF_SLOTS], axis=0, keepdims=True) - (LEAF_SLOTS - 2.0), filled_h - 16.0),
            (seg.astype(F32), None),
        )
    ):
        rows_ref[i : i + 1, 0:nodes] = leaf
        if hub is not None:
            rows_ref[i : i + 1, nodes : nodes + 128] = hub

    ef_t = ef_ref[...].T
    nbr16 = nbr.astype(jnp.int16)
    ef_h = mm(ef_t, g).astype(BF16)
    hub_iota = iota((nodes, 128), 0).astype(jnp.int16)
    one_h, none_h = jnp.ones((nodes, 128), BF16), jnp.zeros((nodes, 128), BF16)
    for first_node, end_node in lane_groups(nodes):
        span = slice(first_node, end_node)
        size = end_node - first_node
        node_iota = iota((nodes, size), 0).astype(jnp.int16)
        one16, none16 = jnp.ones((nodes, size), BF16), jnp.zeros((nodes, size), BF16)
        zero16 = jnp.zeros((16, size), BF16)
        for k in range(LEAF_SLOTS):
            lo = leaf_col(nodes, k, first_node)
            cols = slice(lo, lo + size)
            b_ref[0:nodes, cols] = jnp.where(node_iota == nbr16[k : k + 1, span], one16, none16)
            piece = ef_t[16 * k : 16 * k + 16, span]
            for r, part in enumerate((piece, zero16, piece, zero16)):
                b_ref[nodes + 16 * r : nodes + 16 * r + 16, cols] = part
            live_ref[0:1, cols] = mask[k : k + 1, span] * LOG2E
            live_ref[1:2, cols] = mask[k : k + 1, span]
    own_half = (iota((32, 128), 0) < 16) == (iota((32, 128), 1) < 64)
    for j in range(8):
        lo = LEAF_SLOTS * nodes + 128 * j
        index = jnp.where(lane_h < 64, nbr_h[2 * j : 2 * j + 1], nbr_h[2 * j + 1 : 2 * j + 2])
        b_ref[0:nodes, lo : lo + 128] = jnp.where(hub_iota == index.astype(jnp.int16), one_h, none_h)
        piece = jnp.where(own_half, ef_h[32 * j : 32 * j + 32].astype(F32), 0.0).astype(BF16)
        b_ref[nodes : nodes + 32, lo : lo + 128] = piece
        b_ref[nodes + 32 : nodes + 64, lo : lo + 128] = piece
        live = jnp.where(lane_h < 64, mask_h[2 * j : 2 * j + 1], mask_h[2 * j + 1 : 2 * j + 2])
        live_ref[0:1, lo : lo + 128] = live * LOG2E
        live_ref[1:2, lo : lo + 128] = live


def tower_weights(wpost_ref, layer, t):
    w = wpost_ref[layer, t]
    inner = iota((64, 320), 1) >= 64
    zero = jnp.zeros((64, 320), BF16)
    return jnp.concatenate(
        [w[:, 0:320], jnp.where(inner, w[:, 256:576], zero), jnp.where(inner, w[:, 512:832], zero)], axis=0
    )


def forward_layer(
    layer, x_ref, wedge_ref, wpre_ref, bias, wpost_ref, wmix_ref, b_ref, live_ref, rows_ref, g_ref, gt_ref,
    m_refs, s_ref, z_ref, y_ref, u_ref, part_ref, a_ref, ya_ref, own_ref,
):
    width, nodes = x_ref.shape
    leaf_cols = LEAF_SLOTS * nodes
    x = x_ref[...]
    g = g_ref[...]
    own = mm(wpre_ref[layer, 0:width], x, TN) + bias
    own_ref[:, 0:nodes] = own
    a_ref[:, 0:nodes] = mm(wpre_ref[layer, width : 2 * width], x, TN).astype(BF16)
    wedge = wedge_ref[layer]
    both = mm(wpre_ref[layer, 2 * width :], jnp.concatenate([wedge] * 4, axis=0), TT)
    high, rest = split_two(both)
    a_ref[:, nodes : nodes + 64] = jnp.where(iota((width, 64), 1) < 32, high, rest)
    own_high, own_rest = split_two(own)
    own_ref[:, nodes:] = mm(own_high, g) + mm(own_rest, g)
    a = a_ref[...]

    def messages(m_ref, lo, hi):
        m_ref[...] = mm(a, b_ref[:, lo:hi])

    x_h = mm(x, g).astype(BF16)
    for t in range(4):
        z_ref[320 * t : 320 * t + 64, 0:nodes] = x[64 * t : 64 * t + 64]
        z_ref[320 * t : 320 * t + 64, nodes:] = x_h[64 * t : 64 * t + 64]

    def summarize(i, tiles, m_ref, base_col):
        per = 64 // ROW_CHUNK
        zr = (i // per) * 320 + 64 + (i % per) * ROW_CHUNK
        rows = pl.ds(i * ROW_CHUNK, ROW_CHUNK)
        for c in tiles:
            hub = c == nodes // 128
            lanes = slice(128 * c, 128 * c + 128)
            if hub:
                cols = [128 * j for j in range(8)]
                first = m_ref[rows, 0:128]
                first = jnp.where(iota((1, 128), 1) < 64, first, pltpu.roll(first, 64, 1))
            else:
                zero, *cols = [leaf_col(nodes, k, 128 * c) - base_col for k in range(LEAF_SLOTS)]
                first = m_ref[rows, zero : zero + 128]
            offs = []
            for lo in cols:
                d = (m_ref[rows, lo : lo + 128] - first) * live_ref[0:1, base_col + lo : base_col + lo + 128]
                m_ref[rows, lo : lo + 128] = d
                offs.append(d)

            def total(parts, op):
                while len(parts) > 1:
                    parts = [op(*parts[i : i + 2]) if i + 1 < len(parts) else parts[i] for i in range(0, len(parts), 2)]
                return fold(parts[0], op) if hub else parts[0]

            inv, missing = rows_ref[2:3, lanes], rows_ref[6:7, lanes]
            mean = total(offs, jnp.add) * inv
            var = total([d * d for d in offs], jnp.add) * inv - mean * mean
            spread = jnp.maximum(var * (LN2 * LN2), 0.0) + SPREAD_OFFSET
            rstd = lax.rsqrt(spread)
            top = jnp.maximum(total(offs, jnp.maximum), 0.0)
            low = jnp.minimum(total(offs, jnp.minimum), 0.0)
            ups = total([jnp.exp2(d - top) for d in offs], jnp.add) + missing * jnp.exp2(-top)
            downs = total([jnp.exp2(low - d) for d in offs], jnp.add) + missing * jnp.exp2(low)
            smax = top + jnp.log2(ups)
            smin = low - jnp.log2(downs)
            base = own_ref[rows, lanes] + first
            for n, stat in enumerate((mean, smax, smin, rstd)):
                s_ref[n, rows, lanes] = stat
                value = base + LN2 * stat if n < 3 else spread * rstd
                z_ref[pl.ds(zr + 64 * n, ROW_CHUNK), lanes] = value.astype(BF16)

    groups = column_groups(nodes)
    waiting = None
    for group in [*zip(m_refs, groups), None]:
        if group is not None:
            messages(group[0], *group[1][0:2])
        if waiting is not None:
            for i in range(width // ROW_CHUNK):
                summarize(i, waiting[1][2], waiting[0], waiting[1][0])
        waiting = group

    amp, att = rows_ref[0:1], rows_ref[1:2]
    for t in range(4):
        r = mm(tower_weights(wpost_ref, layer, t), z_ref[320 * t : 320 * t + 320])
        ya_ref[64 * t : 64 * t + 64] = (r[0:64] + amp * r[64:128] + att * r[128:192]).astype(BF16)
    spread_out = mm(ya_ref[:, nodes:], gt_ref[...])
    y = jnp.where(rows_ref[5:6, 0:nodes] > 0, spread_out, ya_ref[:, 0:nodes].astype(F32)).astype(BF16)
    y_ref[...] = y
    u = mm(wmix_ref[layer], y, TN)
    u_ref[...] = u
    alive = rows_ref[3:4, 0:nodes]
    count = jnp.sum(alive, axis=1, keepdims=True)
    mean = jnp.sum(alive * u, axis=1, keepdims=True) / count
    off = u - mean
    square = jnp.sum(alive * off * off, axis=1, keepdims=True)
    row = jnp.concatenate(to_rows(mean, square) + [jnp.broadcast_to(count, (1, 128))], axis=1)
    part_ref[...] = jnp.broadcast_to(row[None], part_ref.shape)


def forward_first_kernel(
    layer, nf_hbm, ef_hbm, seg_hbm, nbr_hbm, mask_hbm, deg_hbm, wedge_hbm, wpre_hbm, bpre_hbm, wpost_hbm, wmix_hbm,
    x_ref, b_ref, live_ref, rows_ref, g_ref, gt_ref, ma_ref, mb_ref, mc_ref, md_ref,
    s_ref, z_ref, y_ref, u_ref, part_ref,
    a_ref, ya_ref, own_ref, nf_ref, ef_ref, seg_ref, nbr_ref, mask_ref, deg_ref, wedge_ref, wpre_ref, bpre_ref, wpost_ref, wmix_ref, in_sems,
):
    loads = start_copies(
        [
            (seg_hbm, seg_ref), (nbr_hbm, nbr_ref), (mask_hbm, mask_ref), (deg_hbm, deg_ref), (ef_hbm, ef_ref), (nf_hbm, nf_ref),
            (wpre_hbm.at[0:1], wpre_ref), (wedge_hbm, wedge_ref), (bpre_hbm, bpre_ref),
            (wpost_hbm.at[0:1], wpost_ref), (wmix_hbm.at[0:1], wmix_ref),
        ],
        in_sems,
    )
    wait_all(loads)
    build_tables(ef_ref, seg_ref, nbr_ref, mask_ref, deg_ref, b_ref, live_ref, rows_ref, g_ref, gt_ref)
    x_ref[...] = nf_ref[...].T
    forward_layer(
        layer, x_ref, wedge_ref, wpre_ref, *to_cols(bpre_ref[layer : layer + 1]), wpost_ref, wmix_ref, b_ref,
        live_ref, rows_ref, g_ref, gt_ref, (ma_ref, mb_ref, mc_ref, md_ref), s_ref, z_ref, y_ref, u_ref, part_ref,
        a_ref, ya_ref, own_ref,
    )


def norm_rows(recv_ref):
    w = (recv_ref.shape[2] - 128) // 2
    recv = recv_ref[...]
    means, squares = recv[:, :, 0:w], recv[:, :, w : 2 * w]
    counts = jnp.concatenate([recv[:, :, 2 * w :]] * (w // 128), axis=2)
    total = jnp.sum(counts, axis=0)
    mean = jnp.sum(counts * means, axis=0) / total
    off = means - mean[None]
    var = jnp.sum(squares + counts * off * off, axis=0) / total
    return mean, lax.rsqrt(var + STABILITY_FLOOR), total


def normed(u, norm_ref, gain_ref, bias_ref, layer):
    mean, scale, gain, bias = to_cols(
        norm_ref[0:1], norm_ref[1:2], gain_ref[layer : layer + 1], bias_ref[layer : layer + 1]
    )
    xh = (u - mean) * scale
    return xh, xh * gain + bias


def store_norm(norm_ref, recv_ref):
    mean, scale, total = norm_rows(recv_ref)
    norm_ref[...] = jnp.zeros_like(norm_ref)
    norm_ref[0:1] = mean
    norm_ref[1:2] = scale
    norm_ref[2:3] = total


def forward_next_kernel(
    layer, recv_ref, u0_ref, x0_ref, gain_ref, bias_ref, wedge_ref, wpre_ref, bpre_ref, wpost_ref, wmix_ref,
    b_ref, live_ref, rows_ref, g_ref, gt_ref,
    norm_ref, h_ref, x_ref, ma_ref, mb_ref, mc_ref, md_ref, s_ref, z_ref, y_ref, u_ref, part_ref,
    a_ref, ya_ref, own_ref,
):
    store_norm(norm_ref, recv_ref)
    _, v = normed(u0_ref[...], norm_ref, gain_ref, bias_ref, layer - 1)
    h = x0_ref[...].astype(F32) + v / (1.0 + jnp.exp(-v))
    h_ref[...] = h
    x_ref[...] = h.astype(BF16)
    forward_layer(
        layer, x_ref, wedge_ref, wpre_ref, *to_cols(bpre_ref[layer : layer + 1]), wpost_ref, wmix_ref, b_ref,
        live_ref, rows_ref, g_ref, gt_ref, (ma_ref, mb_ref, mc_ref, md_ref), s_ref, z_ref, y_ref, u_ref, part_ref,
        a_ref, ya_ref, own_ref,
    )


def gate_grad(dh, xh, v, dv_ref, part_ref):
    sig = 1.0 / (1.0 + jnp.exp(-v))
    dv = dh * sig * (1.0 + v * (1.0 - sig))
    dv_ref[...] = dv
    sums = [jnp.sum(p, axis=1, keepdims=True) for p in (dv, dv * xh)]
    row = jnp.concatenate(to_rows(*sums), axis=1)
    part_ref[...] = jnp.broadcast_to(row[None], part_ref.shape)


def last_gate_kernel(
    layer, recv_ref, u_ref, h_ref, gain_ref, bias_ref, rows_ref, rg_ref, norm_ref, h_out_ref, dh_ref, dv_ref, part_ref
):
    store_norm(norm_ref, recv_ref)
    xh, v = normed(u_ref[...], norm_ref, gain_ref, bias_ref, layer)
    nodes = v.shape[1]
    seeds = rg_ref.shape[0]
    sig = 1.0 / (1.0 + jnp.exp(-v))
    h_out_ref[...] = h_ref[...] + v * sig
    dh = jnp.zeros(v.shape, F32)
    cols = to_cols(*[rg_ref[s : s + 1] / SUB_MAX for s in range(seeds)])
    for s, col in enumerate(cols):
        dh = jnp.where(rows_ref[7:8, 0:nodes] == s, col, dh)
    dh_ref[...] = dh
    gate_grad(dh, xh, v, dv_ref, part_ref)


def backward_layer(
    layer, recv_ref, dv_ref, dh_ref, u_ref, norm_ref, gain_ref, bias_ref, wmix_ref, wpost_ref, wpre_ref,
    b_ref, live_ref, rows_ref, g_ref, gt_ref, m_refs, s_ref,
    gb_ref, du_ref, d_ref, dm_refs, dcat_ref, et_ref, ds_ref, bd_ref, beside=(),
):
    width, nodes = dv_ref.shape
    leaf_cols = LEAF_SLOTS * nodes
    sums = jnp.sum(recv_ref[...], axis=0)
    g_bias, g_gain = sums[:, 0:width], sums[:, width:]
    gb_ref[...] = sums
    xh, _ = normed(u_ref[...], norm_ref, gain_ref, bias_ref, layer)
    alive = rows_ref[3:4, 0:nodes]
    scale, part_bias, part_gain = to_cols(
        norm_ref[1:2] * gain_ref[layer : layer + 1], g_bias / norm_ref[2:3], g_gain / norm_ref[2:3]
    )
    du = scale * (dv_ref[...] - alive * (part_bias + xh * part_gain))
    du = du.astype(BF16)
    du_ref[...] = du
    dy = mm(wmix_ref[layer], du)
    dy_low = dy.astype(BF16)
    dcat_ref[2 * width :] = dy_low
    dy_h = mm(dy_low, g_ref[...])
    keep = rows_ref[4:5]
    amp, att = rows_ref[0:1], rows_ref[1:2]
    dy_all = jnp.concatenate([dy_low.astype(F32), dy_h], axis=1) * keep
    bd_ref[...] = jnp.zeros_like(bd_ref)
    for t in range(4):
        part = dy_all[64 * t : 64 * t + 64]
        d_ref[192 * t : 192 * t + 64] = part.astype(BF16)
        d_ref[192 * t + 64 : 192 * t + 128] = (part * amp).astype(BF16)
        d_ref[192 * t + 128 : 192 * t + 192] = (part * att).astype(BF16)
        w = tower_weights(wpost_ref, layer, t)
        dz = mm(w, d_ref[192 * t : 192 * t + 192], TN)
        for n in range(4):
            rows = slice(64 * t, 64 * t + 64)
            block = dz[64 * (n + 1) : 64 * (n + 2)]
            ds_ref[n, rows, 0:nodes] = block[:, 0:nodes]
            ds_ref[n, rows, nodes:] = fold(block[:, nodes:], jnp.add)
        bd_ref[64 * t : 64 * t + 64, 64 * t : 64 * t + 64] = wpost_ref[layer, t][:, 0:64]

    acc = ds_ref[0] + ds_ref[1] + ds_ref[2]
    down = acc[:, 0:nodes] + mm(acc[:, nodes:].astype(BF16), gt_ref[...])
    dcat_ref[0:width] = down.astype(BF16)
    once = jnp.where(iota((1, nodes + 128), 1) < nodes + 64, acc, 0.0)
    bias = jnp.sum(once, axis=1, keepdims=True)

    def spread_back(i, tiles, m_ref, dm_ref, base_col):
        rows = pl.ds(i * ROW_CHUNK, ROW_CHUNK)
        for c in tiles:
            hub = c == nodes // 128
            lanes = slice(128 * c, 128 * c + 128)
            mean, smax, smin, rstd = (s_ref[n, rows, lanes] for n in range(4))
            dmean, dsmax, dsmin, dstd = (ds_ref[n, rows, lanes] for n in range(4))
            inv = rows_ref[2:3, lanes]
            c1 = dstd * inv * rstd * LN2
            c0 = dmean * inv - mean * c1
            if hub:
                cols = [128 * j for j in range(8)]
            else:
                zero, *cols = [leaf_col(nodes, k, 128 * c) - base_col for k in range(LEAF_SLOTS)]
                d = c0 + dsmax * jnp.exp2(-smax) + dsmin * jnp.exp2(smin)
                dm_ref[rows, zero : zero + 128] = d.astype(BF16)
            for lo in cols:
                m = m_ref[rows, lo : lo + 128]
                d = c0 + m * c1 + dsmax * jnp.exp2(m - smax) + dsmin * jnp.exp2(smin - m)
                d = d * live_ref[1:2, base_col + lo : base_col + lo + 128]
                dm_ref[rows, lo : lo + 128] = d.astype(BF16)

    def land(dm_ref, lo, hi):
        return mm(dm_ref[...], b_ref[0 : nodes + 32, lo:hi], NT)

    groups = column_groups(nodes)
    waiting, landed = None, 0.0
    for step, group in enumerate([*zip(m_refs, dm_refs, groups), None]):
        if group is not None:
            for i in range(width // ROW_CHUNK):
                spread_back(i, group[2][2], group[0], group[1], group[2][0])
        if step < len(beside):
            beside[step]()
        if waiting is not None:
            landed = landed + land(waiting[1], *waiting[2][0:2])
        waiting = group

    dcat_ref[width : 2 * width] = landed[:, 0:nodes].astype(BF16)
    factor = landed[:, nodes : nodes + 16] + landed[:, nodes + 16 : nodes + 32]
    et_ref[...] = jnp.concatenate([factor, jnp.broadcast_to(bias, (width, 48))], axis=1)
    weights = jnp.concatenate([wpre_ref[layer, 0:width], wpre_ref[layer, width : 2 * width]], axis=1)
    dh = mm(weights, dcat_ref[0 : 2 * width])
    dh = dh + mm(bd_ref[...], dcat_ref[2 * width :], TN)
    return dh_ref[...] + dh


def piece_owner(core, half, place, kind):
    choice = [((0,) + MASKS[k])[place >> 2] | ((0,) + MASKS[1 - k])[place & 3] for k in kind]
    return half + jnp.where(core == half, *choice)


def larger(kind):
    return list(zip(*[MASKS[k] for k in kind]))


def smaller(kind):
    return list(zip(*[MASKS[1 - k] for k in kind]))


def put_tower_grad(t, d_ref, z_ref, grads_ref):
    r = mm(d_ref[192 * t : 192 * t + 192], z_ref[320 * t : 320 * t + 320], NT)
    rows = slice(64 * t, 64 * t + 64)
    first = iota((64, 256), 1) < 64
    grads_ref[rows, 0:256] = r[0:64, 0:256]
    grads_ref[rows, 256:512] = jnp.where(first, jnp.concatenate([r[0:64, 256:320]] * 4, axis=1), r[64:128, 0:256])
    grads_ref[rows, 512:768] = jnp.where(first, jnp.concatenate([r[64:128, 256:320]] * 4, axis=1), r[128:192, 0:256])
    grads_ref[rows, 768:832] = r[128:192, 256:320]


def put_mix_grad(y_ref, du_ref, grads_ref):
    grads_ref[:, 896:1152] = mm(y_ref[...], du_ref[...], NT)


def put_message_grads(layer, x_ref, dcat_ref, et_ref, grads_ref, keep_ref, send_ref):
    width = x_ref.shape[0]
    grads_ref[:, 832:896] = et_ref[...]
    grads_ref[:, 1152:1664] = mm(x_ref[...], dcat_ref[0 : 2 * width], NT)
    me = lax.axis_index("dp") & 31
    for place in range(16):
        for half, ref in ((0, keep_ref), (1, send_ref)):
            row = pl.multiple_of((me ^ piece_owner(me & 1, half, place, SUM_KINDS[layer])) * 8, 8)
            ref[8 * place : 8 * place + 8] = grads_ref[pl.ds(row, 8)]


def grad_steps(d_ref, z_ref, y_ref, du_ref, grads_ref):
    steps = [functools.partial(put_tower_grad, t, d_ref, z_ref, grads_ref) for t in range(4)]
    return steps + [functools.partial(put_mix_grad, y_ref, du_ref, grads_ref)]


def backward_first_kernel(
    layer, recv_ref, dv_ref, dh_ref, u_ref, norm_ref, gain_ref, bias_ref, wmix_ref, wpost_ref, wpre_ref,
    b_ref, live_ref, rows_ref, g_ref, gt_ref, ma_ref, mb_ref, mc_ref, md_ref, s_ref, z_ref, y_ref, x_ref, u_low_ref, norm_low_ref,
    gb_ref, dma_ref, dmb_ref, dmc_ref, dmd_ref, dh_out_ref, dv_out_ref, part_ref, keep_ref, send_ref,
    du_ref, d_ref, dcat_ref, et_ref, ds_ref, bd_ref, grads_ref,
):
    dh = backward_layer(
        layer, recv_ref, dv_ref, dh_ref, u_ref, norm_ref, gain_ref, bias_ref, wmix_ref, wpost_ref, wpre_ref,
        b_ref, live_ref, rows_ref, g_ref, gt_ref, (ma_ref, mb_ref, mc_ref, md_ref), s_ref,
        gb_ref, du_ref, d_ref, (dma_ref, dmb_ref, dmc_ref, dmd_ref), dcat_ref, et_ref, ds_ref, bd_ref,
        grad_steps(d_ref, z_ref, y_ref, du_ref, grads_ref),
    )
    put_message_grads(layer, x_ref, dcat_ref, et_ref, grads_ref, keep_ref, send_ref)
    dh_out_ref[...] = dh
    xh, v = normed(u_low_ref[...], norm_low_ref, gain_ref, bias_ref, layer - 1)
    gate_grad(dh, xh, v, dv_out_ref, part_ref)


def backward_last_kernel(
    layer, recv_ref, dv_ref, dh_ref, u_ref, norm_ref, gain_ref, bias_ref, wmix_ref, wpost_ref, wpre_ref,
    b_ref, live_ref, rows_ref, g_ref, gt_ref, ma_ref, mb_ref, mc_ref, md_ref, s_ref, z_ref, y_ref, x_ref,
    gb_ref, dma_ref, dmb_ref, dmc_ref, dmd_ref, dh_out_ref, keep_ref, send_ref,
    du_ref, d_ref, dcat_ref, et_ref, ds_ref, bd_ref, grads_ref,
):
    dh = backward_layer(
        layer, recv_ref, dv_ref, dh_ref, u_ref, norm_ref, gain_ref, bias_ref, wmix_ref, wpost_ref, wpre_ref,
        b_ref, live_ref, rows_ref, g_ref, gt_ref, (ma_ref, mb_ref, mc_ref, md_ref), s_ref,
        gb_ref, du_ref, d_ref, (dma_ref, dmb_ref, dmc_ref, dmd_ref), dcat_ref, et_ref, ds_ref, bd_ref,
        grad_steps(d_ref, z_ref, y_ref, du_ref, grads_ref),
    )
    put_message_grads(layer, x_ref, dcat_ref, et_ref, grads_ref, keep_ref, send_ref)
    dh_out_ref[...] = dh


def edge_kernel(
    a0_ref, b0_ref, c0_ref, d0_ref, a1_ref, b1_ref, c1_ref, d1_ref, wpre_ref, wedge_ref, gt_ref, h_ref, rows_ref, dh_ref, sums0_ref, sums1_ref,
    out_ref, readout_ref, node_ref, g_gain_ref, g_bias_ref, acc_ref,
):
    width = a0_ref.shape[0]
    nodes = gt_ref.shape[1]
    leaf_cols = LEAF_SLOTS * nodes
    w0, w1 = (mm(wedge_ref[layer], wpre_ref[layer, 2 * width :]).astype(BF16) for layer in range(2))
    pairs = ((a0_ref, a1_ref), (b0_ref, b1_ref), (c0_ref, c1_ref), (d0_ref, d1_ref))
    hub, *groups = [mm(w0, lower[...]) + mm(w1, upper[...]) for lower, upper in pairs]
    total = jnp.concatenate(groups, axis=1)
    for j in range(8):
        acc_ref[32 * j : 32 * j + 16] = hub[:, 128 * j : 128 * j + 128]
        acc_ref[32 * j + 16 : 32 * j + 32] = pltpu.roll(hub[:, 128 * j : 128 * j + 128], 64, 1)
    high, rest = split_two(acc_ref[...])
    gt = gt_ref[...]
    spread_out = mm(high, gt) + mm(rest, gt)
    leaf = []
    for k in range(LEAF_SLOTS):
        parts = []
        for lo, hi in lane_groups(nodes):
            col = leaf_col(nodes, k, lo)
            parts.append(total[:, col : col + hi - lo])
        leaf.append(jnp.concatenate(parts, axis=1))
    leaf = jnp.concatenate(leaf, axis=0)
    out = jnp.concatenate([spread_out[0:64] + leaf, spread_out[64:]], axis=0)
    out_ref[...] = out.T
    belong = (iota((8, nodes), 0).astype(F32) == rows_ref[7:8, 0:nodes]).astype(F32)
    total = lax.dot_general(belong, h_ref[...], NT, precision=lax.Precision.HIGHEST, preferred_element_type=F32)
    readout_ref[...] = total[0 : readout_ref.shape[0]] / SUB_MAX
    node_ref[...] = dh_ref[...].T
    for out_ref, cols in ((g_bias_ref, slice(0, width)), (g_gain_ref, slice(width, 2 * width))):
        out_ref[0:1] = sums0_ref[:, cols]
        out_ref[1:2] = sums1_ref[:, cols]


def finish_half(half, half_refs, outs, bufs, sems):
    me = lax.axis_index("dp") & 31
    core = me & 1
    post, mix, pre, et = bufs
    for layer in range(post.shape[0]):
        for place in range(16):
            block = (me ^ piece_owner(core, half, place, GATHER_KINDS[layer])) >> 1
            piece = half_refs[layer][8 * place : 8 * place + 8]
            post[layer, block] = piece[:, 0:832]
            et[layer, block] = piece[:, 832:896]
            mix[layer, block] = piece[:, 896:1152]
            pre[layer, 0, block] = piece[:, 1152:1408]
            pre[layer, 1, block] = piece[:, 1408:1664]
    side = core ^ half
    post_out, mix_out, pre_out = outs
    pairs = [(post, post_out.at[:, :, side]), (mix, mix_out.at[:, :, side]), (pre, pre_out.at[:, 0:2, :, side])]
    return start_copies(pairs, sems)


def finish_first_kernel(half0_ref, half1_ref, post_out, mix_out, pre_out, et, post, mix, pre, sems):
    wait_all(finish_half(0, (half0_ref, half1_ref), (post_out, mix_out, pre_out), (post, mix, pre, et), sems))


def finish_last_kernel(
    post_in, mix_in, pre_in, other_et, half0_ref, half1_ref, wedge_ref, wpre_ref,
    post_out, mix_out, pre_out, gb_out, gedge_out, post, mix, pre, et, term, gb_ref, gedge_ref, sems,
):
    del post_in, mix_in, pre_in
    copies = finish_half(1, (half0_ref, half1_ref), (post_out, mix_out, pre_out), (post, mix, pre, et), sems)
    width = wpre_ref.shape[2]
    core = lax.axis_index("dp") & 1
    for layer in range(2):
        mine, other = et[layer], other_et[layer]
        first, second = jnp.where(core == 0, other, mine), jnp.where(core == 0, mine, other)
        both = jnp.concatenate([first[:, None], second[:, None]], axis=1).reshape(width, 64)
        turned = jnp.concatenate([both, both], axis=1).T
        gb_ref[layer : layer + 1] = turned[16:17]
        factor = turned[0:16]
        high, rest = split_two(factor)
        last = (factor - high.astype(F32) - rest.astype(F32)).astype(BF16)
        three = jnp.concatenate([high, rest, last], axis=0)
        grad = mm(jnp.concatenate([wedge_ref[layer]] * 3, axis=0), three, TN)
        term[layer] = grad.reshape(term.shape[1:])
        parts = mm(three, wpre_ref[layer, 2 * width :], NT)
        gedge_ref[layer] = parts[0:16] + parts[16:32] + parts[32:48]
    pairs = [(term, pre_out.at[:, 2]), (gedge_ref, gedge_out), (gb_ref, gb_out)]
    copies += start_copies(pairs, sems.at[3:6])
    wait_all(copies)


def on_device(
    devices, node_feats, edge_feats, segment_ids, neighbours, nbr_mask, degrees, w_edge, w_pre, b_pre, w_post,
    w_mix, bn_gain, bn_bias, readout_grad,
):
    nodes, width = node_feats.shape
    lanes = nodes + 128
    cols = LEAF_SLOTS * nodes + 1024
    inner = nodes + 64
    nbr_t = neighbours.T
    mask_t = nbr_mask.T
    wpost_t = jnp.swapaxes(w_post, 2, 3)

    def s(shape, dtype=F32):
        return jax.ShapeDtypeStruct(shape, dtype)

    vmem = pl.BlockSpec(memory_space=pltpu.VMEM)
    hbm = pl.BlockSpec(memory_space=pltpu.HBM)

    def call(kernel, args, outs, scratch=(), far=(), free=(), far_out=(), alias={}, cost=0, limit=20):
        args = [pltpu.with_memory_space_constraint(a, pltpu.HBM) if i in far else a for i, a in enumerate(args)]
        return pl.pallas_call(
            kernel,
            in_specs=[hbm if i in far else vmem for i in range(len(args))],
            out_specs=[hbm if i in far_out else vmem for i in range(len(outs))],
            out_shape=[
                o if i in free else (pltpu.HBM if i in far_out else pltpu.VMEM)(o.shape, o.dtype)
                for i, o in enumerate(outs)
            ],
            scratch_shapes=list(scratch),
            input_output_aliases=alias,
            cost_estimate=pl.CostEstimate(flops=int(cost * 1e9), bytes_accessed=0, transcendentals=0) if cost else None,
            compiler_params=pltpu.CompilerParams(vmem_limit_bytes=limit * 1024 * 1024),
        )(*args)

    def like(shapes):
        return [pltpu.VMEM(x.shape, x.dtype) for x in shapes]

    def dma(n):
        return pltpu.SemaphoreType.DMA((n,))

    def exchange(part):
        return lax.all_to_all(part, "dp", 0, 0, tiled=True)

    spans = [hi - lo for lo, hi, _ in column_groups(nodes)]
    m_s, s_s, z_s = [s((width, n)) for n in spans], s((4, width, lanes)), s((4 * 320, lanes), BF16)
    b_s = s((inner, cols), BF16)
    row_s, low_s = s((width, nodes)), s((width, nodes), BF16)
    layer_outs = [*m_s, s_s, z_s, low_s, row_s, s((devices, 1, 2 * width + 128))]
    fwd_scratch = like([s((width, inner), BF16), s((width, lanes), BF16), s((width, lanes))])
    table_outs = [b_s, s((2, cols)), s((8, lanes)), s((nodes, 128), BF16), s((128, nodes), BF16)]
    first_args = [node_feats, edge_feats, segment_ids, nbr_t, mask_t, degrees, w_edge, w_pre, b_pre, wpost_t, w_mix]
    x0, b, live, rows, g, gt, *m0, s0, z0, y0, u0, part = call(
        functools.partial(forward_first_kernel, 0),
        first_args, [low_s] + table_outs + layer_outs,
        fwd_scratch + like([a[0:1] if i in (7, 9, 10) else a for i, a in enumerate(first_args)]) + [dma(11)], range(11),
    )
    tables = [b, live, rows, g, gt]
    recv = exchange(part)
    norm0, h1, x1, *m1, s1, z1, y1, u1, part = call(
        functools.partial(forward_next_kernel, 1),
        [recv, u0, x0, bn_gain, bn_bias, w_edge, w_pre, b_pre, wpost_t, w_mix] + tables,
        [s((8, width)), row_s, low_s] + layer_outs,
        fwd_scratch,
    )
    recv = exchange(part)
    sums_out = s((devices, 1, 2 * width))
    norm1, h2, dh2, dv1, part = call(
        functools.partial(last_gate_kernel, 1),
        [recv, u1, h1, bn_gain, bn_bias, rows, readout_grad],
        [s((8, width)), row_s, row_s, row_s, sums_out],
    )
    sum_s = s((1, 2 * width))
    du_s, d_s, dm_s = low_s, s((4 * 192, lanes), BF16), [s((width, n), BF16) for n in spans]
    dcat_s, et_s = s((3 * width, nodes), BF16), s((width, 64))
    back_scratch = like([s_s, s((width, width), BF16)])
    recv = exchange(part)
    grad_cols = 1664
    grad_s, half_s = s((width, grad_cols)), s((width // 2, grad_cols))
    back_scratch = like([du_s, d_s, dcat_s, et_s]) + back_scratch + like([grad_s])
    sums1, *dm1, dh1, dv0, part, keep1, send1 = call(
        functools.partial(backward_first_kernel, 1),
        [recv, dv1, dh2, u1, norm1, bn_gain, bn_bias, w_mix, wpost_t, w_pre] + tables + [*m1, s1, z1, y1, x1, u0, norm0],
        [sum_s, *dm_s, row_s, row_s, sums_out, half_s, half_s],
        back_scratch,
    )

    def swap(value, masks):
        return lax.ppermute(value, "dp", [(i, i ^ masks[i & 1]) for i in range(devices)])

    def together(*values):
        return lax.optimization_barrier(values)

    def relay(value, masks):
        one, two = swap(value, masks[0]), swap(value, masks[1])
        return jnp.concatenate([value, one, two, swap(two, masks[0])], axis=0)

    def spread(value):
        mask = 32
        while mask < devices:
            value = value + swap(value, (mask, mask))
            mask *= 2
        return value

    def scatter_sum(value, masks, size):
        got = [swap(value[size * (i + 1) : size * (i + 2)], m) for i, m in enumerate(masks)]
        return value[0:size] + got[0] + got[1] + got[2]

    def gather(value, masks):
        return jnp.concatenate([value] + [swap(value, m) for m in masks], axis=0)

    got1 = swap(send1, (1, 1))
    recv, got1 = together(exchange(part), got1)
    part1 = scatter_sum(keep1 + got1, larger(SUM_KINDS[1]), 32)
    sums0, *dm0, dh0, keep0, send0 = call(
        functools.partial(backward_last_kernel, 0),
        [recv, dv0, dh1, u0, norm0, bn_gain, bn_bias, w_mix, wpost_t, w_pre] + tables + [*m0, s0, z0, y0, x0],
        [sum_s, *dm_s, row_s, half_s, half_s],
        back_scratch, cost=8,
    )
    edge_grad, readout, node_grad, g_gain, g_bias = call(
        edge_kernel, [*dm0, *dm1, w_pre, w_edge, gt, h2, rows, dh0, sums0, sums1],
        [s((nodes, width)), s(readout_grad.shape), s((nodes, width)), s(bn_gain.shape), s(bn_bias.shape)],
        [pltpu.VMEM((width, 128), F32)], free=range(5), cost=2,
    )
    part1, edge_grad, readout = together(part1, edge_grad, readout)
    got0 = swap(send0, (1, 1))
    half0 = keep0 + got0
    outer = [swap(half0[32 * (i + 1) : 32 * (i + 2)], m) for i, m in enumerate(larger(SUM_KINDS[0]))]
    part0 = half0[0:32] + outer[0] + outer[1] + outer[2]
    part1 = spread(scatter_sum(part1, smaller(SUM_KINDS[1]), 8))
    part1 = gather(part1, smaller(GATHER_KINDS[1]))
    part1 = relay(together(part1, part0)[0], larger(GATHER_KINDS[1]))
    part0 = spread(scatter_sum(part0, smaller(SUM_KINDS[0]), 8))
    part0 = gather(gather(part0, smaller(GATHER_KINDS[0])), larger(GATHER_KINDS[0]))
    other1 = swap(part1, (1, 1))
    other0 = swap(part0, (1, 1))
    layers, blocks = w_pre.shape[0], width // 16
    finals = [
        s((layers, blocks, 2, 8, 832)), s((layers, blocks, 2, 8, width)), s((layers, 3, blocks, 2, 8, width)),
    ]
    bufs = [s((layers, blocks, 8, 832)), s((layers, blocks, 8, width)), s((layers, 2, blocks, 8, width))]
    ets = s((layers, blocks, 8, 64))
    *finals_in, ets_first = call(
        finish_first_kernel, [part0, part1], finals + [ets], like(bufs) + [dma(3)], far_out=(0, 1, 2), cost=2
    )
    g_post_t, g_mix, g_pre, g_b, g_edge = call(
        finish_last_kernel, [*finals_in, ets_first, other0, other1, w_edge, w_pre], finals + [s(b_pre.shape), s(w_edge.shape)],
        like(bufs + [ets, s((layers, blocks, 2, 8, width)), s(b_pre.shape), s(w_edge.shape)]) + [dma(6)],
        far=(0, 1, 2), far_out=range(5), alias={0: 0, 1: 1, 2: 2},
    )
    g_post = jnp.swapaxes(g_post_t.reshape(wpost_t.shape), 2, 3)
    g_mix, g_pre = g_mix.reshape(w_mix.shape), g_pre.reshape(w_pre.shape)
    return (
        readout, node_grad, edge_grad, g_edge, g_pre, g_b, g_post, g_mix, g_gain, g_bias,
    )


def solution(mesh):
    split, split2, full = P("dp"), P("dp", None), P()
    in_specs = (split2, split2, split, split2, split2, split) + (full,) * 7 + (split2,)
    out_specs = (split2, split2, split2) + (full,) * 7
    return jax.shard_map(
        functools.partial(on_device, mesh.shape["dp"]),
        mesh=mesh, in_specs=in_specs, out_specs=out_specs, check_vma=False,
    )
```
